32 devices in a mesh: section: 2 (over x), batch: 4 (over z), tensor: 4 (over y, core).
Axes of the slice: x: 2, y: 2, z: 4, core: 2. Of those that a mesh axis runs over, the one named last changes fastest.
Arguments:
- inputs: bfloat16 [2, 4096, 768], P(None, ('batch', 'tensor')), may hold values from -6 to 6
- cotangent: bfloat16 [2, 4096, 768], P(None, ('batch', 'tensor')), may hold values from -6 to 6
- segments: int32 [2, 4, 1024], P(None, 'batch'), may hold values from 0 to 3, never falling along the last dimension, each value on 1 to 512 neighbouring positions
- ln1_gain: float32 [2, 768], P('section'), may hold values from 0.5 to 1.5
- ln1_bias: float32 [2, 768], P('section'), may hold values from -1.5 to 1.5
- w_query: bfloat16 [2, 768, 768], P('section', None, 'tensor'), may hold values from -0.21875 to 0.21875
- w_key: bfloat16 [2, 768, 768], P('section', None, 'tensor'), may hold values from -0.21875 to 0.21875
- w_value: bfloat16 [2, 768, 768], P('section', None, 'tensor'), may hold values from -0.21875 to 0.21875
- w_out: bfloat16 [2, 768, 768], P('section', 'tensor'), may hold values from -0.875 to 0.875
- ln2_gain: float32 [2, 768], P('section'), may hold values from 0.5 to 1.5
- ln2_bias: float32 [2, 768], P('section'), may hold values from -1.5 to 1.5
- w_up: bfloat16 [2, 768, 3072], P('section', None, 'tensor'), may hold values from -0.21875 to 0.21875
- b_up: float32 [2, 3072], P('section', 'tensor'), may hold values from -1.5 to 1.5
- w_down: bfloat16 [2, 3072, 768], P('section', 'tensor'), may hold values from -0.109375 to 0.109375
- b_down: float32 [2, 768], P('section'), may hold values from -1.5 to 1.5
Outputs:
- section_out: bfloat16 [2, 2, 4096, 768], P('section', None, ('batch', 'tensor'))
- section_grad: bfloat16 [2, 2, 4096, 768], P('section', None, ('batch', 'tensor'))
- ln1_gain_grad: float32 [2, 768], P('section')
- ln1_bias_grad: float32 [2, 768], P('section')
- w_query_grad: float32 [2, 768, 768], P('section', None, 'tensor')
- w_key_grad: float32 [2, 768, 768], P('section', None, 'tensor')
- w_value_grad: float32 [2, 768, 768], P('section', None, 'tensor')
- w_out_grad: float32 [2, 768, 768], P('section', 'tensor')
- ln2_gain_grad: float32 [2, 768], P('section')
- ln2_bias_grad: float32 [2, 768], P('section')
- w_up_grad: float32 [2, 768, 3072], P('section', None, 'tensor')
- b_up_grad: float32 [2, 3072], P('section', 'tensor')
- w_down_grad: float32 [2, 3072, 768], P('section', 'tensor')
- b_down_grad: float32 [2, 768], P('section')
The draws below stay inside these ranges and needn't reach their ends.
Inputs may be any that keep to these rules, and one draw needn't show every extreme that they name: `segments`: along each sequence the segment numbers never fall.
All inputs are finite; a program needn't handle non-finite values.
Results may differ from the reference program's by a relative error of at most 0.025.
Values may be sent and summed in bfloat16 or wider, within the bound.
No kernel may reach another device: no remote copies, remote signals or barrier semaphores. Data moves between devices by JAX's collectives and lax.ppermute only.
A program may use at most 192 MiB of HBM per device.

```python
import math
import jax
import jax.numpy as jnp
import numpy as np
from jax import lax

D = 768
HEADS = 12
HEAD_DIM = 64
FF = 3072
LEN = 1024
MB = 2
SEQ_ROWS = 4096
N_SECTION = 2
N_BATCH = 4


def levels(rng, dims, pieces, low, top_value):
    level, own = 1.0, jax.random.fold_in(rng, 6)
    for axis_at, blocks in pieces:
        heights = jnp.exp(jax.random.uniform(jax.random.fold_in(own, axis_at), (blocks,), jnp.float32, low / len(pieces), top_value / len(pieces)))
        level = level * jnp.repeat(heights, dims[axis_at] // blocks).reshape([-1 if axis == axis_at else 1 for axis in range(len(dims))])
    return level


def split_up(amount, total, most, skew):
    weights = [(1 << 20) // math.isqrt(standing ** skew) + 1 for standing in range(2, amount + 1)]
    spare, given = total - most - (amount - 1), [1] * (amount - 1)
    while spare > 0:
        movable = [i for i in range(amount - 1) if given[i] < most]
        mass, left = sum([weights[i] for i in movable]), spare
        for i in movable:
            more = min(most - given[i], max(1, left * weights[i] // mass), spare)
            given[i] = given[i] + more
            spare = spare - more
    return np.array([most] + given)


def uneven_parts(rng, amount, total, most, skew):
    if amount == 2:
        one = jax.random.randint(rng, (), max(1, total - most), min(most, total - 1) + 1)
        return jnp.stack([one, total - one])
    sizes = jnp.asarray(split_up(amount, total, most, skew), jnp.int32)
    couples = (amount - 1) // 2
    giver, receiver = sizes[1:1 + 2 * couples:2], sizes[2:2 + 2 * couples:2]
    margin = jnp.minimum(giver - 1, most - receiver)
    shifted = jax.random.randint(jax.random.fold_in(rng, 1), (couples,), 0, 1 << 20) % (margin + 1)
    sizes = sizes.at[1:1 + 2 * couples:2].set(giver - shifted).at[2:2 + 2 * couples:2].set(receiver + shifted)
    return sizes[jax.random.permutation(jax.random.fold_in(rng, 2), amount)]


def scatter_about(stream_key, dims, spread, most, pieces=(), dtype=jnp.bfloat16):
    entries = jax.random.normal(stream_key, dims, jnp.float32) * spread
    if len(pieces) > 0:
        entries = levels(stream_key, dims, pieces, -0.22, 0.18) * entries
    return jnp.clip(entries, min=-most, max=most).astype(dtype)


def setup_inputs(seed: int = 0) -> dict:
    key_list = jax.random.split(jax.random.key(seed), 16)
    inputs = scatter_about(key_list[0], (MB, SEQ_ROWS, D), 1.0, 6.0, ((1, 16),))
    cotangent = scatter_about(key_list[1], (MB, SEQ_ROWS, D), 1.0, 6.0, ((1, 16),))
    segments = jax.vmap(lambda own: jnp.searchsorted(jnp.cumsum(uneven_parts(own, 4, LEN, LEN // 2, 0)), jnp.arange(LEN), side="right"))(jax.random.split(key_list[2], MB * N_BATCH)).reshape((MB, N_BATCH, LEN)).astype(jnp.int32)
    ln1_gain = jnp.clip(1.0 + 0.1 * jax.random.normal(key_list[3], (N_SECTION, D), jnp.float32), 0.5, 1.5)
    ln1_bias = scatter_about(key_list[4], (N_SECTION, D), 0.3, 1.5, ((0, 2),), jnp.float32)
    w_query = scatter_about(key_list[5], (N_SECTION, D, D), D ** -0.5, 0.21875, ((0, 2), (2, 4)))
    w_key = scatter_about(key_list[6], (N_SECTION, D, D), D ** -0.5, 0.21875, ((0, 2), (2, 4)))
    w_value = scatter_about(key_list[7], (N_SECTION, D, D), D ** -0.5, 0.21875, ((0, 2), (2, 4)))
    w_out = scatter_about(key_list[8], (N_SECTION, D, D), (D // 16) ** -0.5, 0.875, ((0, 2), (1, 4)))
    ln2_gain = jnp.clip(1.0 + 0.1 * jax.random.normal(key_list[9], (N_SECTION, D), jnp.float32), 0.5, 1.5)
    ln2_bias = scatter_about(key_list[10], (N_SECTION, D), 0.3, 1.5, ((0, 2),), jnp.float32)
    w_up = scatter_about(key_list[11], (N_SECTION, D, FF), D ** -0.5, 0.21875, ((0, 2), (2, 4)))
    b_up = scatter_about(key_list[12], (N_SECTION, FF), 0.3, 1.5, ((0, 2), (1, 4)), jnp.float32)
    w_down = scatter_about(key_list[13], (N_SECTION, FF, D), FF ** -0.5, 0.109375, ((0, 2), (1, 4)))
    b_down = scatter_about(key_list[14], (N_SECTION, D), 0.3, 1.5, ((0, 2),), jnp.float32)
    return {"inputs": inputs, "cotangent": cotangent, "segments": segments, "ln1_gain": ln1_gain, "ln1_bias": ln1_bias, "w_query": w_query, "w_key": w_key, "w_value": w_value, "w_out": w_out, "ln2_gain": ln2_gain, "ln2_bias": ln2_bias, "w_up": w_up, "b_up": b_up, "w_down": w_down, "b_down": b_down}


@jax.custom_vjp
def low(v):
    return lax.optimization_barrier(v.astype(jnp.bfloat16)).astype(jnp.float32)

@jax.custom_vjp
def low_back(v):
    return v

def low_keep(v):
    return (low(v), None)

def low_pass(kept, grad):
    return (grad,)

def back_keep(v):
    return (v, None)

def back_low(kept, grad):
    return (low(grad),)
low.defvjp(low_keep, low_pass)
low_back.defvjp(back_keep, back_low)

def matmul_high(left, right):
    return jnp.dot(left, right, precision=lax.Precision.HIGHEST)

def norm_rows(values, gain, bias):
    center = values - lax.optimization_barrier(jnp.mean(values, axis=-1, keepdims=True))
    variance = lax.optimization_barrier(jnp.mean(center * center, axis=-1, keepdims=True))
    return center * lax.rsqrt(variance + 1e-05) * gain + bias

def one_layer(layer_in, segment, weights):
    gain_one, bias_one, w_query, w_key, w_value, w_out, gain_two, bias_two, w_up, b_up, w_down, b_down = weights
    length = layer_in.shape[0]
    head_shape = (length, HEADS, HEAD_DIM)
    normed_in = low(norm_rows(layer_in, gain_one, bias_one))
    queries = low_back(low(matmul_high(normed_in, w_query))).reshape(head_shape)
    key_rows = low_back(low(matmul_high(normed_in, w_key))).reshape(head_shape)
    values = low_back(low(matmul_high(normed_in, w_value))).reshape(head_shape)
    scores = jnp.einsum('qhd,khd->hqk', queries, key_rows, precision=lax.Precision.HIGHEST)
    scores = low_back(scores * HEAD_DIM ** (-0.5))
    position = jnp.arange(length)
    allowed = (position[None, :] <= position[:, None]) & (segment[None, :] == segment[:, None])
    scores = jnp.where(allowed[None], scores, -1e+30)
    highest = lax.optimization_barrier(jnp.max(scores, axis=-1, keepdims=True))
    exp_scores = jnp.exp(scores - highest)
    probabilities = low(exp_scores / lax.optimization_barrier(jnp.sum(exp_scores, axis=-1, keepdims=True)))
    mixed_heads = jnp.einsum('hqk,khd->qhd', probabilities, values, precision=lax.Precision.HIGHEST)
    mixed_heads = low_back(low(mixed_heads)).reshape(length, HEADS * HEAD_DIM)
    mid_state = layer_in + low_back(matmul_high(mixed_heads, w_out))
    normed_mid = low(norm_rows(mid_state, gain_two, bias_two))
    pre_act = low_back(matmul_high(normed_mid, w_up) + b_up)
    activated = low(jax.nn.gelu(pre_act, approximate=True))
    return mid_state + low_back(matmul_high(activated, w_down)) + b_down

def reference(inputs, cotangent, segments, ln1_gain, ln1_bias, w_query, w_key, w_value, w_out, ln2_gain, ln2_bias, w_up, b_up, w_down, b_down):
    params = tuple((array.astype(jnp.float32) for array in (ln1_gain, ln1_bias, w_query, w_key, w_value, w_out, ln2_gain, ln2_bias, w_up, b_up, w_down, b_down)))
    count = MB * N_BATCH
    seq_inputs = inputs.astype(jnp.float32).reshape(count, LEN, D)
    seq_cotangent = cotangent.astype(jnp.float32).reshape(count, LEN, D)
    seq_segments = segments.reshape(count, LEN)

    def one_sequence(totals, item):
        seq_in, seq_cot, segment = item

        def model(first_in, offset_term, weights):
            first = tuple((array[0] for array in weights))
            second = tuple((array[1] for array in weights))
            hidden_state = low_back(low(one_layer(first_in, segment, first))) + offset_term
            return (one_layer(hidden_state, segment, second), hidden_state)
        (final_out, hidden_state), backward = jax.vjp(model, seq_in, jnp.zeros_like(seq_in), params)
        grad_in, grad_hidden, grad_params = backward((seq_cot, jnp.zeros_like(hidden_state)))
        totals = jax.tree.map(jnp.add, totals, grad_params)
        return (totals, (final_out, hidden_state, grad_in, grad_hidden))
    initial = jax.tree.map(lambda array: jnp.zeros(array.shape, jnp.float32), params)
    totals, (finals, hiddens, grad_ins, grad_hiddens) = lax.scan(one_sequence, initial, (seq_inputs, seq_cotangent, seq_segments))
    section_out = jnp.stack([hiddens, finals]).reshape(2, MB, N_BATCH * LEN, D).astype(jnp.bfloat16)
    section_grad = jnp.stack([grad_ins, grad_hiddens]).reshape(2, MB, N_BATCH * LEN, D).astype(jnp.bfloat16)
    return (section_out, section_grad, totals[0], totals[1], totals[2], totals[3], totals[4], totals[5], totals[6], totals[7], totals[8], totals[9], totals[10], totals[11])
```

```python
import jax
import jax.numpy as jnp
from jax import lax
from jax.sharding import PartitionSpec as P

HEAD_DIM = 64
EPSILON = 1e-05
LOW = jnp.bfloat16
FULL = jnp.float32

SIBLING = [(0, 1), (1, 0), (2, 3), (3, 2)]
PARTNER = [(0, 3), (3, 0), (1, 2), (2, 1)]
SWAP = [(0, 1), (1, 0)]


def dot(left, right):
    return jnp.dot(left, right, preferred_element_type=FULL)


def dot_rows(left, right):
    return lax.dot_general(left, right, (((0,), (0,)), ((), ())), preferred_element_type=FULL)


def dot_back(left, right):
    return lax.dot_general(left, right, (((1,), (1,)), ((), ())), preferred_element_type=FULL)


def norm_rows(values):
    center = values - jnp.mean(values, axis=-1, keepdims=True)
    inverse = lax.rsqrt(jnp.mean(center * center, axis=-1, keepdims=True) + EPSILON)
    return center * inverse, inverse


def norm_back(grad_norm, normed, inverse, gain):
    scaled = grad_norm * gain
    mean_one = jnp.mean(scaled, axis=-1, keepdims=True)
    mean_two = jnp.mean(scaled * normed, axis=-1, keepdims=True)
    return inverse * (scaled - mean_one - normed * mean_two)


def gelu_tanh(values):
    return jax.nn.gelu(values, approximate=True)


def to_partner(value):
    return lax.ppermute(value, "tensor", PARTNER)


def to_sibling(value):
    return lax.ppermute(value, "tensor", SIBLING)


class Place:
    def __init__(self, block):
        self.section = lax.axis_index("section")
        self.tensor = lax.axis_index("tensor")
        self.block = block
        self.first_core = (self.tensor % 2) == 0
        self.early = self.tensor < 2
        self.outer = (self.tensor == 0) | (self.tensor == 3)

    def low_high(self, own, other):
        return jnp.concatenate([jnp.where(self.early, own, other), jnp.where(self.early, other, own)], axis=0)

    def own(self, rows):
        return jnp.where(self.early, rows[: self.block], rows[self.block :])

    def in_order(self, own, other):
        n = self.block
        lows = own[:n], other[:n]
        highs = own[n:], other[n:]
        pick = self.outer
        return jnp.concatenate(
            [
                jnp.where(pick, lows[0], lows[1]),
                jnp.where(pick, lows[1], lows[0]),
                jnp.where(pick, highs[1], highs[0]),
                jnp.where(pick, highs[0], highs[1]),
            ],
            axis=0,
        )

    def split_order(self, rows):
        n = self.block
        parts = [rows[i * n : (i + 1) * n] for i in range(4)]
        pick = self.outer
        own = jnp.concatenate([jnp.where(pick, parts[0], parts[1]), jnp.where(pick, parts[3], parts[2])], axis=0)
        other = jnp.concatenate([jnp.where(pick, parts[1], parts[0]), jnp.where(pick, parts[2], parts[3])], axis=0)
        return own, other


def windows(place):
    n = place.block
    low = jnp.where(place.outer, 0, 1)
    high = 3 - low
    return ((0, low * n, 0, 2 * n), (n, high * n, (high - 2) * n, 3 * n))


def window_mask(segment, first_query, first_key, n, width):
    query_at = first_query + jnp.arange(n)
    key_at = first_key + jnp.arange(width)
    query_seg = lax.dynamic_slice_in_dim(segment, first_query, n)
    key_seg = lax.dynamic_slice_in_dim(segment, first_key, width)
    return (key_at[None, :] <= query_at[:, None]) & (key_seg[None, :] == query_seg[:, None])


def heads(rows):
    return rows.reshape(rows.shape[0], -1, HEAD_DIM)


def attend(place, segment, queries, keys, values):
    n = place.block
    outs, sums = [], []
    for row, first_query, first_key, width in windows(place):
        mask = window_mask(segment, first_query, first_key, n, width)
        q = heads(queries[row : row + n])
        k = heads(lax.dynamic_slice_in_dim(keys, first_key, width))
        v = heads(lax.dynamic_slice_in_dim(values, first_key, width))
        scores = jnp.einsum("qhd,khd->hqk", q, k, preferred_element_type=FULL) * HEAD_DIM**-0.5
        scores = jnp.where(mask[None], scores, -1e30)
        highest = jnp.max(scores, axis=-1, keepdims=True)
        exp_scores = jnp.exp(scores - highest)
        totals = jnp.sum(exp_scores, axis=-1, keepdims=True)
        probabilities = (exp_scores / totals).astype(LOW)
        mixed = jnp.einsum("hqk,khd->qhd", probabilities, v, preferred_element_type=FULL).astype(LOW)
        outs.append(mixed.reshape(n, -1))
        sums.append((highest + jnp.log(totals))[..., 0])
    return jnp.concatenate(outs, axis=0), jnp.concatenate(sums, axis=1)


def attend_back(place, segment, queries, keys, values, log_sums, grad_mixed):
    n = place.block
    scaling = HEAD_DIM**-0.5
    grad_queries = []
    grad_keys = jnp.zeros((keys.shape[0], keys.shape[1] // HEAD_DIM, HEAD_DIM), FULL)
    grad_values = jnp.zeros_like(grad_keys)
    for row, first_query, first_key, width in windows(place):
        mask = window_mask(segment, first_query, first_key, n, width)
        q = heads(queries[row : row + n])
        do = heads(grad_mixed[row : row + n])
        k = heads(lax.dynamic_slice_in_dim(keys, first_key, width))
        v = heads(lax.dynamic_slice_in_dim(values, first_key, width))
        scores = jnp.einsum("qhd,khd->hqk", q, k, preferred_element_type=FULL) * scaling
        scores = jnp.where(mask[None], scores, -1e30)
        probabilities = jnp.exp(scores - log_sums[:, row : row + n, None])
        dv = jnp.einsum("hqk,qhd->khd", probabilities.astype(LOW), do, preferred_element_type=FULL)
        dp = jnp.einsum("qhd,khd->hqk", do, v, preferred_element_type=FULL)
        inner = jnp.sum(probabilities * dp, axis=-1, keepdims=True)
        ds = (probabilities * (dp - inner)).astype(LOW)
        dq = jnp.einsum("hqk,khd->qhd", ds, k, preferred_element_type=FULL) * scaling
        dk = jnp.einsum("hqk,qhd->khd", ds, q, preferred_element_type=FULL) * scaling
        grad_queries.append(dq.reshape(n, -1).astype(LOW))
        old = lax.dynamic_slice_in_dim(grad_keys, first_key, width)
        grad_keys = lax.dynamic_update_slice_in_dim(grad_keys, old + dk, first_key, 0)
        old = lax.dynamic_slice_in_dim(grad_values, first_key, width)
        grad_values = lax.dynamic_update_slice_in_dim(grad_values, old + dv, first_key, 0)
    flat = (keys.shape[0], keys.shape[1])
    return jnp.concatenate(grad_queries, axis=0), grad_keys.reshape(flat), grad_values.reshape(flat)


def layer_forward(place, layer_in, segment, small, weights):
    gain_one, bias_one, gain_two, bias_two, b_down, b_up = small
    w_qkv, w_out, w_up, w_down = weights
    third = w_qkv.shape[1] // 3
    normed, _ = norm_rows(layer_in)
    a_one = (normed * gain_one + bias_one).astype(LOW)
    qkv = dot(a_one, w_qkv).astype(LOW)
    other = to_sibling(qkv[:, third:])
    both = place.in_order(qkv[:, third:], other)
    keys, values = both[:, :third], both[:, third:]
    queries = qkv[:, :third]
    mixed, log_sums = attend(place, segment, queries, keys, values)
    part = dot(mixed, w_out).astype(LOW)
    mid = layer_in + (part.astype(FULL) + to_partner(part).astype(FULL))
    normed_two, _ = norm_rows(mid)
    a_two = (normed_two * gain_two + bias_two).astype(LOW)
    pre = dot(a_two, w_up) + b_up
    active = gelu_tanh(pre).astype(LOW)
    part = dot(active, w_down).astype(LOW)
    out = mid + (part.astype(FULL) + to_partner(part).astype(FULL)) + b_down
    return out.astype(LOW), (layer_in, a_one, queries, keys, values, mixed, log_sums, mid, a_two, pre, active)


def layer_backward(place, grad_low, stored, segment, small, weights):
    gain_one, bias_one, gain_two, bias_two, b_down, b_up = small
    w_qkv, w_out, w_up, w_down = weights
    layer_in, a_one, queries, keys, values, mixed, log_sums, mid, a_two, pre, active = stored
    grad_out = grad_low.astype(FULL)
    grad_w_down = dot_rows(active, grad_low)
    _, gelu_back = jax.vjp(gelu_tanh, pre)
    grad_pre = gelu_back(dot_back(grad_low, w_down))[0].astype(LOW)
    part = dot_back(grad_pre, w_up).astype(LOW)
    grad_norm = part.astype(FULL) + to_partner(part).astype(FULL)
    grad_w_up = dot_rows(a_two, grad_pre)
    grad_b_up = jnp.sum(grad_pre.astype(FULL), axis=0)
    normed, inverse = norm_rows(mid)
    grad_mid = grad_out + norm_back(grad_norm, normed, inverse, gain_two)
    grad_gain_two = jnp.sum(grad_norm * normed, axis=0)
    grad_bias_two = jnp.sum(grad_norm, axis=0)
    grad_attn = grad_mid.astype(LOW)
    grad_w_out = dot_rows(mixed, grad_attn)
    grad_mixed = dot_back(grad_attn, w_out).astype(LOW)
    grad_q, grad_k, grad_v = attend_back(place, segment, queries, keys, values, log_sums, grad_mixed)
    own, other = place.split_order(jnp.concatenate([grad_k, grad_v], axis=1))
    grad_kv = (own + to_sibling(other.astype(LOW)).astype(FULL)).astype(LOW)
    grad_qkv = jnp.concatenate([grad_q, grad_kv], axis=1)
    part = dot_back(grad_qkv, w_qkv).astype(LOW)
    grad_norm = part.astype(FULL) + to_partner(part).astype(FULL)
    grad_w_qkv = dot_rows(a_one, grad_qkv)
    normed, inverse = norm_rows(layer_in)
    grad_in = grad_mid + norm_back(grad_norm, normed, inverse, gain_one)
    grad_gain_one = jnp.sum(grad_norm * normed, axis=0)
    grad_bias_one = jnp.sum(grad_norm, axis=0)
    grad_b_down = jnp.sum(grad_out, axis=0)
    small_sums = jnp.stack([grad_gain_one, grad_bias_one, grad_gain_two, grad_bias_two, grad_b_down])
    return grad_in.astype(LOW), small_sums, grad_b_up, (grad_w_qkv, grad_w_out, grad_w_up, grad_w_down)


def body(
    inputs, cotangent, segments, ln1_gain, ln1_bias, w_query, w_key, w_value, w_out,
    ln2_gain, ln2_bias, w_up, b_up, w_down, b_down,
):
    place = Place(inputs.shape[1])
    section = place.section
    on_first = section == 0
    first_core = place.first_core
    segment = jnp.where(on_first, segments[0, 0], segments[1, 0])

    def whole_rows(both):
        own = jnp.where(on_first, both[0], both[1])
        return place.low_high(own, to_partner(own))

    layer_in = whole_rows(inputs)
    grad_last = whole_rows(cotangent)

    small_own = jnp.concatenate([ln1_gain, ln1_bias, ln2_gain, ln2_bias, b_down, b_up], axis=0)
    small_other = lax.ppermute(small_own, "section", SWAP)
    qkv_own = jnp.concatenate([w_query[0], w_key[0], w_value[0]], axis=1)
    quarters_own = (qkv_own, w_out[0], w_up[0], w_down[0])
    quarters_other = tuple(lax.ppermute(q, "section", SWAP) for q in quarters_own)

    def layer_weights(layer):
        here = section == layer
        quarters = [jnp.where(here, a, b) for a, b in zip(quarters_own, quarters_other)]
        siblings = [to_sibling(q) for q in quarters]
        small = jnp.where(here, small_own, small_other)
        b_up_sibling = to_sibling(small[5])
        one = [jnp.where(first_core, a, b) for a, b in zip(quarters[:2], siblings[:2])]
        two = [jnp.where(first_core, b, a) for a, b in zip(quarters[:2], siblings[:2])]
        width = one[0].shape[1] // 3
        pieces = []
        for i in range(3):
            pieces += [one[0][:, i * width : (i + 1) * width], two[0][:, i * width : (i + 1) * width]]
        qkv = jnp.concatenate(pieces, axis=1)
        out = jnp.concatenate([one[1], two[1]], axis=0)
        up = jnp.concatenate([quarters[2], siblings[2]], axis=1)
        down = jnp.concatenate([quarters[3], siblings[3]], axis=0)
        rows = tuple(small[i] for i in range(5)) + (jnp.concatenate([small[5], b_up_sibling]),)
        return rows, (qkv, out, up, down)

    small_0, weights_0 = layer_weights(0)
    small_1, weights_1 = layer_weights(1)
    out_0, stored_0 = layer_forward(place, layer_in.astype(FULL), segment, small_0, weights_0)
    out_1, stored_1 = layer_forward(place, out_0.astype(FULL), segment, small_1, weights_1)
    back_1, sums_1, bup_1, grads_1 = layer_backward(place, grad_last, stored_1, segment, small_1, weights_1)
    back_0, sums_0, bup_0, grads_0 = layer_backward(place, back_1, stored_0, segment, small_0, weights_0)

    def quarter_grads(grads, grad_b_up):
        qkv, out, up, down = grads
        width = qkv.shape[1] // 6
        ones = [jnp.concatenate([qkv[:, 2 * i * width : (2 * i + 1) * width] for i in range(3)], axis=1), out[:width]]
        twos = [jnp.concatenate([qkv[:, (2 * i + 1) * width : (2 * i + 2) * width] for i in range(3)], axis=1), out[width:]]
        keep = [jnp.where(first_core, a, b) for a, b in zip(ones, twos)]
        send = [jnp.where(first_core, b, a) for a, b in zip(ones, twos)]
        half = up.shape[1] // 2
        keep += [up[:, :half], down[:half], grad_b_up[:half][None]]
        send += [up[:, half:], down[half:], grad_b_up[half:][None]]
        return [a + to_sibling(b.astype(LOW)).astype(FULL) for a, b in zip(keep, send)]

    quarter_0 = quarter_grads(grads_0, bup_0)
    quarter_1 = quarter_grads(grads_1, bup_1)
    totals = []
    for a, b in zip(quarter_0, quarter_1):
        mine = jnp.where(on_first, a, b)
        theirs = jnp.where(on_first, b, a).astype(LOW)
        total = (mine + lax.ppermute(theirs, "section", SWAP).astype(FULL)).astype(LOW)
        totals.append(lax.psum(total, "batch").astype(FULL))
    sums = lax.psum(jnp.stack([sums_0, sums_1]), ("section", "batch", "tensor")) * 0.5
    sums = jnp.where(on_first, sums[0], sums[1])

    def both_micro(first, second):
        first, second = place.own(first), place.own(second)
        mine = jnp.where(on_first, first, second)
        theirs = lax.ppermute(jnp.where(on_first, second, first), "section", SWAP)
        return jnp.stack([jnp.where(on_first, mine, theirs), jnp.where(on_first, theirs, mine)])[None]

    forward_out = both_micro(out_0, out_1)
    backward_out = both_micro(back_0, back_1)
    width = totals[0].shape[1] // 3
    return (
        forward_out,
        backward_out,
        sums[0][None],
        sums[1][None],
        totals[0][:, :width][None],
        totals[0][:, width : 2 * width][None],
        totals[0][:, 2 * width :][None],
        totals[1][None],
        sums[2][None],
        sums[3][None],
        totals[2][None],
        totals[4],
        totals[3][None],
        sums[4][None],
    )


def solution(mesh):
    rows = P(None, ("batch", "tensor"), None)
    layer = P("section", None)
    by_column = P("section", None, "tensor")
    by_row = P("section", "tensor", None)
    kept = P("section", None, ("batch", "tensor"), None)
    return jax.shard_map(
        body,
        mesh=mesh,
        in_specs=(
            rows, rows, P(None, "batch", None), layer, layer, by_column, by_column, by_column, by_row,
            layer, layer, by_column, P("section", "tensor"), by_row, layer,
        ),
        out_specs=(
            kept, kept, layer, layer, by_column, by_column, by_column, by_row,
            layer, layer, by_column, P("section", "tensor"), by_row, layer,
        ),
        check_vma=False,
    )
```

```python
import functools

import jax
import jax.numpy as jnp
from jax import lax
from jax.experimental import pallas as pl
from jax.experimental.pallas import tpu as pltpu
from jax.sharding import PartitionSpec as P

HEAD_DIM = 64
EPSILON = 1e-05
LOW = jnp.bfloat16
FULL = jnp.float32
SCALING = HEAD_DIM**-0.5
MASKED = -1e30
VMEM_BYTES = 48 * 1024 * 1024

SIBLING = [(0, 1), (1, 0), (2, 3), (3, 2)]
PARTNER = [(0, 3), (3, 0), (1, 2), (2, 1)]
SWAP = [(0, 1), (1, 0)]


def dot(left, right):
    return jnp.dot(left, right, preferred_element_type=FULL)


def dot_rows(left, right):
    return lax.dot_general(left, right, (((0,), (0,)), ((), ())), preferred_element_type=FULL)


def dot_back(left, right):
    return lax.dot_general(left, right, (((1,), (1,)), ((), ())), preferred_element_type=FULL)


def norm_rows(values):
    center = values - jnp.mean(values, axis=-1, keepdims=True)
    inverse = lax.rsqrt(jnp.mean(center * center, axis=-1, keepdims=True) + EPSILON)
    return center * inverse, inverse


def norm_back(grad_norm, normed, inverse, gain):
    scaled = grad_norm * gain
    mean_one = jnp.mean(scaled, axis=-1, keepdims=True)
    mean_two = jnp.mean(scaled * normed, axis=-1, keepdims=True)
    return inverse * (scaled - mean_one - normed * mean_two)


def to_partner(value):
    return lax.ppermute(value, "tensor", PARTNER)


def to_sibling(value):
    return lax.ppermute(value, "tensor", SIBLING)


def call(kernel, operands, outs, flops, scalars=0, scratch=()):
    moved = sum(a.size * a.dtype.itemsize for a in operands) + sum(o.size * o.dtype.itemsize for o in outs)
    specs = [pl.BlockSpec(memory_space=pltpu.SMEM)] * scalars
    specs += [pl.BlockSpec(memory_space=pltpu.VMEM)] * (len(operands) - scalars)
    return pl.pallas_call(
        kernel,
        out_shape=tuple(outs),
        in_specs=specs,
        out_specs=tuple(pl.BlockSpec(memory_space=pltpu.VMEM) for _ in outs),
        scratch_shapes=list(scratch),
        compiler_params=pltpu.CompilerParams(vmem_limit_bytes=VMEM_BYTES),
        cost_estimate=pl.CostEstimate(flops=int(flops), bytes_accessed=int(moved), transcendentals=0),
    )(*operands)


def shape(*dims, dtype=LOW):
    return jax.ShapeDtypeStruct(dims, dtype)


def project_kernel(first, *refs):
    if first:
        rows_ref, gain, bias, w_own, w_sib, a_ref, q_ref, kv_ref, send_ref = refs
        layer_in = rows_ref[...].astype(FULL)
    else:
        mid, part, got, b_down, gain, bias, w_own, w_sib, in_ref, a_ref, q_ref, kv_ref, send_ref = refs
        low = (mid[...] + (part[...].astype(FULL) + got[...].astype(FULL)) + b_down[...]).astype(LOW)
        in_ref[...] = low
        layer_in = low.astype(FULL)
    normed, _ = norm_rows(layer_in)
    a_one = (normed * gain[...] + bias[...]).astype(LOW)
    a_ref[...] = a_one
    own = dot_back(a_one, w_own[...]).astype(LOW)
    sib = dot_back(a_one, w_sib[...]).astype(LOW)
    w = own.shape[1] // 3
    q_own, k_own, v_own = own[:, :w], own[:, w : 2 * w], own[:, 2 * w :]
    q_sib, k_sib, v_sib = sib[:, :w], sib[:, w : 2 * w], sib[:, 2 * w :]
    q_ref[...] = jnp.concatenate([q_own, q_sib], axis=1) * jnp.asarray(SCALING, LOW)
    kv_ref[...] = jnp.concatenate([k_own, k_sib, v_own, v_sib], axis=1)
    send_ref[...] = jnp.concatenate([k_sib, k_own, v_sib, v_own], axis=1)


def project(source, gain, bias, w_own, w_sib, first):
    n, d = source[0].shape
    h = 2 * (w_own.shape[0] // 3)
    outs = [shape(n, d), shape(n, h), shape(n, 2 * h), shape(n, 2 * h)]
    if not first:
        outs = [shape(n, d)] + outs
    got = call(
        functools.partial(project_kernel, first),
        (*source, gain, bias, w_own, w_sib),
        outs,
        2 * n * d * 3 * h,
    )
    return got if not first else (source[0], *got)


def pair_masks(q_pair):
    lane = lax.broadcasted_iota(jnp.int32, q_pair.shape, 1)
    zero = jnp.zeros_like(q_pair)
    return jnp.where(lane < HEAD_DIM, q_pair, zero), jnp.where(lane < HEAD_DIM, zero, q_pair)


def attend_kernel(late, *refs):
    if late:
        outer, q_ref, sib_low, own_high, sib_high, own_low, bias_ref, wo_own, wo_sib, o_ref, lse_ref, part_ref, extra = refs

        @pl.when(outer[0] == 1)
        def _():
            extra[...] = sib_high[...]

        @pl.when(outer[0] == 0)
        def _():
            extra[...] = own_low[...]

        kv = jnp.concatenate([sib_low[...], own_high[...], extra[...]], axis=0)
    else:
        q_ref, own_low, sib_low, bias_ref, wo_own, wo_sib, o_ref, lse_ref, part_ref = refs
        kv = jnp.concatenate([own_low[...], sib_low[...]], axis=0)
    h = kv.shape[1] // 2
    keys, values = kv[:, :h], kv[:, h:]
    values_t = values.T
    outs, sums = [], []
    for pair in range(h // 128):
        lanes = slice(pair * 128, pair * 128 + 128)
        for j, q in enumerate(pair_masks(q_ref[:, lanes])):
            head = 2 * pair + j
            scores = dot_back(keys[:, lanes], q) + bias_ref[...]
            highest = jnp.max(scores, axis=0, keepdims=True)
            e = jnp.exp(scores - highest)
            total = jnp.sum(e, axis=0, keepdims=True)
            mixed = dot(values_t[head * HEAD_DIM : (head + 1) * HEAD_DIM], e.astype(LOW))
            outs.append(mixed * (1.0 / total))
            sums.append(highest + jnp.log(total))
    o = jnp.concatenate(outs, axis=0).T.astype(LOW)
    o_ref[...] = o
    lse_ref[...] = jnp.concatenate(sums + sums[: 8 - len(sums)], axis=0)
    half = wo_own.shape[0]
    part_ref[...] = (dot(o[:, :half], wo_own[...]) + dot(o[:, half:], wo_sib[...])).astype(LOW)


def attend(late, q, blocks, bias, wo_own, wo_sib, outer):
    n, h = q.shape
    d = wo_own.shape[1]
    operands = ((outer,) if late else ()) + (q, *blocks, bias, wo_own, wo_sib)
    return call(
        functools.partial(attend_kernel, late),
        operands,
        [shape(n, h), shape(8, n, dtype=FULL), shape(n, d)],
        2 * n * h * (4 * bias.shape[0] + d),
        scalars=1 if late else 0,
        scratch=[pltpu.VMEM((n, 2 * h), LOW)] if late else (),
    )


def gelu_parts(z):
    c = 0.7978845608028654
    square = z * z
    t = jnp.tanh(c * (z + 0.044715 * (square * z)))
    half = 0.5 * (1.0 + t)
    return z * half, half + 0.5 * z * (1.0 - t * t) * (c + (3.0 * 0.044715 * c) * square)


def feed_kernel(last, *refs):
    if last:
        (u, part, got, gain, bias, up_own, up_sib, b_own, b_sib, dn_own, dn_sib, grad_ref,
         mid_ref, a_ref, g_ref, dz_ref, back_ref, hidden_sum, row_sum) = refs
    else:
        (u, part, got, gain, bias, up_own, up_sib, b_own, b_sib, dn_own, dn_sib,
         mid_ref, a_ref, g_ref, slope_ref, out_ref) = refs
    mid = u[...].astype(FULL) + (part[...].astype(FULL) + got[...].astype(FULL))
    mid_ref[...] = mid
    normed, _ = norm_rows(mid)
    a_two = (normed * gain[...] + bias[...]).astype(LOW)
    a_ref[...] = a_two
    f = up_own.shape[1]
    step = 256
    total = jnp.zeros(mid.shape, FULL)
    for side, (up, b, dn) in enumerate(((up_own, b_own, dn_own), (up_sib, b_sib, dn_sib))):
        for at in range(0, f, step):
            cols = slice(at, at + step)
            here = slice(side * f + at, side * f + at + step)
            z = dot(a_two, up[:, cols]) + b[:, cols]
            g, slope = gelu_parts(z)
            g = g.astype(LOW)
            g_ref[:, here] = g
            if last:
                dz = (dot_back(grad_ref[...], dn[cols, :]) * slope).astype(LOW)
                dz_ref[:, here] = dz
                hidden_sum[:, here] = jnp.sum(dz.astype(FULL), axis=0, keepdims=True)
                total = total + dot_back(dz, up[:, cols])
            else:
                slope_ref[:, here] = slope.astype(LOW)
                total = total + dot(g, dn[cols, :])
    if last:
        back_ref[...] = total.astype(LOW)
        row_sum[...] = jnp.sum(grad_ref[...].astype(FULL), axis=0, keepdims=True)
    else:
        out_ref[...] = total.astype(LOW)


def feed(u, part, got, gain, bias, up, b_up, dn, grad=None):
    n, d = u.shape
    f = up[0].shape[1]
    last = grad is not None
    outs = [shape(n, d, dtype=FULL), shape(n, d), shape(n, 2 * f), shape(n, 2 * f), shape(n, d)]
    operands = (u, part, got, gain, bias, *up, *b_up, *dn) + ((grad,) if last else ())
    if last:
        outs += [shape(1, 2 * f, dtype=FULL), shape(1, d, dtype=FULL)]
    return call(functools.partial(feed_kernel, last), operands, outs, 2 * n * d * 2 * f * (3 if last else 2))


def feed_back_kernel(mid_grad, part, got, in_ref, gain, slope, up_own, up_sib, dn_own, dn_sib,
                     grad_ref, sums_ref, dz_ref, back_ref, hidden_sum):
    grad_norm = part[...].astype(FULL) + got[...].astype(FULL)
    normed, inverse = norm_rows(in_ref[...].astype(FULL))
    grad = (mid_grad[...] + norm_back(grad_norm, normed, inverse, gain[...])).astype(LOW)
    grad_ref[...] = grad
    sums_ref[...] = jnp.concatenate(
        [
            jnp.sum(grad_norm * normed, axis=0, keepdims=True),
            jnp.sum(grad_norm, axis=0, keepdims=True),
            jnp.sum(grad.astype(FULL), axis=0, keepdims=True),
        ],
        axis=0,
    )
    f = up_own.shape[1]
    step = 256
    total = jnp.zeros(grad.shape, FULL)
    for side, (up, dn) in enumerate(((up_own, dn_own), (up_sib, dn_sib))):
        for at in range(0, f, step):
            cols = slice(at, at + step)
            here = slice(side * f + at, side * f + at + step)
            dz = (dot_back(grad, dn[cols, :]) * slope[:, here].astype(FULL)).astype(LOW)
            dz_ref[:, here] = dz
            hidden_sum[:, here] = jnp.sum(dz.astype(FULL), axis=0, keepdims=True)
            total = total + dot_back(dz, up[:, cols])
    back_ref[...] = total.astype(LOW)


def feed_back(mid_grad, part, got, layer_in, gain, slope, up, dn):
    n, d = mid_grad.shape
    f = up[0].shape[1]
    outs = [shape(n, d), shape(3, d, dtype=FULL), shape(n, 2 * f), shape(n, d), shape(1, 2 * f, dtype=FULL)]
    return call(
        feed_back_kernel, (mid_grad, part, got, layer_in, gain, slope, *up, *dn), outs, 2 * n * d * 2 * f * 2
    )


def attend_back_kernel(outer, *refs):
    (mids, parts, gots, grads, gain, wo_own, wo_sib, qs, owns, sibs, biases, lses) = (
        refs[0:2], refs[2:4], refs[4:6], refs[6:8], refs[8], refs[9], refs[10], refs[11:13], refs[13:15],
        refs[15:17], refs[17:19], refs[19:21],
    )
    mid_grads, lows, sums_ref, dq_refs, keep_refs, send_refs = (
        refs[21:23], refs[23:25], refs[25], refs[26:28], refs[28:30], refs[30:32]
    )
    extra, acc_own, acc_sib = refs[32], refs[33:35], refs[35:37]
    n = mids[0].shape[0]
    outside = outer[0].astype(FULL)

    @pl.when(outer[0] == 1)
    def _():
        extra[...] = sibs[1][...]

    @pl.when(outer[0] == 0)
    def _():
        extra[...] = owns[0][...]

    sums = None
    for late in (0, 1):
        grad_norm = parts[late][...].astype(FULL) + gots[late][...].astype(FULL)
        normed, inverse = norm_rows(mids[late][...])
        mid_grad = grads[late][...].astype(FULL) + norm_back(grad_norm, normed, inverse, gain[...])
        mid_grads[late][...] = mid_grad
        low = mid_grad.astype(LOW)
        lows[late][...] = low
        now = jnp.concatenate(
            [jnp.sum(grad_norm * normed, axis=0, keepdims=True), jnp.sum(grad_norm, axis=0, keepdims=True)], axis=0
        )
        sums = now if sums is None else sums + now
        do = jnp.concatenate([dot_back(low, wo_own[...]), dot_back(low, wo_sib[...])], axis=1).astype(LOW)
        blocks = (sibs[0], owns[1], extra) if late else (owns[0], sibs[0])
        kv = jnp.concatenate([b[...] for b in blocks], axis=0)
        h = kv.shape[1] // 2
        keys, values = kv[:, :h], kv[:, h:]
        keys_t = keys.T
        dq = []
        for pair in range(h // 128):
            lanes = slice(pair * 128, pair * 128 + 128)
            dk = dv = None
            qs_two, do_two = pair_masks(qs[late][:, lanes]), pair_masks(do[:, lanes])
            for j in (0, 1):
                head = 2 * pair + j
                scores = dot_back(keys[:, lanes], qs_two[j]) + biases[late][...]
                p = jnp.exp(scores - lses[late][head : head + 1, :])
                dp = dot_back(values[:, lanes], do_two[j])
                inner = jnp.sum(p * dp, axis=0, keepdims=True)
                ds = (p * (dp - inner)).astype(LOW)
                dv_now = dot(p.astype(LOW), do_two[j])
                dk_now = dot(ds, qs_two[j])
                dk = dk_now if dk is None else dk + dk_now
                dv = dv_now if dv is None else dv + dv_now
                dq.append(dot(keys_t[head * HEAD_DIM : (head + 1) * HEAD_DIM], ds) * SCALING)
            high_lanes = slice(h + pair * 128, h + pair * 128 + 128)
            for value, where in ((dk, lanes), (dv, high_lanes)):
                if not late:
                    acc_own[0][:, where] = value[:n]
                    acc_sib[0][:, where] = value[n:]
                else:
                    acc_sib[0][:, where] += value[:n]
                    acc_own[1][:, where] = value[n : 2 * n]
                    acc_own[0][:, where] += value[2 * n :] * (1.0 - outside)
                    acc_sib[1][:, where] = value[2 * n :] * outside
        dq_refs[late][...] = jnp.concatenate(dq, axis=0).T.astype(LOW)
    sums_ref[...] = sums

    for i in (0, 1):
        keep_refs[i][...] = acc_own[i][...]
        send = acc_sib[i][...].astype(LOW)
        w = send.shape[1] // 4
        send_refs[i][...] = jnp.concatenate(
            [send[:, w : 2 * w], send[:, :w], send[:, 3 * w :], send[:, 2 * w : 3 * w]], axis=1
        )


def attend_back(outer, mids, parts, gots, grads, gain, wo, qs, owns, sibs, biases, lses):
    n, d = mids[0].shape
    h = qs[0].shape[1]
    two = lambda *dims, dtype=LOW: [shape(*dims, dtype=dtype)] * 2
    outs = (
        two(n, d, dtype=FULL) + two(n, d) + [shape(2, d, dtype=FULL)] + two(n, h) + two(n, 2 * h, dtype=FULL)
        + two(n, 2 * h)
    )
    got = call(
        attend_back_kernel,
        (outer, *mids, *parts, *gots, *grads, gain, *wo, *qs, *owns, *sibs, *biases, *lses),
        outs,
        2 * n * h * (10 * (biases[0].shape[0] + biases[1].shape[0]) + 2 * d),
        scalars=1,
        scratch=[pltpu.VMEM((n, 2 * h), LOW)] + [pltpu.VMEM((n, 2 * h), FULL)] * 4,
    )
    return got[0:2], got[2:4], got[4], got[5:7], got[7:9], got[9:11]


def project_back_kernel(dq, keep, got, w_own, w_sib, own_ref, sib_ref, part_ref):
    dkv = (keep[...] + got[...].astype(FULL)).astype(LOW)
    w = dkv.shape[1] // 4
    own = jnp.concatenate([dq[:, :w], dkv[:, :w], dkv[:, 2 * w : 3 * w]], axis=1)
    sib = jnp.concatenate([dq[:, w:], dkv[:, w : 2 * w], dkv[:, 3 * w :]], axis=1)
    own_ref[...] = own
    sib_ref[...] = sib
    part_ref[...] = (dot(own, w_own[...]) + dot(sib, w_sib[...])).astype(LOW)


def project_back(dq, keep, got, w_own, w_sib):
    n = dq.shape[0]
    w, d = w_own.shape
    outs = [shape(n, w), shape(n, w), shape(n, d)]
    return call(project_back_kernel, (dq, keep, got, w_own, w_sib), outs, 2 * n * d * 2 * w)


def body(
    inputs, cotangent, segments, ln1_gain, ln1_bias, w_query, w_key, w_value, w_out,
    ln2_gain, ln2_bias, w_up, b_up, w_down, b_down, *, n_batch,
):
    n = inputs.shape[1]
    section = lax.axis_index("section")
    tensor = lax.axis_index("tensor")
    on_first = section == 0
    early = tensor < 2
    outer = (tensor == 0) | (tensor == 3)
    outer_flag = outer.astype(jnp.int32).reshape(1)
    segment = jnp.where(on_first, segments[0, 0], segments[1, 0])

    def low_high(both):
        own = jnp.where(on_first, both[0], both[1])
        other = to_partner(own)
        return jnp.where(early, own, other), jnp.where(early, other, own)

    low_at = jnp.where(outer, 0, 1)
    block_at = {"own_low": low_at, "sib_low": 1 - low_at, "own_high": 3 - low_at, "sib_high": 2 + low_at}

    def block_bias(query, key_blocks):
        span = jnp.arange(n)
        query_at = block_at[query] * n + span
        query_seg = lax.dynamic_slice_in_dim(segment, block_at[query] * n, n)
        rows = []
        for key in key_blocks:
            key_at = key * n + span
            key_seg = lax.dynamic_slice_in_dim(segment, key * n, n)
            kept = (key_at[:, None] <= query_at[None, :]) & (key_seg[:, None] == query_seg[None, :])
            rows.append(jnp.where(kept, 0.0, MASKED).astype(FULL))
        return jnp.concatenate(rows, axis=0)

    bias_low = block_bias("own_low", [block_at["own_low"], block_at["sib_low"]])
    bias_high = block_bias(
        "own_high",
        [block_at["sib_low"], block_at["own_high"], jnp.where(outer, block_at["sib_high"], block_at["own_low"])],
    )
    biases = (bias_low, bias_high)

    rows_in = low_high(inputs)
    grad_last = low_high(cotangent)

    small_own = jnp.concatenate([ln1_gain, ln1_bias, ln2_gain, ln2_bias, b_down, b_up], axis=0)
    small_other = lax.ppermute(small_own, "section", SWAP)
    qkv_own = jnp.concatenate([w_query[0].T, w_key[0].T, w_value[0].T], axis=0)
    quarters_own = [qkv_own, w_out[0], w_up[0], w_down[0]]
    quarters_other = []
    after = None
    for quarter in quarters_own:
        if after is not None:
            quarter, _ = lax.optimization_barrier((quarter, after))
        after = lax.ppermute(quarter, "section", SWAP)
        quarters_other.append(after)

    def layer_weights(layer):
        here = section == layer
        quarters = [jnp.where(here, a, b) for a, b in zip(quarters_own, quarters_other)]
        pairs = [(q, to_sibling(q)) for q in quarters]
        small = jnp.where(here, small_own, small_other)
        rows = [small[i : i + 1] for i in range(6)]
        return rows[:5] + [(rows[5], to_sibling(rows[5]))], pairs

    small_0, weights_0 = layer_weights(0)
    small_1, weights_1 = layer_weights(1)

    def attention(projected, wo):
        lo, hi = projected
        sib = [to_sibling(p[4]) for p in projected]
        own = [p[3] for p in projected]
        o_lo = attend(False, lo[2], (own[0], sib[0]), biases[0], *wo, None)
        got_lo = to_partner(o_lo[2])
        o_hi = attend(True, hi[2], (sib[0], own[1], sib[1], own[0]), biases[1], *wo, outer_flag)
        got_hi = to_partner(o_hi[2])
        return (o_lo, o_hi), (got_lo, got_hi), own, sib

    qkv, wo, up, dn = weights_0
    proj_0 = [project((rows_in[i],), small_0[0], small_0[1], *qkv, True) for i in (0, 1)]
    att_0, got, own_0, sib_0 = attention(proj_0, wo)
    feed_0, feed_got = [], []
    for i in (0, 1):
        feed_0.append(feed(proj_0[i][0], att_0[i][2], got[i], small_0[2], small_0[3], up, small_0[5], dn))
        feed_got.append(to_partner(feed_0[i][4]))

    qkv, wo, up, dn = weights_1
    proj_1 = [
        project((feed_0[i][0], feed_0[i][4], feed_got[i], small_0[4]), small_1[0], small_1[1], *qkv, False)
        for i in (0, 1)
    ]
    att_1, got, own_1, sib_1 = attention(proj_1, wo)
    feed_1, back_got = [], []
    for i in (0, 1):
        feed_1.append(
            feed(proj_1[i][0], att_1[i][2], got[i], small_1[2], small_1[3], up, small_1[5], dn, grad_last[i])
        )
        back_got.append(to_partner(feed_1[i][4]))

    half = up[0].shape[1]

    def join(two):
        return jnp.concatenate(two, axis=0)

    def grads_feed(g, grads, a_two, dz):
        g, grads, a_two, dz = map(join, (g, grads, a_two, dz))
        return [
            (dot_rows(a_two, dz[:, i : i + half]).astype(LOW), dot_rows(g[:, i : i + half], grads).astype(LOW))
            for i in (0, half)
        ]

    def grads_attend(o, lows, a_one, d_own, d_sib):
        o, lows, a_one = map(join, (o, lows, a_one))
        w = o.shape[1] // 2
        return [
            (dot_rows(join(d), a_one).astype(LOW), dot_rows(o[:, i : i + w], lows).astype(LOW))
            for i, d in ((0, d_own), (w, d_sib))
        ]

    def attention_back(mids, parts, gots, grads, gain, wo, projected, own, sib, att, qkv):
        mid_grads, lows, sums, dq, keep, send = attend_back(
            outer_flag, mids, parts, gots, grads, gain, wo, [p[2] for p in projected], own, sib, biases,
            [a[1] for a in att],
        )
        back = [project_back(dq[i], keep[i], to_sibling(send[i]), *qkv) for i in (0, 1)]
        return mid_grads, lows, sums, back

    mids = [f[0] for f in feed_1]
    mid_grads_1, lows_1, sums_two_1, back_1 = attention_back(
        mids, [f[4] for f in feed_1], back_got, grad_last, small_1[2], wo, proj_1, own_1, sib_1, att_1, qkv
    )
    part_got = [to_partner(b[2]) for b in back_1]
    by_feed_1 = grads_feed([f[2] for f in feed_1], grad_last, [f[1] for f in feed_1], [f[3] for f in feed_1])
    by_att_1 = grads_attend(
        [a[0] for a in att_1], lows_1, [p[1] for p in proj_1], [b[0] for b in back_1], [b[1] for b in back_1]
    )

    gain_one_1 = small_1[0]
    qkv, wo, up, dn = weights_0
    fb_0, back_got = [], []
    for i in (0, 1):
        fb_0.append(
            feed_back(mid_grads_1[i], back_1[i][2], part_got[i], proj_1[i][0], gain_one_1, feed_0[i][3], up, dn)
        )
        back_got.append(to_partner(fb_0[i][3]))
    grad_mid = [f[0] for f in fb_0]
    mid_grads_0, lows_0, sums_two_0, back_0 = attention_back(
        [f[0] for f in feed_0], [f[3] for f in fb_0], back_got, grad_mid, small_0[2], wo, proj_0, own_0, sib_0,
        att_0, qkv,
    )
    by_feed_0 = grads_feed([f[2] for f in feed_0], grad_mid, [f[1] for f in feed_0], [f[2] for f in fb_0])
    by_att_0 = grads_attend(
        [a[0] for a in att_0], lows_0, [p[1] for p in proj_0], [b[0] for b in back_0], [b[1] for b in back_0]
    )
    part_got = [to_partner(b[2]) for b in back_0]
    last, sums_one_0 = [], 0.0
    for i in (0, 1):
        grad_norm = back_0[i][2].astype(FULL) + part_got[i].astype(FULL)
        normed, inverse = norm_rows(rows_in[i].astype(FULL))
        last.append((mid_grads_0[i] + norm_back(grad_norm, normed, inverse, small_0[0])).astype(LOW))
        sums_one_0 += jnp.stack([jnp.sum(grad_norm * normed, axis=0), jnp.sum(grad_norm, axis=0)])
    sums_one_1 = fb_0[0][1] + fb_0[1][1]

    outs_1 = []
    for i in (0, 1):
        part = (dot(feed_1[i][2][:, :half], weights_1[3][0]) + dot(feed_1[i][2][:, half:], weights_1[3][1])).astype(LOW)
        total = part.astype(FULL) + to_partner(part).astype(FULL)
        outs_1.append((feed_1[i][0] + total + small_1[4]).astype(LOW))

    def ready(first, second):
        first, second = [own.astype(FULL) + to_sibling(sib).astype(FULL) for own, sib in (first, second)]
        return jnp.where(on_first, first, second).astype(LOW), jnp.where(on_first, second, first).astype(LOW)

    def side(both, kind):
        return tuple(part[kind] for part in both)

    w_rows = by_att_0[0][1].shape[0]
    f_rows = half // 2
    feed_parts = [ready(side(by_feed_0, kind), side(by_feed_1, kind)) for kind in (1, 0)]
    att_parts = [ready(side(by_att_0, kind), side(by_att_1, kind)) for kind in (1, 0)]
    cuts = [(part, k * f_rows, f_rows) for part in feed_parts for k in (0, 1)]
    cuts += [(att_parts[0], 0, w_rows)] + [(att_parts[1], k * w_rows, w_rows) for k in range(3)]
    pieces = [tuple(x[at : at + size] for x in part) for part, at, size in cuts]
    crossed = [lax.ppermute(theirs, "section", SWAP) for _, theirs in pieces]

    sums_two = [sums_two_0, sums_two_1]
    last_rows = [fb_0[0][1][2:] + fb_0[1][1][2:], feed_1[0][6] + feed_1[1][6]]
    sums_one = [sums_one_0, fb_0[0][1][:2] + fb_0[1][1][:2]]
    hidden = [fb_0[0][4] + fb_0[1][4], feed_1[0][5] + feed_1[1][5]]
    rows = join([join([a, b, c]) for a, b, c in zip(sums_one, sums_two, last_rows)])
    count = rows.shape[0]
    hidden_own = join([x[:, :half] for x in hidden])
    hidden_sib = join([x[:, half:] for x in hidden])
    five = count // 2

    def to_both(values):
        got = to_sibling(join([values, hidden_sib]))
        return values + got[:count], hidden_own + got[count:]

    def to_all(both):
        values = (both[0] + to_partner(both[0])) * 0.5
        a = join([values[:five], both[1][:1]])
        b = join([values[five:], both[1][1:]])
        return jnp.where(on_first, a, b) + lax.ppermute(jnp.where(on_first, b, a), "section", SWAP)

    def doubled(distance):
        return lambda x: x + lax.ppermute(x, "batch", [(i, i ^ distance) for i in range(n_batch)])

    small_steps = [to_both, to_all]
    if n_batch & (n_batch - 1):
        small_steps.append(lambda x: lax.psum(x, "batch"))
    else:
        distance = 1
        while distance < n_batch:
            small_steps.append(doubled(distance))
            distance *= 2

    if n_batch == 4:
        batch = lax.axis_index("batch")
        middle = (batch == 1) | (batch == 2)
        stage = [None] * len(pieces)
        latest = rows

        def added(left, right):
            left, right, _ = lax.optimization_barrier((left, right, latest))
            return left + right

        small = rows
        for turn in range(len(pieces) + 3):
            if turn < len(pieces):
                k = turn
                latest = added(pieces[k][0], crossed[k])
                stage[k] = (latest, lax.ppermute(latest, "batch", [(0, 1), (3, 2)]))
            if 0 <= turn - 1 < len(pieces):
                k = turn - 1
                latest = added(*stage[k])
                stage[k] = (latest, lax.ppermute(latest, "batch", [(1, 2), (2, 1)]))
            if 0 <= turn - 2 < len(pieces):
                k = turn - 2
                latest = added(*stage[k])
                stage[k] = (latest, lax.ppermute(latest, "batch", [(1, 0), (2, 3)]))
            if 0 <= turn - 3 < len(pieces):
                k = turn - 3
                low, got, _ = lax.optimization_barrier((*stage[k], latest))
                stage[k] = jnp.where(middle, low, got).astype(FULL)
            if turn >= 6 and small_steps:
                small = small_steps.pop(0)(small)
    else:
        small = rows
        stage = [lax.psum(mine + got, "batch").astype(FULL) for (mine, _), got in zip(pieces, crossed)]
    for step in small_steps:
        small = step(small)
    sums = small
    total_feed = [join(stage[2:4]), join(stage[0:2])]
    total_out = stage[4]
    total_qkv = [x.T[None] for x in stage[5:8]]

    def both_micro(first, second):
        first, second = jnp.where(early, *first), jnp.where(early, *second)
        mine = jnp.where(on_first, first, second)
        theirs = lax.ppermute(jnp.where(on_first, second, first), "section", SWAP)
        return jnp.stack([jnp.where(on_first, mine, theirs), jnp.where(on_first, theirs, mine)])[None]

    forward_out = both_micro([p[0] for p in proj_1], outs_1)
    backward_out = both_micro(last, [f[0] for f in fb_0])
    return (
        forward_out,
        backward_out,
        sums[0:1],
        sums[1:2],
        *total_qkv,
        total_out[None],
        sums[2:3],
        sums[3:4],
        total_feed[0][None],
        sums[5:6],
        total_feed[1][None],
        sums[4:5],
    )


def solution(mesh):
    rows = P(None, ("batch", "tensor"), None)
    layer = P("section", None)
    by_column = P("section", None, "tensor")
    by_row = P("section", "tensor", None)
    kept = P("section", None, ("batch", "tensor"), None)
    return jax.shard_map(
        functools.partial(body, n_batch=mesh.shape["batch"]),
        mesh=mesh,
        in_specs=(
            rows, rows, P(None, "batch", None), layer, layer, by_column, by_column, by_column, by_row,
            layer, layer, by_column, P("section", "tensor"), by_row, layer,
        ),
        out_specs=(
            kept, kept, layer, layer, by_column, by_column, by_column, by_row,
            layer, layer, by_column, P("section", "tensor"), by_row, layer,
        ),
        check_vma=False,
    )
```

```python
import functools

import jax
import jax.numpy as jnp
from jax import lax
from jax.experimental import pallas as pl
from jax.experimental.pallas import tpu as pltpu
from jax.sharding import PartitionSpec as P

HEAD_DIM = 64
EPSILON = 1e-05
LOW = jnp.bfloat16
FULL = jnp.float32
SCALING = HEAD_DIM**-0.5
MASKED = -1e30
VMEM_BYTES = 16 * 1024 * 1024

SIBLING = [(0, 1), (1, 0), (2, 3), (3, 2)]
PARTNER = [(0, 3), (3, 0), (1, 2), (2, 1)]
SWAP = [(0, 1), (1, 0)]


def dot(left, right):
    return jnp.dot(left, right, preferred_element_type=FULL)


def dot_rows(left, right):
    return lax.dot_general(left, right, (((0,), (0,)), ((), ())), preferred_element_type=FULL)


def dot_back(left, right):
    return lax.dot_general(left, right, (((1,), (1,)), ((), ())), preferred_element_type=FULL)


def norm_rows(values):
    center = values - jnp.mean(values, axis=-1, keepdims=True)
    inverse = lax.rsqrt(jnp.mean(center * center, axis=-1, keepdims=True) + EPSILON)
    return center * inverse, inverse


def norm_back(grad_norm, normed, inverse, gain):
    scaled = grad_norm * gain
    mean_one = jnp.mean(scaled, axis=-1, keepdims=True)
    mean_two = jnp.mean(scaled * normed, axis=-1, keepdims=True)
    return inverse * (scaled - mean_one - normed * mean_two)


def to_partner(value):
    return lax.ppermute(value, "tensor", PARTNER)


def to_sibling(value):
    return lax.ppermute(value, "tensor", SIBLING)


LATEST = []
CHAINED = [False]
PACE = 6e7


def call(kernel, operands, outs, scalars=0, scratch=(), after=(), micros=0.6):
    after = (*LATEST, *after) if CHAINED[0] else tuple(after)
    count, waited = len(operands), len(after)
    specs = [pl.BlockSpec(memory_space=pltpu.SMEM)] * scalars
    specs += [pl.BlockSpec(memory_space=pltpu.VMEM)] * (count - scalars)
    specs += [pl.BlockSpec(memory_space=pl.ANY)] * waited
    got = pl.pallas_call(
        lambda *refs: kernel(*refs[:count], *refs[count + waited :]),
        out_shape=tuple(outs),
        in_specs=specs,
        out_specs=tuple(pl.BlockSpec(memory_space=pltpu.VMEM) for _ in outs),
        scratch_shapes=list(scratch),
        compiler_params=pltpu.CompilerParams(vmem_limit_bytes=VMEM_BYTES),
        cost_estimate=pl.CostEstimate(flops=int(micros * PACE), bytes_accessed=1024, transcendentals=0),
    )(*operands, *after)
    LATEST[:] = [min(got, key=lambda array: array.size)]
    return got


def shape(*dims, dtype=LOW):
    return jax.ShapeDtypeStruct(dims, dtype)


def halves(pieces):
    middle = len(pieces) // 2
    return pieces[:middle], pieces[middle:]


def stacked(pieces, axis=0):
    return jnp.concatenate([p[...] for p in pieces], axis=axis) if len(pieces) > 1 else pieces[0][...]


def project_kernel(first, *refs):
    if first:
        rows_ref, gain, bias, *ws, a_ref, q_ref, kv_ref, send_ref = refs
        layer_in = rows_ref[...].astype(FULL)
    else:
        mid, part, got, b_down, gain, bias, *ws, in_ref, a_ref, q_ref, kv_ref, send_ref = refs
        low = (mid[...] + (part[...].astype(FULL) + got[...].astype(FULL)) + b_down[...]).astype(LOW)
        in_ref[...] = low
        layer_in = low.astype(FULL)
    normed, _ = norm_rows(layer_in)
    a_one = (normed * gain[...] + bias[...]).astype(LOW)
    a_ref[...] = a_one
    own, sib = [dot_back(a_one, stacked(w)).astype(LOW) for w in halves(ws)]
    w = own.shape[1] // 3
    q_own, k_own, v_own = own[:, :w], own[:, w : 2 * w], own[:, 2 * w :]
    q_sib, k_sib, v_sib = sib[:, :w], sib[:, w : 2 * w], sib[:, 2 * w :]
    q_ref[...] = jnp.concatenate([q_own, q_sib], axis=1) * jnp.asarray(SCALING, LOW)
    kv_ref[...] = jnp.concatenate([k_own, k_sib, v_own, v_sib], axis=1)
    send_ref[...] = jnp.concatenate([k_sib, k_own, v_sib, v_own], axis=1)


def project(source, gain, bias, weights, first, after=()):
    n, d = source[0].shape
    h = sum(w.shape[0] for w in weights) // 3
    outs = [shape(n, d), shape(n, h), shape(n, 2 * h), shape(n, 2 * h)]
    if not first:
        outs = [shape(n, d)] + outs
    got = call(
        functools.partial(project_kernel, first),
        (*source, gain, bias, *weights),
        outs,
        after=after,
        micros=1.1,
    )
    return got if not first else (source[0], *got)


def pair_masks(q_pair):
    lane = lax.broadcasted_iota(jnp.int32, q_pair.shape, 1)
    zero = jnp.zeros_like(q_pair)
    return jnp.where(lane < HEAD_DIM, q_pair, zero), jnp.where(lane < HEAD_DIM, zero, q_pair)


def attend_kernel(late, *refs):
    if late:
        outer, q_ref, sib_low, own_high, sib_high, own_low, bias_ref, wo_own, wo_sib, o_ref, lse_ref, part_ref, extra = refs

        @pl.when(outer[0] == 1)
        def _():
            extra[...] = sib_high[...]

        @pl.when(outer[0] == 0)
        def _():
            extra[...] = own_low[...]

        kv = jnp.concatenate([sib_low[...], own_high[...], extra[...]], axis=0)
    else:
        q_ref, own_low, sib_low, bias_ref, wo_own, wo_sib, o_ref, lse_ref, part_ref = refs
        kv = jnp.concatenate([own_low[...], sib_low[...]], axis=0)
    h = kv.shape[1] // 2
    keys, values = kv[:, :h], kv[:, h:]
    values_t = values.T
    outs, sums = [], []
    for pair in range(h // 128):
        lanes = slice(pair * 128, pair * 128 + 128)
        for j, q in enumerate(pair_masks(q_ref[:, lanes])):
            head = 2 * pair + j
            scores = dot_back(keys[:, lanes], q) + bias_ref[...]
            highest = jnp.max(scores, axis=0, keepdims=True)
            e = jnp.exp(scores - highest)
            total = jnp.sum(e, axis=0, keepdims=True)
            mixed = dot(values_t[head * HEAD_DIM : (head + 1) * HEAD_DIM], e.astype(LOW))
            outs.append(mixed * (1.0 / total))
            sums.append(highest + jnp.log(total))
    o = jnp.concatenate(outs, axis=0).T.astype(LOW)
    o_ref[...] = o
    lse_ref[...] = jnp.concatenate(sums + sums[: 8 - len(sums)], axis=0)
    half = wo_own.shape[0]
    part_ref[...] = (dot(o[:, :half], wo_own[...]) + dot(o[:, half:], wo_sib[...])).astype(LOW)


def attend(late, q, blocks, bias, wo_own, wo_sib, outer, after=()):
    n, h = q.shape
    d = wo_own.shape[1]
    operands = ((outer,) if late else ()) + (q, *blocks, bias, wo_own, wo_sib)
    return call(
        functools.partial(attend_kernel, late),
        operands,
        [shape(n, h), shape(8, n, dtype=FULL), shape(n, d)],
        scalars=1 if late else 0,
        scratch=[pltpu.VMEM((n, 2 * h), LOW)] if late else (),
        after=after,
        micros=4.5 if late else 3.2,
    )


def gelu_parts(z):
    c = 0.7978845608028654
    square = z * z
    t = jnp.tanh(c * (z + 0.044715 * (square * z)))
    half = 0.5 * (1.0 + t)
    return z * half, half + 0.5 * z * (1.0 - t * t) * (c + (3.0 * 0.044715 * c) * square)


def feed_kernel(last, ups, dns, *refs):
    refs = (*refs[:7], refs[7 : 7 + ups], refs[7 + ups : 7 + ups + dns], *refs[7 + ups + dns :])
    if last:
        (u, part, got, gain, bias, b_own, b_sib, ups, dns, grad_ref,
         mid_ref, a_ref, g_ref, dz_ref, back_ref, hidden_sum, row_sum) = refs
    else:
        (u, part, got, gain, bias, b_own, b_sib, ups, dns,
         mid_ref, a_ref, g_ref, slope_ref, out_ref) = refs
    mid = u[...].astype(FULL) + (part[...].astype(FULL) + got[...].astype(FULL))
    mid_ref[...] = mid
    normed, _ = norm_rows(mid)
    a_two = (normed * gain[...] + bias[...]).astype(LOW)
    a_ref[...] = a_two
    f = b_own.shape[1]
    step = 256
    total = jnp.zeros(mid.shape, FULL)
    for side, (up, b, dn) in enumerate(zip(halves(ups), (b_own, b_sib), halves(dns))):
        up, dn = stacked(up, axis=1), stacked(dn)
        for at in range(0, f, step):
            cols = slice(at, at + step)
            here = slice(side * f + at, side * f + at + step)
            z = dot(a_two, up[:, cols]) + b[:, cols]
            g, slope = gelu_parts(z)
            g = g.astype(LOW)
            g_ref[:, here] = g
            if last:
                dz = (dot_back(grad_ref[...], dn[cols, :]) * slope).astype(LOW)
                dz_ref[:, here] = dz
                hidden_sum[:, here] = jnp.sum(dz.astype(FULL), axis=0, keepdims=True)
                total = total + dot_back(dz, up[:, cols])
            else:
                slope_ref[:, here] = slope.astype(LOW)
                total = total + dot(g, dn[cols, :])
    if last:
        back_ref[...] = total.astype(LOW)
        row_sum[...] = jnp.sum(grad_ref[...].astype(FULL), axis=0, keepdims=True)
    else:
        out_ref[...] = total.astype(LOW)


def feed(u, part, got, gain, bias, up, b_up, dn, grad=None, after=()):
    n, d = u.shape
    f = b_up[0].shape[1]
    last = grad is not None
    outs = [shape(n, d, dtype=FULL), shape(n, d), shape(n, 2 * f), shape(n, 2 * f), shape(n, d)]
    operands = (u, part, got, gain, bias, *b_up, *up, *dn) + ((grad,) if last else ())
    if last:
        outs += [shape(1, 2 * f, dtype=FULL), shape(1, d, dtype=FULL)]
    return call(functools.partial(feed_kernel, last, len(up), len(dn)), operands, outs, after=after, micros=3.2)


def feed_back_kernel(ups, dns, mid_grad, part, got, in_ref, gain, slope, *refs):
    grad_ref, sums_ref, dz_ref, back_ref, hidden_sum = refs[ups + dns :]
    ups, dns = refs[:ups], refs[ups : ups + dns]
    grad_norm = part[...].astype(FULL) + got[...].astype(FULL)
    normed, inverse = norm_rows(in_ref[...].astype(FULL))
    grad = (mid_grad[...] + norm_back(grad_norm, normed, inverse, gain[...])).astype(LOW)
    grad_ref[...] = grad
    sums_ref[...] = jnp.concatenate(
        [
            jnp.sum(grad_norm * normed, axis=0, keepdims=True),
            jnp.sum(grad_norm, axis=0, keepdims=True),
            jnp.sum(grad.astype(FULL), axis=0, keepdims=True),
        ],
        axis=0,
    )
    f = slope.shape[1] // 2
    step = 256
    total = jnp.zeros(grad.shape, FULL)
    for side, (up, dn) in enumerate(zip(halves(ups), halves(dns))):
        up, dn = stacked(up, axis=1), stacked(dn)
        for at in range(0, f, step):
            cols = slice(at, at + step)
            here = slice(side * f + at, side * f + at + step)
            dz = (dot_back(grad, dn[cols, :]) * slope[:, here].astype(FULL)).astype(LOW)
            dz_ref[:, here] = dz
            hidden_sum[:, here] = jnp.sum(dz.astype(FULL), axis=0, keepdims=True)
            total = total + dot_back(dz, up[:, cols])
    back_ref[...] = total.astype(LOW)


def feed_back(mid_grad, part, got, layer_in, gain, slope, up, dn, after=()):
    n, d = mid_grad.shape
    f = slope.shape[1] // 2
    outs = [shape(n, d), shape(3, d, dtype=FULL), shape(n, 2 * f), shape(n, d), shape(1, 2 * f, dtype=FULL)]
    return call(
        functools.partial(feed_back_kernel, len(up), len(dn)), (mid_grad, part, got, layer_in, gain, slope, *up, *dn), outs, after=after, micros=2.9
    )


def attend_back_kernel(outer, *refs):
    (mids, parts, gots, grads, gain, wo_own, wo_sib, qs, owns, sibs, biases, lses) = (
        refs[0:2], refs[2:4], refs[4:6], refs[6:8], refs[8], refs[9], refs[10], refs[11:13], refs[13:15],
        refs[15:17], refs[17:19], refs[19:21],
    )
    mid_grads, lows, sums_ref, dq_refs, keep_refs, send_refs = (
        refs[21:23], refs[23:25], refs[25], refs[26:28], refs[28:30], refs[30:32]
    )
    extra, acc_own, acc_sib = refs[32], refs[33:35], refs[35:37]
    n = mids[0].shape[0]
    outside = outer[0].astype(FULL)

    @pl.when(outer[0] == 1)
    def _():
        extra[...] = sibs[1][...]

    @pl.when(outer[0] == 0)
    def _():
        extra[...] = owns[0][...]

    sums = None
    for late in (0, 1):
        grad_norm = parts[late][...].astype(FULL) + gots[late][...].astype(FULL)
        normed, inverse = norm_rows(mids[late][...])
        mid_grad = grads[late][...].astype(FULL) + norm_back(grad_norm, normed, inverse, gain[...])
        mid_grads[late][...] = mid_grad
        low = mid_grad.astype(LOW)
        lows[late][...] = low
        now = jnp.concatenate(
            [jnp.sum(grad_norm * normed, axis=0, keepdims=True), jnp.sum(grad_norm, axis=0, keepdims=True)], axis=0
        )
        sums = now if sums is None else sums + now
        do = jnp.concatenate([dot_back(low, wo_own[...]), dot_back(low, wo_sib[...])], axis=1).astype(LOW)
        blocks = (sibs[0], owns[1], extra) if late else (owns[0], sibs[0])
        kv = jnp.concatenate([b[...] for b in blocks], axis=0)
        h = kv.shape[1] // 2
        keys, values = kv[:, :h], kv[:, h:]
        keys_t = keys.T
        dq = []
        for pair in range(h // 128):
            lanes = slice(pair * 128, pair * 128 + 128)
            dk = dv = None
            qs_two, do_two = pair_masks(qs[late][:, lanes]), pair_masks(do[:, lanes])
            for j in (0, 1):
                head = 2 * pair + j
                scores = dot_back(keys[:, lanes], qs_two[j]) + biases[late][...]
                p = jnp.exp(scores - lses[late][head : head + 1, :])
                dp = dot_back(values[:, lanes], do_two[j])
                inner = jnp.sum(p * dp, axis=0, keepdims=True)
                ds = (p * (dp - inner)).astype(LOW)
                dv_now = dot(p.astype(LOW), do_two[j])
                dk_now = dot(ds, qs_two[j])
                dk = dk_now if dk is None else dk + dk_now
                dv = dv_now if dv is None else dv + dv_now
                dq.append(dot(keys_t[head * HEAD_DIM : (head + 1) * HEAD_DIM], ds) * SCALING)
            high_lanes = slice(h + pair * 128, h + pair * 128 + 128)
            for value, where in ((dk, lanes), (dv, high_lanes)):
                if not late:
                    acc_own[0][:, where] = value[:n]
                    acc_sib[0][:, where] = value[n:]
                else:
                    acc_sib[0][:, where] += value[:n]
                    acc_own[1][:, where] = value[n : 2 * n]
                    acc_own[0][:, where] += value[2 * n :] * (1.0 - outside)
                    acc_sib[1][:, where] = value[2 * n :] * outside
        dq_refs[late][...] = jnp.concatenate(dq, axis=0).T.astype(LOW)
    sums_ref[...] = sums

    for i in (0, 1):
        keep_refs[i][...] = acc_own[i][...]
        send = acc_sib[i][...].astype(LOW)
        w = send.shape[1] // 4
        send_refs[i][...] = jnp.concatenate(
            [send[:, w : 2 * w], send[:, :w], send[:, 3 * w :], send[:, 2 * w : 3 * w]], axis=1
        )


def attend_back(outer, mids, parts, gots, grads, gain, wo, qs, owns, sibs, biases, lses, after=()):
    n, d = mids[0].shape
    h = qs[0].shape[1]
    two = lambda *dims, dtype=LOW: [shape(*dims, dtype=dtype)] * 2
    outs = (
        two(n, d, dtype=FULL) + two(n, d) + [shape(2, d, dtype=FULL)] + two(n, h) + two(n, 2 * h, dtype=FULL)
        + two(n, 2 * h)
    )
    got = call(
        attend_back_kernel,
        (outer, *mids, *parts, *gots, *grads, gain, *wo, *qs, *owns, *sibs, *biases, *lses),
        outs,
        scalars=1,
        scratch=[pltpu.VMEM((n, 2 * h), LOW)] + [pltpu.VMEM((n, 2 * h), FULL)] * 4,
        after=after,
        micros=9.5,
    )
    return got[0:2], got[2:4], got[4], got[5:7], got[7:9], got[9:11]


def project_back_kernel(dq, keep, got, *refs):
    *ws, own_ref, sib_ref, part_ref = refs
    dkv = (keep[...] + got[...].astype(FULL)).astype(LOW)
    w = dkv.shape[1] // 4
    own = jnp.concatenate([dq[:, :w], dkv[:, :w], dkv[:, 2 * w : 3 * w]], axis=1)
    sib = jnp.concatenate([dq[:, w:], dkv[:, w : 2 * w], dkv[:, 3 * w :]], axis=1)
    own_ref[...] = own
    sib_ref[...] = sib
    w_own, w_sib = [stacked(x) for x in halves(ws)]
    part_ref[...] = (dot(own, w_own) + dot(sib, w_sib)).astype(LOW)


def project_back(dq, keep, got, weights):
    n = dq.shape[0]
    w, d = sum(x.shape[0] for x in weights) // 2, weights[0].shape[1]
    outs = [shape(n, w), shape(n, w), shape(n, d)]
    return call(project_back_kernel, (dq, keep, got, *weights), outs, micros=0.9)


def outer_kernel(plan, *refs):
    outs = refs[-2:]
    for lefts, first, count, rights, at, width, which, base in plan:
        right = jnp.concatenate([refs[i][:, at : at + width] for i in rights], axis=0)
        for row in range(0, count, 256):
            size = min(256, count - row)
            cols = slice(first + row, first + row + size)
            left = jnp.concatenate([refs[i][:, cols] for i in lefts], axis=0)
            outs[which][base + row : base + row + size, :] = dot_rows(left, right).astype(LOW)


def outer_products(operands, plan, rows, width, after=()):
    return call(functools.partial(outer_kernel, plan), operands, [shape(rows, width)] * 2, after=after, micros=2.5)


def down_kernel(count, *refs):
    gs, dns, outs = refs[:2], refs[2 : 2 + count], refs[2 + count :]
    dn = stacked(dns)
    for g, out in zip(gs, outs):
        out[...] = dot(g[...], dn).astype(LOW)


def down(gs, dns, after=()):
    n, d = gs[0].shape[0], dns[0].shape[1]
    return call(functools.partial(down_kernel, len(dns)), (*gs, *dns), [shape(n, d)] * 2, after=after, micros=1.4)


def ready_kernel(cuts, flags, first_own, first_got, second_own, second_got, *outs):
    on_first = flags[1] == 1
    for i, (at, size) in enumerate(cuts):
        rows = slice(at, at + size)
        first = (first_own[rows, :].astype(FULL) + first_got[rows, :].astype(FULL)).astype(LOW)
        second = (second_own[rows, :].astype(FULL) + second_got[rows, :].astype(FULL)).astype(LOW)
        mine, theirs = outs[2 * i], outs[2 * i + 1]

        @pl.when(on_first)
        def _():
            mine[...] = first
            theirs[...] = second

        @pl.when(flags[1] == 0)
        def _():
            mine[...] = second
            theirs[...] = first


def ready_pieces(flags, first, second, sizes):
    cuts, at = [], 0
    for size in sizes:
        cuts.append((at, size))
        at += size
    width = first[0].shape[1]
    outs = [shape(size, width) for size in sizes for _ in (0, 1)]
    got = call(functools.partial(ready_kernel, tuple(cuts)), (flags, *first, *second), outs, scalars=1)
    return [(got[2 * i], got[2 * i + 1]) for i in range(len(sizes))]


def added_kernel(left, right, out):
    out[...] = (left[...].astype(FULL) + right[...].astype(FULL)).astype(out.dtype)


def sums_kernel(*refs):
    count = len(refs) // 3
    for i in range(count):
        refs[2 * count + i][...] = (refs[2 * i][...].astype(FULL) + refs[2 * i + 1][...].astype(FULL)).astype(LOW)


def added(left, right, after=()):
    return call(added_kernel, (left, right), [shape(*left.shape, dtype=left.dtype)], after=after)[0]


def chosen_kernel(count, which, flags, *refs):
    sums, gots, outs = refs[:count], refs[count : 2 * count], refs[2 * count :]
    for flag, pieces in ((1, sums), (0, gots)):

        @pl.when(flags[which] == flag)
        def _():
            first = 0
            for out in outs:
                at, last = 0, first + out.shape[0]
                for piece in pieces:
                    low, high = max(first, at), min(last, at + piece.shape[0])
                    if low < high:
                        out[low - first : high - first, :] = piece[low - at : high - at, :].astype(FULL)
                    at += piece.shape[0]
                first = last


def chosen(flags, stages, sizes, which):
    if which is None:
        flags, which = jnp.ones_like(flags), 0
    operands = (flags, *[low for low, _ in stages], *[got for _, got in stages])
    outs = [shape(size, stages[0][0].shape[1], dtype=FULL) for size in sizes]
    return call(functools.partial(chosen_kernel, len(stages), which), operands, outs, scalars=1)


def last_kernel(flags, part_low, part_high, got, mid_low, mid_high, in_low, in_high, gain, out, sums):
    for flag, part, mid, rows in ((1, part_low, mid_low, in_low), (0, part_high, mid_high, in_high)):

        @pl.when(flags[4] == flag)
        def _():
            grad_norm = part[...].astype(FULL) + got[...].astype(FULL)
            normed, inverse = norm_rows(rows[...].astype(FULL))
            out[...] = (mid[...] + norm_back(grad_norm, normed, inverse, gain[...])).astype(LOW)
            sums[0:1, :] = 2.0 * jnp.sum(grad_norm * normed, axis=0, keepdims=True)
            sums[1:2, :] = 2.0 * jnp.sum(grad_norm, axis=0, keepdims=True)


def last_rows(flags, parts, got, mids, rows, gain):
    n, d = got.shape
    return call(
        last_kernel, (flags, *parts, got, *mids, *rows, gain), [shape(n, d), shape(2, d, dtype=FULL)], scalars=1,
        micros=1.0,
    )


def gather_kernel(one_0, one_lo, one_hi, two_0, two_1, down_lo, down_hi, up_lo_0, up_hi_0, up_lo_1, up_hi_1, rows, own):
    half = own.shape[1]
    both = one_lo[...] + one_hi[...]
    rows[0:2, :] = one_0[...]
    rows[2:4, :] = two_0[...]
    rows[4:5, :] = both[2:3]
    rows[5:7, :] = both[0:2]
    rows[7:9, :] = two_1[...]
    rows[9:10, :] = down_lo[...] + down_hi[...]
    for i, hidden in enumerate((up_lo_0[...] + up_hi_0[...], up_lo_1[...] + up_hi_1[...])):
        rows[10 + i : 11 + i, :] = hidden[:, half:]
        own[i : i + 1, :] = hidden[:, :half]


def chip_kernel(rows, own, got, out):
    out[0:10, :] = rows[0:10, :] + got[0:10, :]
    out[10:12, :] = own[...] + got[10:12, :]


def layers_kernel(flags, rows, got, mine, theirs):
    both = (rows[0:10, :] + got[0:10, :]) * 0.5
    for flag, first, second in ((1, mine, theirs), (0, theirs, mine)):

        @pl.when(flags[1] == flag)
        def _():
            first[0:5, :] = both[0:5]
            first[5:6, :] = rows[10:11, :]
            second[0:5, :] = both[5:10]
            second[5:6, :] = rows[11:12, :]


def fill(out, wholes, axis, first):
    if axis:
        out[...] = wholes[0][:, first : first + out.shape[1]]
        return
    at, last = 0, first + out.shape[0]
    for whole in wholes:
        low, high = max(first, at), min(last, at + whole.shape[0])
        if low < high:
            out[low - first : high - first, :] = whole[low - at : high - at, :]
        at += whole.shape[0]


def half_kernel(axis, flags, *refs):
    *wholes, out = refs
    for flag in (1, 0):

        @pl.when(flags[3] == flag)
        def _():
            fill(out, wholes, axis, 0 if flag else out.shape[axis])


def half_of(flags, wholes, axis, after=()):
    dims = [sum(w.shape[0] for w in wholes), wholes[0].shape[1]]
    dims[axis] //= 2
    return call(functools.partial(half_kernel, axis), (flags, *wholes), [shape(*dims)], scalars=1, after=after)[0]


def pick_kernel(layer, count, got_count, flags, *refs):
    wholes, gots, outs = refs[:count], refs[count : count + got_count], refs[count + got_count :]
    ways = [(flags[1] == 1 - layer, wholes), (flags[1] == layer, gots)]
    if got_count == 2:
        ways = [ways[0]] + [((flags[1] == layer) & (flags[3] == flag), gots[::step]) for flag, step in ((1, 1), (0, -1))]
    for wanted, sources in ways:

        @pl.when(wanted)
        def _():
            at = 0
            for out in outs:
                fill(out, sources, 0, at)
                at += out.shape[0]


def picked(flags, layer, wholes, gots, sizes, after=()):
    outs = [shape(size, wholes[0].shape[1]) for size in sizes]
    kernel = functools.partial(pick_kernel, layer, len(wholes), len(gots))
    return call(kernel, (flags, *wholes, *gots), outs, scalars=1, after=after)


def stack_kernel(*refs):
    *wholes, out = refs
    fill(out, wholes, 0, 0)


def stacked_rows(wholes, after):
    rows = sum(w.shape[0] for w in wholes)
    return call(stack_kernel, wholes, [shape(rows, wholes[0].shape[1])], after=after)[0]


def copy_kernel(source, out):
    out[...] = source[...]


def copied(source, after):
    return call(copy_kernel, (source,), [shape(*source.shape)], after=after)[0]


def micro_kernel(flags, both, out):
    for flag in (1, 0):

        @pl.when(flags[1] == flag)
        def _():
            out[...] = both[1 - flag]


def output_kernel(flags, mid_low, mid_high, part_low, part_high, got, bias, out):
    for flag, mid, part in ((1, mid_low, part_low), (0, mid_high, part_high)):

        @pl.when(flags[4] == flag)
        def _():
            out[...] = (mid[...] + (part[...].astype(FULL) + got[...].astype(FULL)) + bias[...]).astype(LOW)


def own_kernel(flags, if_low, if_high, out):
    for flag, rows in ((1, if_low), (0, if_high)):

        @pl.when(flags[4] == flag)
        def _():
            out[...] = rows[...]


def own_or(flags, if_low, if_high, after=()):
    return call(own_kernel, (flags, if_low, if_high), [shape(*if_low.shape)], scalars=1, after=after)[0]


def output_rows(flags, mids, parts, got, bias):
    return call(output_kernel, (flags, *mids, *parts, got, bias), [shape(*got.shape)], scalars=1)[0]


def body(
    inputs, cotangent, segments, ln1_gain, ln1_bias, w_query, w_key, w_value, w_out,
    ln2_gain, ln2_bias, w_up, b_up, w_down, b_down, *, n_batch,
):
    LATEST.clear()
    CHAINED[0] = False
    n, d = inputs.shape[1:]
    half = w_up.shape[2]
    section = lax.axis_index("section")
    tensor = lax.axis_index("tensor")
    batch = lax.axis_index("batch")
    on_first = section == 0
    early = tensor < 2
    outer = (tensor == 0) | (tensor == 3)
    middle = (batch == 1) | (batch == 2)
    even = batch % 2 == 0
    flags = jnp.stack([outer, on_first, middle, even, early]).astype(jnp.int32)
    paired = n_batch % 2 == 0
    beside = [(i, i ^ 1) for i in range(n_batch)]

    def across(value):
        return lax.ppermute(value, "section", SWAP)

    qkv_parts = (w_query[0].T, w_key[0].T, w_value[0].T)
    if paired:
        got_qkv = across(half_of(flags, qkv_parts, 0))
    else:
        got_qkv = across(jnp.concatenate(qkv_parts, axis=0))
    own_in = call(micro_kernel, (flags, inputs), [shape(n, d)], scalars=1)[0]
    other_in = to_partner(own_in)
    own_cot = call(micro_kernel, (flags, cotangent), [shape(n, d)], scalars=1)[0]
    other_cot = to_partner(own_cot)
    small_own = jnp.concatenate([ln1_gain, ln1_bias, ln2_gain, ln2_bias, b_down, b_up], axis=0)
    small_other = across(small_own)
    got_wo = across(copied(w_out[0], (got_qkv,)))
    got_feed = across(stacked_rows((w_up[0], w_down[0]), (got_wo,)))
    gots_qkv = (got_qkv, lax.ppermute(got_qkv, "batch", beside)) if paired else jnp.split(got_qkv, 2)

    def low_high(own, other):
        return jnp.where(early, own, other), jnp.where(early, other, own)

    rows_in = low_high(own_in, other_in)
    grad_last = low_high(own_cot, other_cot)

    segment = jnp.where(on_first, segments[0, 0], segments[1, 0])
    low_at = jnp.where(outer, 0, 1)
    block_at = {"own_low": low_at, "sib_low": 1 - low_at, "own_high": 3 - low_at, "sib_high": 2 + low_at}

    def block_bias(query, key_blocks):
        span = jnp.arange(n)
        query_at = block_at[query] * n + span
        query_seg = lax.dynamic_slice_in_dim(segment, block_at[query] * n, n)
        rows = []
        for key in key_blocks:
            key_at = key * n + span
            key_seg = lax.dynamic_slice_in_dim(segment, key * n, n)
            kept = (key_at[:, None] <= query_at[None, :]) & (key_seg[:, None] == query_seg[None, :])
            rows.append(jnp.where(kept, 0.0, MASKED).astype(FULL))
        return jnp.concatenate(rows, axis=0)

    biases = (
        block_bias("own_low", [block_at["own_low"], block_at["sib_low"]]),
        block_bias(
            "own_high",
            [block_at["sib_low"], block_at["own_high"], jnp.where(outer, block_at["sib_high"], block_at["own_low"])],
        ),
    )

    def layer_rows(layer):
        small = jnp.where(section == layer, small_own, small_other)
        rows = [small[i : i + 1] for i in range(6)]
        return rows[:5] + [(rows[5], to_sibling(rows[5]))]

    small_0, small_1 = layer_rows(0), layer_rows(1)

    def weights(layer, wholes, gots, sizes, after):
        return [(own, to_sibling(own)) for own in picked(flags, layer, wholes, gots, sizes, after)]

    def qkv_weight(layer, after=()):
        return weights(layer, qkv_parts, gots_qkv, [3 * w_query.shape[2]], after)[0]

    def out_weight(layer, after=()):
        return weights(layer, (w_out[0],), (got_wo,), [w_out.shape[1]], after)[0]

    def feed_weights(layer, after=()):
        return weights(layer, (w_up[0], w_down[0]), (got_feed,), [d, half], after)

    def attend_low(projected, sib, wo):
        return attend(False, projected[2], (projected[3], sib[0]), biases[0], *wo, None)

    def attend_high(both, sib, wo):
        return attend(True, both[1][2], (sib[0], both[1][3], sib[1], both[0][3]), biases[1], *wo, flags)

    qkv_0 = qkv_weight(0, (got_wo,))
    wo_0 = out_weight(0)
    tied = (other_cot, small_0[5][1], small_1[5][1])
    proj_0, sib_0 = [], []
    for i in (0, 1):
        proj_0.append(project((rows_in[i],), small_0[0], small_0[1], qkv_0, True, tied))
        sib_0.append(to_sibling(proj_0[i][4]))
    att_0 = [attend_low(proj_0[0], sib_0, wo_0)]
    got = [to_partner(att_0[0][2])]
    att_0.append(attend_high(proj_0, sib_0, wo_0))
    got.append(to_partner(att_0[1][2]))
    up_0, down_0 = feed_weights(0, got)
    feed_0, feed_got, after = [], [], ()
    for i in (0, 1):
        feed_0.append(
            feed(proj_0[i][0], att_0[i][2], got[i], small_0[2], small_0[3], up_0, small_0[5], down_0, after=after)
        )
        feed_got.append(to_partner(feed_0[i][4]))
        if i == 0:
            qkv_1 = qkv_weight(1, (feed_0[0][4],))
            wo_1 = out_weight(1, (feed_0[0][4],))
            after = (qkv_1[0], wo_1[0])

    proj_1, sib_1, att_1, got, after = [], [], [], [], ()
    for i in (0, 1):
        source = (feed_0[i][0], feed_0[i][4], feed_got[i], small_0[4])
        proj_1.append(project(source, small_1[0], small_1[1], qkv_1, False, after))
        sib_1.append(to_sibling(proj_1[i][4]))
        if i == 0:
            up_1, down_1 = feed_weights(1, (proj_1[0][2],))
            after = (up_1[0], down_1[0])
            att_1.append(attend_low(proj_1[0], sib_1, wo_1))
        else:
            att_1.append(attend_high(proj_1, sib_1, wo_1))
        got.append(to_partner(att_1[i][2]))
    feed_1, back_got = [], []
    for i in (0, 1):
        feed_1.append(
            feed(proj_1[i][0], att_1[i][2], got[i], small_1[2], small_1[3], up_1, small_1[5], down_1, grad_last[i])
        )
        back_got.append(to_partner(feed_1[i][4]))

    def grads_feed(g, grads, a_two, dz):
        plan = (
            ((4, 5), 0, d, (6, 7), 0, half, 0, 0),
            ((4, 5), 0, d, (6, 7), half, half, 1, 0),
            ((0, 1), 0, half, (2, 3), 0, d, 0, d),
            ((0, 1), half, half, (2, 3), 0, d, 1, d),
        )
        return outer_products((*g, *grads, *a_two, *dz), plan, d + half, d)

    def grads_attend(o, lows, a_one, d_own, d_sib):
        w, w3 = o[0].shape[1] // 2, d_own[0].shape[1]
        plan = (
            ((6, 7), 0, w3, (4, 5), 0, d, 0, 0),
            ((8, 9), 0, w3, (4, 5), 0, d, 1, 0),
            ((0, 1), 0, w, (2, 3), 0, d, 0, w3),
            ((0, 1), w, w, (2, 3), 0, d, 1, w3),
        )
        return outer_products((*o, *lows, *a_one, *d_own, *d_sib), plan, w3 + w, d)

    mids = [f[0] for f in feed_1]
    by_feed_1 = grads_feed([f[2] for f in feed_1], grad_last, [f[1] for f in feed_1], [f[3] for f in feed_1])
    feed_1_got = to_sibling(by_feed_1[1])
    out_parts = down([f[2] for f in feed_1], down_1)
    mid_grads_1, lows_1, two_1, dq, keep, send = attend_back(
        flags, mids, [f[4] for f in feed_1], back_got, grad_last, small_1[2], wo_1, [p[2] for p in proj_1],
        [p[3] for p in proj_1], sib_1, biases, [a[1] for a in att_1], (*out_parts, *by_feed_1),
    )
    kv_got = [to_sibling(x) for x in send]
    back_1, part_got = [], []
    for i in (0, 1):
        back_1.append(project_back(dq[i], keep[i], kv_got[i], qkv_1))
        part_got.append(to_partner(back_1[i][2]))
    by_att_1 = grads_attend(
        [a[0] for a in att_1], lows_1, [p[1] for p in proj_1], [b[0] for b in back_1], [b[1] for b in back_1]
    )
    att_1_got = to_sibling(by_att_1[1])

    fb_0, back_got, after = [], [], by_att_1
    for i in (0, 1):
        fb_0.append(
            feed_back(
                mid_grads_1[i], back_1[i][2], part_got[i], proj_1[i][0], small_1[0], feed_0[i][3], up_0, down_0, after
            )
        )
        after = ()
        back_got.append(to_partner(fb_0[i][3]))
    grad_mid = [f[0] for f in fb_0]
    by_feed_0 = grads_feed([f[2] for f in feed_0], grad_mid, [f[1] for f in feed_0], [f[2] for f in fb_0])
    feed_0_got = to_sibling(by_feed_0[1])

    CHAINED[0] = True
    along = [[(0, 1), (3, 2)], [(1, 2), (2, 1)], [(1, 0), (2, 3)]]
    feed_pieces = ready_pieces(
        flags, (by_feed_0[0], feed_0_got), (by_feed_1[0], feed_1_got), [(d + half) // 4] * 4
    )
    stage, hops = {}, {}

    def begin(k, piece):
        stage[k], hops[k] = (piece[0], across(piece[1])), 0

    def advance(*ks, after=()):
        if n_batch != 4:
            ks = [k for k in ks if hops[k] == 0]
        if not ks:
            return
        values = call(
            sums_kernel, [x for k in ks for x in stage[k]], [shape(*stage[k][0].shape) for k in ks],
            after=[stage[k][1] for k in after], micros=0.5 * len(ks),
        )
        for k, value in zip(ks, values):
            stage[k] = (value, lax.ppermute(value, "batch", along[hops[k]]) if n_batch == 4 else value)
            hops[k] += 1

    def settled(ks, sizes):
        if n_batch == 4:
            return chosen(flags, [stage[k] for k in ks], sizes, 2)
        return chosen(flags, [(lax.psum(stage[k][0], "batch"), stage[k][0]) for k in ks], sizes, None)

    begin(0, feed_pieces[0])
    begin(1, feed_pieces[1])
    advance(0)
    begin(2, feed_pieces[2])
    mid_grads_0, lows_0, two_0, dq, keep, send = attend_back(
        flags, [f[0] for f in feed_0], [f[3] for f in fb_0], back_got, grad_mid, small_0[2], wo_0,
        [p[2] for p in proj_0], [p[3] for p in proj_0], sib_0, biases, [a[1] for a in att_0],
    )
    advance(1)
    begin(3, feed_pieces[3])
    kv_got = [to_sibling(x) for x in send]
    back_0 = [project_back(dq[i], keep[i], kv_got[i], qkv_0) for i in (0, 1)]
    part_got = to_partner(own_or(flags, back_0[1][2], back_0[0][2]))
    by_att_0 = grads_attend(
        [a[0] for a in att_0], lows_0, [p[1] for p in proj_0], [b[0] for b in back_0], [b[1] for b in back_0]
    )
    att_0_got = to_sibling(by_att_0[1])
    advance(0, 2)
    att_rows = by_att_0[0].shape[0]
    att_pieces = ready_pieces(flags, (by_att_0[0], att_0_got), (by_att_1[0], att_1_got), [att_rows // 2] * 2)
    begin(4, att_pieces[0])
    begin(5, att_pieces[1])
    last, one_0 = last_rows(flags, [b[2] for b in back_0], part_got, mid_grads_0, rows_in, small_0[0])

    def both_micro(first, second):
        mine = jnp.where(on_first, first, second)
        theirs = across(jnp.where(on_first, second, first))
        return jnp.stack([jnp.where(on_first, mine, theirs), jnp.where(on_first, theirs, mine)])[None]

    backward_out = both_micro(last, jnp.where(early, *grad_mid))

    def output_sent():
        return to_partner(own_or(flags, out_parts[1], out_parts[0]))

    def output_done(got):
        out_1 = output_rows(flags, mids, out_parts, got, small_1[4])
        return both_micro(jnp.where(early, *[p[0] for p in proj_1]), out_1)

    def sums_gathered():
        operands = (
            one_0, fb_0[0][1], fb_0[1][1], two_0, two_1, feed_1[0][6], feed_1[1][6], fb_0[0][4], fb_0[1][4],
            feed_1[0][5], feed_1[1][5],
        )
        rows, own = call(gather_kernel, operands, [shape(12, d, dtype=FULL), shape(2, half, dtype=FULL)])
        return rows, own, to_sibling(rows)

    def sums_chip(rows, own, got):
        rows = call(chip_kernel, (rows, own, got), [shape(12, d, dtype=FULL)])[0]
        return rows, to_partner(rows)

    def sums_layers(rows, got):
        mine, theirs = call(layers_kernel, (flags, rows, got), [shape(6, d, dtype=FULL)] * 2, scalars=1)
        return mine, across(theirs)

    def sums_on(distance):
        def step(left, right):
            value = added(left, right)
            return value, lax.ppermute(value, "batch", [(i, i ^ distance) for i in range(n_batch)])

        return step

    side = [lambda: (output_sent(),), lambda got: (output_done(got),)]
    sums_steps = [sums_gathered, sums_chip, sums_layers]
    whole_power = n_batch & (n_batch - 1) == 0
    distance = 1
    while whole_power and distance < n_batch:
        sums_steps.append(sums_on(distance))
        distance *= 2
    sums_steps.append(lambda left, right: (added(left, right),))
    advance(1, 3)
    sums_state = sums_gathered()
    advance(0, 2, 4)
    sums_state = sums_chip(*sums_state)
    out_state = side[0]()
    advance(1, 3, 5)
    sums_state = sums_layers(*sums_state)
    advance(2, 4, after=(0,))
    out_state = side[1](*out_state)
    advance(3, 5, after=(1,))
    up_total = settled((0, 1), [d])[0]
    for step in sums_steps[3:-1]:
        sums_state = step(*sums_state)
    advance(4, after=(2,))
    sums_state = sums_steps[-1](*sums_state)
    advance(5, after=(3,))
    down_total = settled((2, 3), [half])[0]
    att_totals = settled((4, 5), [att_rows // 4] * 4)
    forward_out = out_state[0]
    sums = sums_state[0] if whole_power else lax.psum(sums_state[0], "batch")
    return (
        forward_out,
        backward_out,
        sums[0:1],
        sums[1:2],
        *[x.T[None] for x in att_totals[:3]],
        att_totals[3][None],
        sums[2:3],
        sums[3:4],
        up_total[None],
        sums[5:6],
        down_total[None],
        sums[4:5],
    )


def solution(mesh):
    rows = P(None, ("batch", "tensor"), None)
    layer = P("section", None)
    by_column = P("section", None, "tensor")
    by_row = P("section", "tensor", None)
    kept = P("section", None, ("batch", "tensor"), None)
    return jax.shard_map(
        functools.partial(body, n_batch=mesh.shape["batch"]),
        mesh=mesh,
        in_specs=(
            rows, rows, P(None, "batch", None), layer, layer, by_column, by_column, by_column, by_row,
            layer, layer, by_column, P("section", "tensor"), by_row, layer,
        ),
        out_specs=(
            kept, kept, layer, layer, by_column, by_column, by_column, by_row,
            layer, layer, by_column, P("section", "tensor"), by_row, layer,
        ),
        check_vma=False,
    )
```

```python
import functools

import jax
import jax.numpy as jnp
from jax import lax
from jax.experimental import pallas as pl
from jax.experimental.pallas import tpu as pltpu
from jax.sharding import PartitionSpec as P

HEAD_DIM = 64
EPSILON = 1e-05
LOW = jnp.bfloat16
FULL = jnp.float32
SCALING = HEAD_DIM**-0.5
EXTRA = 32
MASKED = -1e30
VMEM_BYTES = 16 * 1024 * 1024

SIBLING = [(0, 1), (1, 0), (2, 3), (3, 2)]
PARTNER = [(0, 3), (3, 0), (1, 2), (2, 1)]
SWAP = [(0, 1), (1, 0)]


def dot(left, right):
    return jnp.dot(left, right, preferred_element_type=FULL)


def dot_rows(left, right):
    return lax.dot_general(left, right, (((0,), (0,)), ((), ())), preferred_element_type=FULL)


def dot_back(left, right):
    return lax.dot_general(left, right, (((1,), (1,)), ((), ())), preferred_element_type=FULL)


def norm_rows(values):
    center = values - jnp.mean(values, axis=-1, keepdims=True)
    inverse = lax.rsqrt(jnp.mean(center * center, axis=-1, keepdims=True) + EPSILON)
    return center * inverse, inverse


def norm_back(grad_norm, normed, inverse, gain):
    scaled = grad_norm * gain
    mean_one = jnp.mean(scaled, axis=-1, keepdims=True)
    mean_two = jnp.mean(scaled * normed, axis=-1, keepdims=True)
    return inverse * (scaled - mean_one - normed * mean_two)


def to_partner(value):
    return lax.ppermute(value, "tensor", PARTNER)


def to_sibling(value):
    return lax.ppermute(value, "tensor", SIBLING)


LATEST = []
CHAINED = [False]
PACE = 6e7


def call(kernel, operands, outs, scalars=0, scratch=(), after=(), micros=0.6):
    after = (*LATEST, *after) if CHAINED[0] else tuple(after)
    count, waited = len(operands), len(after)
    specs = [pl.BlockSpec(memory_space=pltpu.SMEM)] * scalars
    specs += [pl.BlockSpec(memory_space=pltpu.VMEM)] * (count - scalars)
    specs += [pl.BlockSpec(memory_space=pl.ANY)] * waited
    got = pl.pallas_call(
        lambda *refs: kernel(*refs[:count], *refs[count + waited :]),
        out_shape=tuple(outs),
        in_specs=specs,
        out_specs=tuple(pl.BlockSpec(memory_space=pltpu.VMEM) for _ in outs),
        scratch_shapes=list(scratch),
        compiler_params=pltpu.CompilerParams(vmem_limit_bytes=VMEM_BYTES),
        cost_estimate=pl.CostEstimate(flops=int(micros * PACE), bytes_accessed=1024, transcendentals=0),
    )(*operands, *after)
    LATEST[:] = [min(got, key=lambda array: array.size)]
    return got


def shape(*dims, dtype=LOW):
    return jax.ShapeDtypeStruct(dims, dtype)


def halves(pieces):
    middle = len(pieces) // 2
    return pieces[:middle], pieces[middle:]


def stacked(pieces, axis=0):
    return jnp.concatenate([p[...] for p in pieces], axis=axis) if len(pieces) > 1 else pieces[0][...]


def project_kernel(first, *refs):
    if first:
        rows_ref, gain, bias, *ws, a_ref, q_ref, kv_ref, send_ref = refs
        layer_in = rows_ref[...].astype(FULL)
    else:
        mid, part, got, b_down, gain, bias, *ws, in_ref, a_ref, q_ref, kv_ref, send_ref = refs
        low = (mid[...] + (part[...].astype(FULL) + got[...].astype(FULL)) + b_down[...]).astype(LOW)
        in_ref[...] = low
        layer_in = low.astype(FULL)
    normed, _ = norm_rows(layer_in)
    a_one = (normed * gain[...] + bias[...]).astype(LOW)
    a_ref[...] = a_one
    own, sib = [dot_back(a_one, stacked(w)).astype(LOW) for w in halves(ws)]
    w = own.shape[1] // 3
    q_own, k_own, v_own = own[:, :w], own[:, w : 2 * w], own[:, 2 * w :]
    q_sib, k_sib, v_sib = sib[:, :w], sib[:, w : 2 * w], sib[:, 2 * w :]
    q_ref[...] = jnp.concatenate([q_own, q_sib], axis=1) * jnp.asarray(SCALING, LOW)
    kv_ref[...] = jnp.concatenate([k_own, k_sib, v_own, v_sib], axis=1)
    send_ref[...] = jnp.concatenate([k_sib, k_own, v_sib, v_own], axis=1)


def project(source, gain, bias, weights, first, after=()):
    n, d = source[0].shape
    h = sum(w.shape[0] for w in weights) // 3
    outs = [shape(n, d), shape(n, h), shape(n, 2 * h), shape(n, 2 * h)]
    if not first:
        outs = [shape(n, d)] + outs
    got = call(
        functools.partial(project_kernel, first),
        (*source, gain, bias, *weights),
        outs,
        after=after,
        micros=1.1,
    )
    return got if not first else (source[0], *got)


def pair_masks(q_pair):
    lane = lax.broadcasted_iota(jnp.int32, q_pair.shape, 1)
    zero = jnp.zeros_like(q_pair)
    return jnp.where(lane < HEAD_DIM, q_pair, zero), jnp.where(lane < HEAD_DIM, zero, q_pair)


def attend_kernel(late, *refs):
    if late:
        outer, q_ref, sib_low, own_high, sib_high, own_low, bias_ref, wo_own, wo_sib, o_ref, lse_ref, part_ref, extra = refs

        @pl.when(outer[0] == 1)
        def _():
            extra[...] = sib_high[...]

        @pl.when(outer[0] == 0)
        def _():
            extra[...] = own_low[...]

        kv = jnp.concatenate([sib_low[...], own_high[...], extra[...]], axis=0)
    else:
        q_ref, own_low, sib_low, bias_ref, wo_own, wo_sib, o_ref, lse_ref, part_ref = refs
        kv = jnp.concatenate([own_low[...], sib_low[...]], axis=0)
    h = kv.shape[1] // 2
    keys, values = kv[:, :h], kv[:, h:]
    values_t = values.T
    outs, sums = [], []
    for pair in range(h // 128):
        lanes = slice(pair * 128, pair * 128 + 128)
        for j, q in enumerate(pair_masks(q_ref[:, lanes])):
            head = 2 * pair + j
            scores = dot_back(keys[:, lanes], q) + bias_ref[...]
            highest = jnp.max(scores, axis=0, keepdims=True)
            e = jnp.exp(scores - highest)
            total = jnp.sum(e, axis=0, keepdims=True)
            mixed = dot(values_t[head * HEAD_DIM : (head + 1) * HEAD_DIM], e.astype(LOW))
            outs.append(mixed * (1.0 / total))
            sums.append(highest + jnp.log(total))
    o = jnp.concatenate(outs, axis=0).T.astype(LOW)
    o_ref[...] = o
    lse_ref[...] = jnp.concatenate(sums + sums[: 8 - len(sums)], axis=0)
    half = wo_own.shape[0]
    part_ref[...] = (dot(o[:, :half], wo_own[...]) + dot(o[:, half:], wo_sib[...])).astype(LOW)


def attend(late, q, blocks, bias, wo_own, wo_sib, outer, after=()):
    n, h = q.shape
    d = wo_own.shape[1]
    operands = ((outer,) if late else ()) + (q, *blocks, bias, wo_own, wo_sib)
    return call(
        functools.partial(attend_kernel, late),
        operands,
        [shape(n, h), shape(8, n, dtype=FULL), shape(n, d)],
        scalars=1 if late else 0,
        scratch=[pltpu.VMEM((n, 2 * h), LOW)] if late else (),
        after=after,
        micros=4.5 if late else 3.2,
    )


def gelu_parts(z):
    c = 0.7978845608028654
    square = z * z
    t = jnp.tanh(c * (z + 0.044715 * (square * z)))
    half = 0.5 * (1.0 + t)
    return z * half, half + 0.5 * z * (1.0 - t * t) * (c + (3.0 * 0.044715 * c) * square)


def feed_kernel(last, ups, dns, *refs):
    refs = (*refs[:7], refs[7 : 7 + ups], refs[7 + ups : 7 + ups + dns], *refs[7 + ups + dns :])
    if last:
        (u, part, got, gain, bias, b_own, b_sib, ups, dns, grad_ref,
         mid_ref, a_ref, g_ref, dz_ref, back_ref, hidden_sum, row_sum) = refs
    else:
        (u, part, got, gain, bias, b_own, b_sib, ups, dns,
         mid_ref, a_ref, g_ref, slope_ref, out_ref) = refs
    mid = u[...].astype(FULL) + (part[...].astype(FULL) + got[...].astype(FULL))
    mid_ref[...] = mid
    normed, _ = norm_rows(mid)
    a_two = (normed * gain[...] + bias[...]).astype(LOW)
    a_ref[...] = a_two
    f = b_own.shape[1]
    step = 256
    total = jnp.zeros(mid.shape, FULL)
    for side, (up, b, dn) in enumerate(zip(halves(ups), (b_own, b_sib), halves(dns))):
        up, dn = stacked(up, axis=1), stacked(dn)
        for at in range(0, f, step):
            cols = slice(at, at + step)
            here = slice(side * f + at, side * f + at + step)
            z = dot(a_two, up[:, cols]) + b[:, cols]
            g, slope = gelu_parts(z)
            g = g.astype(LOW)
            g_ref[:, here] = g
            if last:
                dz = (dot_back(grad_ref[...], dn[cols, :]) * slope).astype(LOW)
                dz_ref[:, here] = dz
                hidden_sum[:, here] = jnp.sum(dz.astype(FULL), axis=0, keepdims=True)
                total = total + dot_back(dz, up[:, cols])
            else:
                slope_ref[:, here] = slope.astype(LOW)
                total = total + dot(g, dn[cols, :])
    if last:
        back_ref[...] = total.astype(LOW)
        row_sum[...] = jnp.sum(grad_ref[...].astype(FULL), axis=0, keepdims=True)
    else:
        out_ref[...] = total.astype(LOW)


def feed(u, part, got, gain, bias, up, b_up, dn, grad=None, after=()):
    n, d = u.shape
    f = b_up[0].shape[1]
    last = grad is not None
    outs = [shape(n, d, dtype=FULL), shape(n, d), shape(n, 2 * f), shape(n, 2 * f), shape(n, d)]
    operands = (u, part, got, gain, bias, *b_up, *up, *dn) + ((grad,) if last else ())
    if last:
        outs += [shape(1, 2 * f, dtype=FULL), shape(1, d, dtype=FULL)]
    return call(functools.partial(feed_kernel, last, len(up), len(dn)), operands, outs, after=after, micros=3.2)


def feed_back_kernel(ups, dns, mid_grad, part, got, in_ref, gain, slope, *refs):
    grad_ref, sums_ref, dz_ref, back_ref, hidden_sum = refs[ups + dns :]
    ups, dns = refs[:ups], refs[ups : ups + dns]
    grad_norm = part[...].astype(FULL) + got[...].astype(FULL)
    normed, inverse = norm_rows(in_ref[...].astype(FULL))
    grad = (mid_grad[...] + norm_back(grad_norm, normed, inverse, gain[...])).astype(LOW)
    grad_ref[...] = grad
    sums_ref[...] = jnp.concatenate(
        [
            jnp.sum(grad_norm * normed, axis=0, keepdims=True),
            jnp.sum(grad_norm, axis=0, keepdims=True),
            jnp.sum(grad.astype(FULL), axis=0, keepdims=True),
        ],
        axis=0,
    )
    f = slope.shape[1] // 2
    step = 256
    total = jnp.zeros(grad.shape, FULL)
    for side, (up, dn) in enumerate(zip(halves(ups), halves(dns))):
        up, dn = stacked(up, axis=1), stacked(dn)
        for at in range(0, f, step):
            cols = slice(at, at + step)
            here = slice(side * f + at, side * f + at + step)
            dz = (dot_back(grad, dn[cols, :]) * slope[:, here].astype(FULL)).astype(LOW)
            dz_ref[:, here] = dz
            hidden_sum[:, here] = jnp.sum(dz.astype(FULL), axis=0, keepdims=True)
            total = total + dot_back(dz, up[:, cols])
    back_ref[...] = total.astype(LOW)


def feed_back(mid_grad, part, got, layer_in, gain, slope, up, dn, after=()):
    n, d = mid_grad.shape
    f = slope.shape[1] // 2
    outs = [shape(n, d), shape(3, d, dtype=FULL), shape(n, 2 * f), shape(n, d), shape(1, 2 * f, dtype=FULL)]
    return call(
        functools.partial(feed_back_kernel, len(up), len(dn)), (mid_grad, part, got, layer_in, gain, slope, *up, *dn), outs, after=after, micros=2.9
    )


def attend_back_kernel(late, *refs):
    if late:
        (flags, mid, part, got, grad, gain, wo_own, wo_sib, q_ref, bias, lse, own_low, own_high, sib_low, sib_high,
         low_kept, low_sent, mid_ref, low_ref, sums_ref, dq_ref, keep_low, keep_high, send_low, send_high,
         extra, acc_low, acc_high) = refs
        outside = flags[0].astype(FULL)

        @pl.when(flags[0] == 1)
        def _():
            extra[...] = sib_high[...]

        @pl.when(flags[0] == 0)
        def _():
            extra[...] = own_low[...]

        blocks = (sib_low, own_high, extra)
    else:
        (mid, part, got, grad, gain, wo_own, wo_sib, q_ref, bias, lse, own_low, sib_low,
         mid_ref, low_ref, sums_ref, dq_ref, keep_low, acc_low) = refs
        blocks = (own_low, sib_low)
    n = mid.shape[0]
    grad_norm = part[...].astype(FULL) + got[...].astype(FULL)
    normed, inverse = norm_rows(mid[...])
    mid_grad = grad[...].astype(FULL) + norm_back(grad_norm, normed, inverse, gain[...])
    mid_ref[...] = mid_grad
    low = mid_grad.astype(LOW)
    low_ref[...] = low
    sums_ref[0:1, :] = jnp.sum(grad_norm * normed, axis=0, keepdims=True)
    sums_ref[1:2, :] = jnp.sum(grad_norm, axis=0, keepdims=True)
    do = jnp.concatenate([dot_back(low, wo_own[...]), dot_back(low, wo_sib[...])], axis=1).astype(LOW)
    kv = jnp.concatenate([b[...] for b in blocks], axis=0)
    h = kv.shape[1] // 2
    keys, values = kv[:, :h], kv[:, h:]
    keys_t = keys.T
    dq = []
    for pair in range(h // 128):
        lanes = slice(pair * 128, pair * 128 + 128)
        dk = dv = None
        qs_two, do_two = pair_masks(q_ref[:, lanes]), pair_masks(do[:, lanes])
        for j in (0, 1):
            head = 2 * pair + j
            scores = dot_back(keys[:, lanes], qs_two[j]) + bias[...]
            p = jnp.exp(scores - lse[head : head + 1, :])
            dp = dot_back(values[:, lanes], do_two[j])
            inner = jnp.sum(p * dp, axis=0, keepdims=True)
            ds = (p * (dp - inner)).astype(LOW)
            dv_now = dot(p.astype(LOW), do_two[j])
            dk_now = dot(ds, qs_two[j])
            dk = dk_now if dk is None else dk + dk_now
            dv = dv_now if dv is None else dv + dv_now
            dq.append(dot(keys_t[head * HEAD_DIM : (head + 1) * HEAD_DIM], ds) * SCALING)
        for value, where in ((dk, lanes), (dv, slice(h + pair * 128, h + pair * 128 + 128))):
            if late:
                acc_low[:, where] = low_sent[:, where] + value[:n]
                keep_high[:, where] = value[n : 2 * n]
                keep_low[:, where] = low_kept[:, where] + value[2 * n :] * (1.0 - outside)
                acc_high[:, where] = value[2 * n :] * outside
            else:
                keep_low[:, where] = value[:n]
                acc_low[:, where] = value[n:]
    dq_ref[...] = jnp.concatenate(dq, axis=0).T.astype(LOW)
    if late:
        for acc, out in ((acc_low, send_low), (acc_high, send_high)):
            send = acc[...].astype(LOW)
            w = send.shape[1] // 4
            out[...] = jnp.concatenate(
                [send[:, w : 2 * w], send[:, :w], send[:, 3 * w :], send[:, 2 * w : 3 * w]], axis=1
            )


def attend_back(late, flags, mid, part, got, grad, gain, wo, q, own, sib, bias, lse, earlier, long):
    n, d = mid.shape
    h = q.shape[1]
    outs = [shape(n, d, dtype=FULL), shape(n, d), shape(2, d, dtype=FULL), shape(n, h)]
    outs += [shape(n, 2 * h, dtype=FULL)] * 2
    common = (mid, part, got, grad, gain, *wo, q, bias, lse)
    if late:
        outs += [shape(n, 2 * h)] * 2
        operands = (flags, *common, *own, *sib, *earlier)
    else:
        operands = (*common, own[0], sib[0])
    return call(
        functools.partial(attend_back_kernel, late),
        operands,
        outs,
        scalars=int(late),
        scratch=[pltpu.VMEM((n, 2 * h), LOW)] + [pltpu.VMEM((n, 2 * h), FULL)] * 2 if late else (),
        micros=300.0 if long else 5.5 if late else 4.0,
    )


def project_back_kernel(dq, keep, got, *refs):
    *ws, own_ref, sib_ref, part_ref = refs
    dkv = (keep[...] + got[...].astype(FULL)).astype(LOW)
    w = dkv.shape[1] // 4
    own = jnp.concatenate([dq[:, :w], dkv[:, :w], dkv[:, 2 * w : 3 * w]], axis=1)
    sib = jnp.concatenate([dq[:, w:], dkv[:, w : 2 * w], dkv[:, 3 * w :]], axis=1)
    own_ref[...] = own
    sib_ref[...] = sib
    w_own, w_sib = [stacked(x) for x in halves(ws)]
    part_ref[...] = (dot(own, w_own) + dot(sib, w_sib)).astype(LOW)


def project_back(dq, keep, got, weights):
    n = dq.shape[0]
    w, d = sum(x.shape[0] for x in weights) // 2, weights[0].shape[1]
    outs = [shape(n, w), shape(n, w), shape(n, d)]
    return call(project_back_kernel, (dq, keep, got, *weights), outs, micros=0.9)


def outer_kernel(plan, *refs):
    outs = refs[-2:]
    for lefts, first, count, rights, at, width, which, base in plan:
        right = jnp.concatenate([refs[i][:, at : at + width] for i in rights], axis=0)
        for row in range(0, count, 256):
            size = min(256, count - row)
            cols = slice(first + row, first + row + size)
            left = jnp.concatenate([refs[i][:, cols] for i in lefts], axis=0)
            outs[which][base + row : base + row + size, :] = dot_rows(left, right).astype(LOW)


def outer_products(operands, plan, rows, width, after=()):
    return call(functools.partial(outer_kernel, plan), operands, [shape(rows, width)] * 2, after=after, micros=2.5)


def down_kernel(count, *refs):
    gs, dns, outs = refs[:2], refs[2 : 2 + count], refs[2 + count :]
    dn = stacked(dns)
    for g, out in zip(gs, outs):
        out[...] = dot(g[...], dn).astype(LOW)


def down(gs, dns, after=()):
    n, d = gs[0].shape[0], dns[0].shape[1]
    return call(functools.partial(down_kernel, len(dns)), (*gs, *dns), [shape(n, d)] * 2, after=after, micros=1.4)


def ready_kernel(cuts, extra, flags, first_own, first_got, second_own, second_got, *refs):
    small, outs = refs[:extra], refs[extra:]
    for i, (at, size) in enumerate(cuts):
        rows = slice(at, at + size)
        first = (first_own[rows, :].astype(FULL) + first_got[rows, :].astype(FULL)).astype(LOW)
        second = (second_own[rows, :].astype(FULL) + second_got[rows, :].astype(FULL)).astype(LOW)
        mine, theirs = outs[2 * i], outs[2 * i + 1]

        @pl.when(flags[1] == 1)
        def _():
            mine[:size, :] = first
            theirs[:size, :] = second

        @pl.when(flags[1] == 0)
        def _():
            mine[:size, :] = second
            theirs[:size, :] = first

    for values, out in zip(small, outs[-2:]):
        split_rows(values[...], out)


def split_rows(values, out):
    first = out.shape[0] - EXTRA
    rounded = values.astype(LOW)
    out[first : first + EXTRA // 2, :] = rounded
    out[first + EXTRA // 2 :, :] = (values - rounded.astype(FULL)).astype(LOW)


def joined_rows(ref):
    first = ref.shape[0] - EXTRA
    return ref[first : first + EXTRA // 2, :].astype(FULL) + ref[first + EXTRA // 2 :, :].astype(FULL)


def ready_pieces(flags, first, second, sizes, at=0, small=()):
    cuts = []
    for size in sizes:
        cuts.append((at, size))
        at += size
    width = first[0].shape[1]
    outs = [shape(size, width) for size in sizes for _ in (0, 1)]
    if small:
        outs[-2:] = [shape(sizes[-1] + EXTRA, width)] * 2
    got = call(
        functools.partial(ready_kernel, tuple(cuts), len(small)), (flags, *first, *second, *small), outs, scalars=1
    )
    return [(got[2 * i], got[2 * i + 1]) for i in range(len(sizes))]


def sums_kernel(extra, *refs):
    count = len(refs) // 3
    for i in range(count):
        left, right, out = refs[2 * i], refs[2 * i + 1], refs[2 * count + i]
        if not extra[i]:
            out[...] = (left[...].astype(FULL) + right[...].astype(FULL)).astype(LOW)
        else:
            bulk = slice(0, out.shape[0] - EXTRA)
            out[bulk, :] = (left[bulk, :].astype(FULL) + right[bulk, :].astype(FULL)).astype(LOW)
            split_rows(joined_rows(left) + joined_rows(right), out)


def added(left, right, after=()):
    return call(added_kernel, (left, right), [shape(*left.shape, dtype=left.dtype)], after=after)[0]


def chosen_kernel(count, which, extra, flags, *refs):
    sums, gots, outs = refs[:count], refs[count : 2 * count], refs[2 * count :]
    outs, small = outs[: len(outs) - extra], outs[len(outs) - extra :]
    for flag, pieces in ((1, sums), (0, gots)):

        @pl.when(flags[which] == flag)
        def _():
            first = 0
            for out in outs:
                at, last = 0, first + out.shape[0]
                for piece in pieces:
                    low, high = max(first, at), min(last, at + piece.shape[0])
                    if low < high:
                        out[low - first : high - first, :] = piece[low - at : high - at, :].astype(FULL)
                    at += piece.shape[0]
                first = last
            for out in small:
                out[...] = joined_rows(pieces[-1])


def chosen(flags, stages, sizes, which, extra=False):
    if which is None:
        flags, which = jnp.ones_like(flags), 0
    operands = (flags, *[low for low, _ in stages], *[got for _, got in stages])
    outs = [shape(size, stages[0][0].shape[1], dtype=FULL) for size in (*sizes, EXTRA // 2)[: len(sizes) + extra]]
    return call(functools.partial(chosen_kernel, len(stages), which, int(extra)), operands, outs, scalars=1)


def micro_out_kernel(flags, mine, got, out):
    for flag, first, second in ((1, mine, got), (0, got, mine)):

        @pl.when(flags[1] == flag)
        def _():
            out[0] = first[...]
            out[1] = second[...]


def last_kernel(flags, part_low, part_high, got, mid_low, mid_high, in_low, in_high, gain, out, sums):
    for flag, part, mid, rows in ((1, part_low, mid_low, in_low), (0, part_high, mid_high, in_high)):

        @pl.when(flags[4] == flag)
        def _():
            grad_norm = part[...].astype(FULL) + got[...].astype(FULL)
            normed, inverse = norm_rows(rows[...].astype(FULL))
            out[...] = (mid[...] + norm_back(grad_norm, normed, inverse, gain[...])).astype(LOW)
            sums[0:1, :] = 2.0 * jnp.sum(grad_norm * normed, axis=0, keepdims=True)
            sums[1:2, :] = 2.0 * jnp.sum(grad_norm, axis=0, keepdims=True)


def last_rows(flags, parts, got, mids, rows, gain):
    n, d = got.shape
    return call(
        last_kernel, (flags, *parts, got, *mids, *rows, gain), [shape(n, d), shape(2, d, dtype=FULL)], scalars=1,
        micros=1.0,
    )


def gather_kernel(one_0, one_lo, one_hi, two_lo_0, two_hi_0, two_lo_1, two_hi_1, down_lo, down_hi, up_lo_0, up_hi_0, up_lo_1, up_hi_1, rows, own):
    half = own.shape[1]
    both = one_lo[...] + one_hi[...]
    rows[0:2, :] = one_0[...]
    rows[2:4, :] = two_lo_0[...] + two_hi_0[...]
    rows[4:5, :] = both[2:3]
    rows[5:7, :] = both[0:2]
    rows[7:9, :] = two_lo_1[...] + two_hi_1[...]
    rows[9:10, :] = down_lo[...] + down_hi[...]
    for i, hidden in enumerate((up_lo_0[...] + up_hi_0[...], up_lo_1[...] + up_hi_1[...])):
        rows[10 + i : 11 + i, :] = hidden[:, half:]
        own[i : i + 1, :] = hidden[:, :half]


def chip_kernel(rows, own, got, out):
    out[0:10, :] = rows[0:10, :] + got[0:10, :]
    out[10:12, :] = own[...] + got[10:12, :]


def layers_kernel(flags, rows, got, mine, theirs):
    both = (rows[0:10, :] + got[0:10, :]) * 0.5
    for flag, first, second in ((1, mine, theirs), (0, theirs, mine)):

        @pl.when(flags[1] == flag)
        def _():
            first[...] = jnp.zeros_like(first)
            second[...] = jnp.zeros_like(second)
            first[0:5, :] = both[0:5]
            first[5:6, :] = rows[10:11, :]
            second[0:5, :] = both[5:10]
            second[5:6, :] = rows[11:12, :]


def fill(out, wholes, axis, first):
    if axis:
        out[...] = wholes[0][:, first : first + out.shape[1]]
        return
    at, last = 0, first + out.shape[0]
    for whole in wholes:
        low, high = max(first, at), min(last, at + whole.shape[0])
        if low < high:
            out[low - first : high - first, :] = whole[low - at : high - at, :]
        at += whole.shape[0]


def half_kernel(axis, flags, *refs):
    *wholes, out = refs
    for flag in (1, 0):

        @pl.when(flags[3] == flag)
        def _():
            fill(out, wholes, axis, 0 if flag else out.shape[axis])


def half_of(flags, wholes, axis, after=()):
    dims = [sum(w.shape[0] for w in wholes), wholes[0].shape[1]]
    dims[axis] //= 2
    return call(functools.partial(half_kernel, axis), (flags, *wholes), [shape(*dims)], scalars=1, after=after)[0]


def pick_kernel(layer, count, got_count, flags, *refs):
    wholes, gots, outs = refs[:count], refs[count : count + got_count], refs[count + got_count :]
    ways = [(flags[1] == 1 - layer, wholes), (flags[1] == layer, gots)]
    if got_count == 2:
        ways = [ways[0]] + [((flags[1] == layer) & (flags[3] == flag), gots[::step]) for flag, step in ((1, 1), (0, -1))]
    for wanted, sources in ways:

        @pl.when(wanted)
        def _():
            at = 0
            for out in outs:
                fill(out, sources, 0, at)
                at += out.shape[0]


def picked(flags, layer, wholes, gots, sizes, after=()):
    outs = [shape(size, wholes[0].shape[1]) for size in sizes]
    kernel = functools.partial(pick_kernel, layer, len(wholes), len(gots))
    return call(kernel, (flags, *wholes, *gots), outs, scalars=1, after=after)


def stack_kernel(*refs):
    *wholes, out = refs
    fill(out, wholes, 0, 0)


def stacked_rows(wholes, after):
    rows = sum(w.shape[0] for w in wholes)
    return call(stack_kernel, wholes, [shape(rows, wholes[0].shape[1])], after=after)[0]


def copy_kernel(source, out):
    out[...] = source[...]


def copied(source, after):
    return call(copy_kernel, (source,), [shape(*source.shape)], after=after)[0]


def micro_kernel(flags, both, out):
    for flag in (1, 0):

        @pl.when(flags[1] == flag)
        def _():
            out[...] = both[1 - flag]


def output_kernel(flags, mid_low, mid_high, part_low, part_high, got, bias, out):
    for flag, mid, part in ((1, mid_low, part_low), (0, mid_high, part_high)):

        @pl.when(flags[4] == flag)
        def _():
            out[...] = (mid[...] + (part[...].astype(FULL) + got[...].astype(FULL)) + bias[...]).astype(LOW)


def own_kernel(flags, if_low, if_high, out):
    for flag, rows in ((1, if_low), (0, if_high)):

        @pl.when(flags[4] == flag)
        def _():
            out[...] = rows[...]


def own_or(flags, if_low, if_high, after=()):
    return call(own_kernel, (flags, if_low, if_high), [shape(*if_low.shape)], scalars=1, after=after)[0]


def output_rows(flags, mids, parts, got, bias):
    return call(output_kernel, (flags, *mids, *parts, got, bias), [shape(*got.shape)], scalars=1)[0]


def body(
    inputs, cotangent, segments, ln1_gain, ln1_bias, w_query, w_key, w_value, w_out,
    ln2_gain, ln2_bias, w_up, b_up, w_down, b_down, *, n_batch,
):
    LATEST.clear()
    CHAINED[0] = False
    n, d = inputs.shape[1:]
    half = w_up.shape[2]
    section = lax.axis_index("section")
    tensor = lax.axis_index("tensor")
    batch = lax.axis_index("batch")
    on_first = section == 0
    early = tensor < 2
    outer = (tensor == 0) | (tensor == 3)
    middle = (batch == 1) | (batch == 2)
    even = batch % 2 == 0
    flags = jnp.stack([outer, on_first, middle, even, early]).astype(jnp.int32)
    paired = n_batch % 2 == 0
    beside = [(i, i ^ 1) for i in range(n_batch)]

    def across(value):
        return lax.ppermute(value, "section", SWAP)

    qkv_parts = (w_query[0].T, w_key[0].T, w_value[0].T)
    CHAINED[0] = True
    got_qkv = across(half_of(flags, qkv_parts, 0) if paired else stacked_rows(qkv_parts, ()))
    got_wo = across(copied(w_out[0], ()))
    small_own = jnp.concatenate([ln1_gain, ln1_bias, ln2_gain, ln2_bias, b_down, b_up], axis=0)
    small_other = across(small_own)
    got_feed = across(stacked_rows((w_up[0], w_down[0]), (small_other,)))
    own_in = call(micro_kernel, (flags, inputs), [shape(n, d)], scalars=1)[0]
    other_in = to_partner(own_in)
    own_cot = call(micro_kernel, (flags, cotangent), [shape(n, d)], scalars=1)[0]
    other_cot = to_partner(own_cot)
    CHAINED[0] = False
    gots_qkv = (got_qkv, lax.ppermute(got_qkv, "batch", beside)) if paired else jnp.split(got_qkv, 2)

    def low_high(own, other):
        return jnp.where(early, own, other), jnp.where(early, other, own)

    rows_in = low_high(own_in, other_in)
    grad_last = low_high(own_cot, other_cot)

    segment = jnp.where(on_first, segments[0, 0], segments[1, 0])
    low_at = jnp.where(outer, 0, 1)
    block_at = {"own_low": low_at, "sib_low": 1 - low_at, "own_high": 3 - low_at, "sib_high": 2 + low_at}

    def block_bias(query, key_blocks):
        span = jnp.arange(n)
        query_at = block_at[query] * n + span
        query_seg = lax.dynamic_slice_in_dim(segment, block_at[query] * n, n)
        rows = []
        for key in key_blocks:
            key_at = key * n + span
            key_seg = lax.dynamic_slice_in_dim(segment, key * n, n)
            kept = (key_at[:, None] <= query_at[None, :]) & (key_seg[:, None] == query_seg[None, :])
            rows.append(jnp.where(kept, 0.0, MASKED).astype(FULL))
        return jnp.concatenate(rows, axis=0)

    biases = (
        block_bias("own_low", [block_at["own_low"], block_at["sib_low"]]),
        block_bias(
            "own_high",
            [block_at["sib_low"], block_at["own_high"], jnp.where(outer, block_at["sib_high"], block_at["own_low"])],
        ),
    )

    def layer_rows(layer):
        small = jnp.where(section == layer, small_own, small_other)
        rows = [small[i : i + 1] for i in range(6)]
        return rows[:5] + [(rows[5], to_sibling(rows[5]))]

    small_0, small_1 = layer_rows(0), layer_rows(1)

    def weights(layer, wholes, gots, sizes, after):
        return [(own, to_sibling(own)) for own in picked(flags, layer, wholes, gots, sizes, after)]

    def qkv_weight(layer, after=()):
        return weights(layer, qkv_parts, gots_qkv, [3 * w_query.shape[2]], after)[0]

    def out_weight(layer, after=()):
        return weights(layer, (w_out[0],), (got_wo,), [w_out.shape[1]], after)[0]

    def feed_weights(layer, after=()):
        return weights(layer, (w_up[0], w_down[0]), (got_feed,), [d, half], after)

    def attend_low(projected, sib, wo):
        return attend(False, projected[2], (projected[3], sib[0]), biases[0], *wo, None)

    def attend_high(both, sib, wo):
        return attend(True, both[1][2], (sib[0], both[1][3], sib[1], both[0][3]), biases[1], *wo, flags)

    qkv_0 = qkv_weight(0, (got_wo,))
    wo_0 = out_weight(0)
    tied = (other_cot, small_0[5][1], small_1[5][1])
    proj_0, sib_0 = [], []
    for i in (0, 1):
        proj_0.append(project((rows_in[i],), small_0[0], small_0[1], qkv_0, True, tied))
        sib_0.append(to_sibling(proj_0[i][4]))
    att_0 = [attend_low(proj_0[0], sib_0, wo_0)]
    got = [to_partner(att_0[0][2])]
    att_0.append(attend_high(proj_0, sib_0, wo_0))
    got.append(to_partner(att_0[1][2]))
    up_0, down_0 = feed_weights(0, got)
    feed_0, feed_got, after = [], [], ()
    for i in (0, 1):
        feed_0.append(
            feed(proj_0[i][0], att_0[i][2], got[i], small_0[2], small_0[3], up_0, small_0[5], down_0, after=after)
        )
        feed_got.append(to_partner(feed_0[i][4]))
        if i == 0:
            qkv_1 = qkv_weight(1, (feed_0[0][4],))
            wo_1 = out_weight(1, (feed_0[0][4],))
            after = (qkv_1[0], wo_1[0])

    proj_1, sib_1, att_1, got, after = [], [], [], [], ()
    for i in (0, 1):
        source = (feed_0[i][0], feed_0[i][4], feed_got[i], small_0[4])
        proj_1.append(project(source, small_1[0], small_1[1], qkv_1, False, after))
        sib_1.append(to_sibling(proj_1[i][4]))
        if i == 0:
            up_1, down_1 = feed_weights(1, (proj_1[0][2],))
            after = (up_1[0], down_1[0])
            att_1.append(attend_low(proj_1[0], sib_1, wo_1))
        else:
            att_1.append(attend_high(proj_1, sib_1, wo_1))
        got.append(to_partner(att_1[i][2]))
    feed_1, back_got = [], []
    for i in (0, 1):
        feed_1.append(
            feed(proj_1[i][0], att_1[i][2], got[i], small_1[2], small_1[3], up_1, small_1[5], down_1, grad_last[i])
        )
        back_got.append(to_partner(feed_1[i][4]))

    def grads_feed(g, grads, a_two, dz):
        plan = (
            ((4, 5), 0, d, (6, 7), 0, half, 0, 0),
            ((4, 5), 0, d, (6, 7), half, half, 1, 0),
            ((0, 1), 0, half, (2, 3), 0, d, 0, d),
            ((0, 1), half, half, (2, 3), 0, d, 1, d),
        )
        return outer_products((*g, *grads, *a_two, *dz), plan, d + half, d)

    def grads_attend(o, lows, a_one, d_own, d_sib):
        w, w3 = o[0].shape[1] // 2, d_own[0].shape[1]
        plan = (
            ((6, 7), 0, w3, (4, 5), 0, d, 0, 0),
            ((8, 9), 0, w3, (4, 5), 0, d, 1, 0),
            ((0, 1), 0, w, (2, 3), 0, d, 0, w3),
            ((0, 1), w, w, (2, 3), 0, d, 1, w3),
        )
        return outer_products((*o, *lows, *a_one, *d_own, *d_sib), plan, w3 + w, d)

    mids = [f[0] for f in feed_1]
    by_feed_1 = grads_feed([f[2] for f in feed_1], grad_last, [f[1] for f in feed_1], [f[3] for f in feed_1])
    feed_1_got = to_sibling(by_feed_1[1])
    out_parts = down([f[2] for f in feed_1], down_1)
    def attend_backward(i, mids, parts, grads, gain, wo, projected, sib, att, earlier, long=False):
        return attend_back(
            bool(i), flags, mids[i], parts[i], back_got[i], grads[i], gain, wo, projected[i][2],
            [p[3] for p in projected], sib, biases[i], att[i][1], earlier, long,
        )

    ab_1 = []
    for i in (0, 1):
        earlier = ab_1[0][4:6] if i else ()
        ab_1.append(
            attend_backward(i, mids, [f[4] for f in feed_1], grad_last, small_1[2], wo_1, proj_1, sib_1, att_1, earlier)
        )
    mid_grads_1, lows_1, dq = [[a[k] for a in ab_1] for k in (0, 1, 3)]
    keep, send = ab_1[1][4:6], ab_1[1][6:8]
    kv_got = [to_sibling(x) for x in send]
    back_1, part_got = [], []
    for i in (0, 1):
        back_1.append(project_back(dq[i], keep[i], kv_got[i], qkv_1))
        part_got.append(to_partner(back_1[i][2]))
    by_att_1 = grads_attend(
        [a[0] for a in att_1], lows_1, [p[1] for p in proj_1], [b[0] for b in back_1], [b[1] for b in back_1]
    )
    att_1_got = to_sibling(by_att_1[1])

    fb_0, back_got, after = [], [], by_att_1
    for i in (0, 1):
        fb_0.append(
            feed_back(
                mid_grads_1[i], back_1[i][2], part_got[i], proj_1[i][0], small_1[0], feed_0[i][3], up_0, down_0, after
            )
        )
        after = ()
        back_got.append(to_partner(fb_0[i][3]))
    grad_mid = [f[0] for f in fb_0]
    by_feed_0 = grads_feed([f[2] for f in feed_0], grad_mid, [f[1] for f in feed_0], [f[2] for f in fb_0])
    feed_0_got = to_sibling(by_feed_0[1])

    CHAINED[0] = True
    along = [[(0, 1), (3, 2)], [(1, 2), (2, 1)], [(1, 0), (2, 3)]]
    feed_pieces = ready_pieces(
        flags, (by_feed_0[0], feed_0_got), (by_feed_1[0], feed_1_got), [(d + half) // 3] * 3
    )
    stage, hops = {}, {}

    def begin(k, piece):
        stage[k], hops[k] = (piece[0], across(piece[1])), 0

    def advance(*ks, after=(), extra=4):
        if n_batch != 4:
            ks = [k for k in ks if hops[k] == 0]
        if not ks:
            return
        values = call(
            functools.partial(sums_kernel, tuple(k == extra for k in ks)), [x for k in ks for x in stage[k]], [shape(*stage[k][0].shape) for k in ks],
            after=[stage[k][1] for k in after], micros=0.5 * len(ks),
        )
        for k, value in zip(ks, values):
            stage[k] = (value, lax.ppermute(value, "batch", along[hops[k]]) if n_batch == 4 else value)
            hops[k] += 1

    def settled(ks, sizes, extra=False):
        if n_batch == 4:
            return chosen(flags, [stage[k] for k in ks], sizes, 2, extra)
        return chosen(flags, [(lax.psum(stage[k][0], "batch"), stage[k][0]) for k in ks], sizes, None, extra)

    begin(0, feed_pieces[0])
    begin(1, feed_pieces[1])
    begin(2, feed_pieces[2])
    parts_0 = [f[3] for f in fb_0]
    mids_0 = [f[0] for f in feed_0]
    ab_0 = []
    for i in (0, 1):
        earlier = ab_0[0][4:6] if i else ()
        ab_0.append(
            attend_backward(i, mids_0, parts_0, grad_mid, small_0[2], wo_0, proj_0, sib_0, att_0, earlier, True)
        )
    mid_grads_0, lows_0, dq = [[a[k] for a in ab_0] for k in (0, 1, 3)]
    keep, send = ab_0[1][4:6], ab_0[1][6:8]
    advance(0)
    kv_got = [to_sibling(x) for x in send]
    back_0 = [project_back(dq[i], keep[i], kv_got[i], qkv_0) for i in (0, 1)]
    part_got = to_partner(own_or(flags, back_0[1][2], back_0[0][2]))
    by_att_0 = grads_attend(
        [a[0] for a in att_0], lows_0, [p[1] for p in proj_0], [b[0] for b in back_0], [b[1] for b in back_0]
    )
    att_0_got = to_sibling(by_att_0[1])
    att_rows = by_att_0[0].shape[0]
    att_sides = (by_att_0[0], att_0_got), (by_att_1[0], att_1_got)

    last, one_0 = last_rows(flags, [b[2] for b in back_0], part_got, mid_grads_0, rows_in, small_0[0])
    operands = (
        one_0, fb_0[0][1], fb_0[1][1], ab_0[0][2], ab_0[1][2], ab_1[0][2], ab_1[1][2], feed_1[0][6], feed_1[1][6], fb_0[0][4], fb_0[1][4],
        feed_1[0][5], feed_1[1][5],
    )
    rows, own = call(gather_kernel, operands, [shape(12, d, dtype=FULL), shape(2, half, dtype=FULL)])
    rows = call(chip_kernel, (rows, own, to_sibling(rows)), [shape(12, d, dtype=FULL)])[0]
    advance(0, 1)
    small = call(layers_kernel, (flags, rows, to_partner(rows)), [shape(EXTRA // 2, d, dtype=FULL)] * 2, scalars=1)
    att_pieces = ready_pieces(flags, *att_sides, [att_rows // 2] * 2, small=small)
    begin(3, att_pieces[0])
    begin(4, att_pieces[1])
    advance(2, 1, 0)

    def micro_sent(first, second):
        mine = jnp.where(on_first, first, second)
        return mine, across(jnp.where(on_first, second, first))

    def micro_out(mine, got):
        return call(micro_out_kernel, (flags, mine, got), [shape(2, n, d)], scalars=1)[0][None]

    advance(3, 2, 1)
    backward = micro_sent(last, jnp.where(early, *grad_mid))
    out_got = to_partner(own_or(flags, out_parts[1], out_parts[0]))
    advance(4, 3, 2, after=(0,))
    out_1 = output_rows(flags, mids, out_parts, out_got, small_1[4])
    forward = micro_sent(jnp.where(early, *[p[0] for p in proj_1]), out_1)
    advance(4, 3, after=(1,))
    advance(4, after=(2,))
    up_total, down_total = settled((0, 1, 2), [d, half])
    query_total, key_total = settled((3,), [att_rows // 4] * 2)
    backward_out = micro_out(*backward)
    forward_out = micro_out(*forward)
    value_total, out_total, sums = settled((4,), [att_rows // 4] * 2, True)
    att_totals = [query_total, key_total, value_total, out_total]
    return (
        forward_out,
        backward_out,
        sums[0:1],
        sums[1:2],
        *[x.T[None] for x in att_totals[:3]],
        att_totals[3][None],
        sums[2:3],
        sums[3:4],
        up_total[None],
        sums[5:6],
        down_total[None],
        sums[4:5],
    )


def solution(mesh):
    rows = P(None, ("batch", "tensor"), None)
    layer = P("section", None)
    by_column = P("section", None, "tensor")
    by_row = P("section", "tensor", None)
    kept = P("section", None, ("batch", "tensor"), None)
    return jax.shard_map(
        functools.partial(body, n_batch=mesh.shape["batch"]),
        mesh=mesh,
        in_specs=(
            rows, rows, P(None, "batch", None), layer, layer, by_column, by_column, by_column, by_row,
            layer, layer, by_column, P("section", "tensor"), by_row, layer,
        ),
        out_specs=(
            kept, kept, layer, layer, by_column, by_column, by_column, by_row,
            layer, layer, by_column, P("section", "tensor"), by_row, layer,
        ),
        check_vma=False,
    )
```

```python
import functools

import jax
import jax.numpy as jnp
from jax import lax
from jax.experimental import pallas as pl
from jax.experimental.pallas import tpu as pltpu
from jax.sharding import PartitionSpec as P

HEAD_DIM = 64
EPSILON = 1e-05
LOW = jnp.bfloat16
FULL = jnp.float32
SCALING = HEAD_DIM**-0.5
EXTRA = 32
MASKED = -1e30
VMEM_BYTES = 16 * 1024 * 1024

SIBLING = [(0, 1), (1, 0), (2, 3), (3, 2)]
PARTNER = [(0, 3), (3, 0), (1, 2), (2, 1)]
SWAP = [(0, 1), (1, 0)]


def dot(left, right):
    return jnp.dot(left, right, preferred_element_type=FULL)


def dot_rows(left, right):
    return lax.dot_general(left, right, (((0,), (0,)), ((), ())), preferred_element_type=FULL)


def dot_back(left, right):
    return lax.dot_general(left, right, (((1,), (1,)), ((), ())), preferred_element_type=FULL)


def norm_rows(values):
    center = values - jnp.mean(values, axis=-1, keepdims=True)
    inverse = lax.rsqrt(jnp.mean(center * center, axis=-1, keepdims=True) + EPSILON)
    return center * inverse, inverse


def norm_back(grad_norm, normed, inverse, gain):
    scaled = grad_norm * gain
    mean_one = jnp.mean(scaled, axis=-1, keepdims=True)
    mean_two = jnp.mean(scaled * normed, axis=-1, keepdims=True)
    return inverse * (scaled - mean_one - normed * mean_two)


def to_partner(value):
    return lax.ppermute(value, "tensor", PARTNER)


def to_sibling(value):
    return lax.ppermute(value, "tensor", SIBLING)


LATEST = []
CHAINED = [False]
PACE = 6e7


def call(kernel, operands, outs, scalars=0, scratch=(), after=(), micros=0.6):
    after = (*LATEST, *after) if CHAINED[0] else tuple(after)
    count, waited = len(operands), len(after)
    specs = [pl.BlockSpec(memory_space=pltpu.SMEM)] * scalars
    specs += [pl.BlockSpec(memory_space=pltpu.VMEM)] * (count - scalars)
    specs += [pl.BlockSpec(memory_space=pl.ANY)] * waited
    got = pl.pallas_call(
        lambda *refs: kernel(*refs[:count], *refs[count + waited :]),
        out_shape=tuple(outs),
        in_specs=specs,
        out_specs=tuple(pl.BlockSpec(memory_space=pltpu.VMEM) for _ in outs),
        scratch_shapes=list(scratch),
        compiler_params=pltpu.CompilerParams(vmem_limit_bytes=VMEM_BYTES),
        cost_estimate=pl.CostEstimate(flops=int(micros * PACE), bytes_accessed=1024, transcendentals=0),
    )(*operands, *after)
    LATEST[:] = [min(got, key=lambda array: array.size)]
    return got


def shape(*dims, dtype=LOW):
    return jax.ShapeDtypeStruct(dims, dtype)


def halves(pieces):
    middle = len(pieces) // 2
    return pieces[:middle], pieces[middle:]


def stacked(pieces, axis=0):
    return jnp.concatenate([p[...] for p in pieces], axis=axis) if len(pieces) > 1 else pieces[0][...]


def project_kernel(first, *refs):
    if first:
        rows_ref, gain, bias, *ws, a_ref, q_ref, kv_ref, send_ref = refs
        layer_in = rows_ref[...].astype(FULL)
    else:
        mid, part, got, b_down, gain, bias, *ws, in_ref, a_ref, q_ref, kv_ref, send_ref = refs
        low = (mid[...] + (part[...].astype(FULL) + got[...].astype(FULL)) + b_down[...]).astype(LOW)
        in_ref[...] = low
        layer_in = low.astype(FULL)
    normed, _ = norm_rows(layer_in)
    a_one = (normed * gain[...] + bias[...]).astype(LOW)
    a_ref[...] = a_one
    own, sib = [dot_back(a_one, stacked(w)).astype(LOW) for w in halves(ws)]
    w = own.shape[1] // 3
    q_own, k_own, v_own = own[:, :w], own[:, w : 2 * w], own[:, 2 * w :]
    q_sib, k_sib, v_sib = sib[:, :w], sib[:, w : 2 * w], sib[:, 2 * w :]
    q_ref[...] = jnp.concatenate([q_own, q_sib], axis=1) * jnp.asarray(SCALING, LOW)
    kv_ref[...] = jnp.concatenate([k_own, k_sib, v_own, v_sib], axis=1)
    send_ref[...] = jnp.concatenate([k_sib, k_own, v_sib, v_own], axis=1)


def project(source, gain, bias, weights, first, after=()):
    n, d = source[0].shape
    h = sum(w.shape[0] for w in weights) // 3
    outs = [shape(n, d), shape(n, h), shape(n, 2 * h), shape(n, 2 * h)]
    if not first:
        outs = [shape(n, d)] + outs
    got = call(
        functools.partial(project_kernel, first),
        (*source, gain, bias, *weights),
        outs,
        after=after,
        micros=1.1,
    )
    return got if not first else (source[0], *got)


def pair_masks(q_pair):
    lane = lax.broadcasted_iota(jnp.int32, q_pair.shape, 1)
    zero = jnp.zeros_like(q_pair)
    return jnp.where(lane < HEAD_DIM, q_pair, zero), jnp.where(lane < HEAD_DIM, zero, q_pair)


def attend_kernel(late, *refs):
    if late:
        outer, q_ref, sib_low, own_high, sib_high, own_low, bias_ref, wo_own, wo_sib, o_ref, lse_ref, part_ref, extra = refs

        @pl.when(outer[0] == 1)
        def _():
            extra[...] = sib_high[...]

        @pl.when(outer[0] == 0)
        def _():
            extra[...] = own_low[...]

        kv = jnp.concatenate([sib_low[...], own_high[...], extra[...]], axis=0)
    else:
        q_ref, own_low, sib_low, bias_ref, wo_own, wo_sib, o_ref, lse_ref, part_ref = refs
        kv = jnp.concatenate([own_low[...], sib_low[...]], axis=0)
    h = kv.shape[1] // 2
    keys, values = kv[:, :h], kv[:, h:]
    values_t = values.T
    outs, sums = [], []
    for pair in range(h // 128):
        lanes = slice(pair * 128, pair * 128 + 128)
        for j, q in enumerate(pair_masks(q_ref[:, lanes])):
            head = 2 * pair + j
            scores = dot_back(keys[:, lanes], q) + bias_ref[...]
            highest = jnp.max(scores, axis=0, keepdims=True)
            e = jnp.exp(scores - highest)
            total = jnp.sum(e, axis=0, keepdims=True)
            mixed = dot(values_t[head * HEAD_DIM : (head + 1) * HEAD_DIM], e.astype(LOW))
            outs.append(mixed * (1.0 / total))
            sums.append(highest + jnp.log(total))
    o = jnp.concatenate(outs, axis=0).T.astype(LOW)
    o_ref[...] = o
    lse_ref[...] = jnp.concatenate(sums + sums[: 8 - len(sums)], axis=0)
    half = wo_own.shape[0]
    part_ref[...] = (dot(o[:, :half], wo_own[...]) + dot(o[:, half:], wo_sib[...])).astype(LOW)


def attend(late, q, blocks, bias, wo_own, wo_sib, outer, after=()):
    n, h = q.shape
    d = wo_own.shape[1]
    operands = ((outer,) if late else ()) + (q, *blocks, bias, wo_own, wo_sib)
    return call(
        functools.partial(attend_kernel, late),
        operands,
        [shape(n, h), shape(8, n, dtype=FULL), shape(n, d)],
        scalars=1 if late else 0,
        scratch=[pltpu.VMEM((n, 2 * h), LOW)] if late else (),
        after=after,
        micros=4.5 if late else 3.2,
    )


def gelu_parts(z):
    c = 0.7978845608028654
    square = z * z
    t = jnp.tanh(c * (z + 0.044715 * (square * z)))
    half = 0.5 * (1.0 + t)
    return z * half, half + 0.5 * z * (1.0 - t * t) * (c + (3.0 * 0.044715 * c) * square)


def feed_kernel(last, ups, dns, *refs):
    refs = (*refs[:7], refs[7 : 7 + ups], refs[7 + ups : 7 + ups + dns], *refs[7 + ups + dns :])
    if last:
        (u, part, got, gain, bias, b_own, b_sib, ups, dns, grad_ref,
         mid_ref, a_ref, g_ref, dz_ref, back_ref, hidden_sum, row_sum) = refs
    else:
        (u, part, got, gain, bias, b_own, b_sib, ups, dns,
         mid_ref, a_ref, g_ref, slope_ref, out_ref) = refs
    mid = u[...].astype(FULL) + (part[...].astype(FULL) + got[...].astype(FULL))
    mid_ref[...] = mid
    normed, _ = norm_rows(mid)
    a_two = (normed * gain[...] + bias[...]).astype(LOW)
    a_ref[...] = a_two
    f = b_own.shape[1]
    step = 256
    total = jnp.zeros(mid.shape, FULL)
    for side, (up, b, dn) in enumerate(zip(halves(ups), (b_own, b_sib), halves(dns))):
        up, dn = stacked(up, axis=1), stacked(dn)
        for at in range(0, f, step):
            cols = slice(at, at + step)
            here = slice(side * f + at, side * f + at + step)
            z = dot(a_two, up[:, cols]) + b[:, cols]
            g, slope = gelu_parts(z)
            g = g.astype(LOW)
            g_ref[:, here] = g
            if last:
                dz = (dot_back(grad_ref[...], dn[cols, :]) * slope).astype(LOW)
                dz_ref[:, here] = dz
                hidden_sum[:, here] = jnp.sum(dz.astype(FULL), axis=0, keepdims=True)
                total = total + dot_back(dz, up[:, cols])
            else:
                slope_ref[:, here] = slope.astype(LOW)
                total = total + dot(g, dn[cols, :])
    if last:
        back_ref[...] = total.astype(LOW)
        row_sum[...] = jnp.sum(grad_ref[...].astype(FULL), axis=0, keepdims=True)
    else:
        out_ref[...] = total.astype(LOW)


def feed(u, part, got, gain, bias, up, b_up, dn, grad=None, after=()):
    n, d = u.shape
    f = b_up[0].shape[1]
    last = grad is not None
    outs = [shape(n, d, dtype=FULL), shape(n, d), shape(n, 2 * f), shape(n, 2 * f), shape(n, d)]
    operands = (u, part, got, gain, bias, *b_up, *up, *dn) + ((grad,) if last else ())
    if last:
        outs += [shape(1, 2 * f, dtype=FULL), shape(1, d, dtype=FULL)]
    return call(functools.partial(feed_kernel, last, len(up), len(dn)), operands, outs, after=after, micros=3.2)


def feed_back_kernel(ups, dns, mid_grad, part, got, in_ref, gain, slope, *refs):
    grad_ref, sums_ref, dz_ref, back_ref, hidden_sum = refs[ups + dns :]
    ups, dns = refs[:ups], refs[ups : ups + dns]
    grad_norm = part[...].astype(FULL) + got[...].astype(FULL)
    normed, inverse = norm_rows(in_ref[...].astype(FULL))
    grad = (mid_grad[...] + norm_back(grad_norm, normed, inverse, gain[...])).astype(LOW)
    grad_ref[...] = grad
    sums_ref[...] = jnp.concatenate(
        [
            jnp.sum(grad_norm * normed, axis=0, keepdims=True),
            jnp.sum(grad_norm, axis=0, keepdims=True),
            jnp.sum(grad.astype(FULL), axis=0, keepdims=True),
        ],
        axis=0,
    )
    f = slope.shape[1] // 2
    step = 256
    total = jnp.zeros(grad.shape, FULL)
    for side, (up, dn) in enumerate(zip(halves(ups), halves(dns))):
        up, dn = stacked(up, axis=1), stacked(dn)
        for at in range(0, f, step):
            cols = slice(at, at + step)
            here = slice(side * f + at, side * f + at + step)
            dz = (dot_back(grad, dn[cols, :]) * slope[:, here].astype(FULL)).astype(LOW)
            dz_ref[:, here] = dz
            hidden_sum[:, here] = jnp.sum(dz.astype(FULL), axis=0, keepdims=True)
            total = total + dot_back(dz, up[:, cols])
    back_ref[...] = total.astype(LOW)


def feed_back(mid_grad, part, got, layer_in, gain, slope, up, dn, after=()):
    n, d = mid_grad.shape
    f = slope.shape[1] // 2
    outs = [shape(n, d), shape(3, d, dtype=FULL), shape(n, 2 * f), shape(n, d), shape(1, 2 * f, dtype=FULL)]
    return call(
        functools.partial(feed_back_kernel, len(up), len(dn)), (mid_grad, part, got, layer_in, gain, slope, *up, *dn), outs, after=after, micros=2.9
    )


def attend_back_kernel(late, *refs):
    if late:
        (flags, mid, part, got, grad, gain, wo_own, wo_sib, q_ref, bias, lse, own_low, own_high, sib_low, sib_high,
         low_kept, low_sent, mid_ref, low_ref, sums_ref, dq_ref, keep_low, keep_high, send_low, send_high,
         extra, acc_low, acc_high) = refs
        outside = flags[0].astype(FULL)

        @pl.when(flags[0] == 1)
        def _():
            extra[...] = sib_high[...]

        @pl.when(flags[0] == 0)
        def _():
            extra[...] = own_low[...]

        blocks = (sib_low, own_high, extra)
    else:
        (mid, part, got, grad, gain, wo_own, wo_sib, q_ref, bias, lse, own_low, sib_low,
         mid_ref, low_ref, sums_ref, dq_ref, keep_low, acc_low) = refs
        blocks = (own_low, sib_low)
    n = mid.shape[0]
    grad_norm = part[...].astype(FULL) + got[...].astype(FULL)
    normed, inverse = norm_rows(mid[...])
    mid_grad = grad[...].astype(FULL) + norm_back(grad_norm, normed, inverse, gain[...])
    mid_ref[...] = mid_grad
    low = mid_grad.astype(LOW)
    low_ref[...] = low
    sums_ref[0:1, :] = jnp.sum(grad_norm * normed, axis=0, keepdims=True)
    sums_ref[1:2, :] = jnp.sum(grad_norm, axis=0, keepdims=True)
    do = jnp.concatenate([dot_back(low, wo_own[...]), dot_back(low, wo_sib[...])], axis=1).astype(LOW)
    kv = jnp.concatenate([b[...] for b in blocks], axis=0)
    h = kv.shape[1] // 2
    keys, values = kv[:, :h], kv[:, h:]
    keys_t = keys.T
    dq = []
    for pair in range(h // 128):
        lanes = slice(pair * 128, pair * 128 + 128)
        dk = dv = None
        qs_two, do_two = pair_masks(q_ref[:, lanes]), pair_masks(do[:, lanes])
        for j in (0, 1):
            head = 2 * pair + j
            scores = dot_back(keys[:, lanes], qs_two[j]) + bias[...]
            p = jnp.exp(scores - lse[head : head + 1, :])
            dp = dot_back(values[:, lanes], do_two[j])
            inner = jnp.sum(p * dp, axis=0, keepdims=True)
            ds = (p * (dp - inner)).astype(LOW)
            dv_now = dot(p.astype(LOW), do_two[j])
            dk_now = dot(ds, qs_two[j])
            dk = dk_now if dk is None else dk + dk_now
            dv = dv_now if dv is None else dv + dv_now
            dq.append(dot(keys_t[head * HEAD_DIM : (head + 1) * HEAD_DIM], ds) * SCALING)
        for value, where in ((dk, lanes), (dv, slice(h + pair * 128, h + pair * 128 + 128))):
            if late:
                acc_low[:, where] = low_sent[:, where] + value[:n]
                keep_high[:, where] = value[n : 2 * n]
                keep_low[:, where] = low_kept[:, where] + value[2 * n :] * (1.0 - outside)
                acc_high[:, where] = value[2 * n :] * outside
            else:
                keep_low[:, where] = value[:n]
                acc_low[:, where] = value[n:]
    dq_ref[...] = jnp.concatenate(dq, axis=0).T.astype(LOW)
    if late:
        for acc, out in ((acc_low, send_low), (acc_high, send_high)):
            send = acc[...].astype(LOW)
            w = send.shape[1] // 4
            out[...] = jnp.concatenate(
                [send[:, w : 2 * w], send[:, :w], send[:, 3 * w :], send[:, 2 * w : 3 * w]], axis=1
            )


def attend_back(late, flags, mid, part, got, grad, gain, wo, q, own, sib, bias, lse, earlier, long):
    n, d = mid.shape
    h = q.shape[1]
    outs = [shape(n, d, dtype=FULL), shape(n, d), shape(2, d, dtype=FULL), shape(n, h)]
    outs += [shape(n, 2 * h, dtype=FULL)] * 2
    common = (mid, part, got, grad, gain, *wo, q, bias, lse)
    if late:
        outs += [shape(n, 2 * h)] * 2
        operands = (flags, *common, *own, *sib, *earlier)
    else:
        operands = (*common, own[0], sib[0])
    return call(
        functools.partial(attend_back_kernel, late),
        operands,
        outs,
        scalars=int(late),
        scratch=[pltpu.VMEM((n, 2 * h), LOW)] + [pltpu.VMEM((n, 2 * h), FULL)] * 2 if late else (),
        micros=300.0 if long else 5.5 if late else 4.0,
    )


def project_back_kernel(dq, keep, got, *refs):
    *ws, own_ref, sib_ref, part_ref = refs
    dkv = (keep[...] + got[...].astype(FULL)).astype(LOW)
    w = dkv.shape[1] // 4
    own = jnp.concatenate([dq[:, :w], dkv[:, :w], dkv[:, 2 * w : 3 * w]], axis=1)
    sib = jnp.concatenate([dq[:, w:], dkv[:, w : 2 * w], dkv[:, 3 * w :]], axis=1)
    own_ref[...] = own
    sib_ref[...] = sib
    w_own, w_sib = [stacked(x) for x in halves(ws)]
    part_ref[...] = (dot(own, w_own) + dot(sib, w_sib)).astype(LOW)


def project_back(dq, keep, got, weights):
    n = dq.shape[0]
    w, d = sum(x.shape[0] for x in weights) // 2, weights[0].shape[1]
    outs = [shape(n, w), shape(n, w), shape(n, d)]
    return call(project_back_kernel, (dq, keep, got, *weights), outs, micros=0.9)


def outer_kernel(plan, *refs):
    outs = refs[-2:]
    for lefts, first, count, rights, at, width, which, base in plan:
        right = jnp.concatenate([refs[i][:, at : at + width] for i in rights], axis=0)
        for row in range(0, count, 256):
            size = min(256, count - row)
            cols = slice(first + row, first + row + size)
            left = jnp.concatenate([refs[i][:, cols] for i in lefts], axis=0)
            outs[which][base + row : base + row + size, :] = dot_rows(left, right).astype(LOW)


def outer_products(operands, plan, rows, width, after=()):
    return call(functools.partial(outer_kernel, plan), operands, [shape(rows, width)] * 2, after=after, micros=2.5)


def down_kernel(count, *refs):
    gs, dns, outs = refs[:2], refs[2 : 2 + count], refs[2 + count :]
    dn = stacked(dns)
    for g, out in zip(gs, outs):
        out[...] = dot(g[...], dn).astype(LOW)


def down(gs, dns, after=()):
    n, d = gs[0].shape[0], dns[0].shape[1]
    return call(functools.partial(down_kernel, len(dns)), (*gs, *dns), [shape(n, d)] * 2, after=after, micros=1.4)


def ready_kernel(cuts, extra, flags, first_own, first_got, second_own, second_got, *refs):
    small, outs = refs[:extra], refs[extra:]
    for i, (at, size) in enumerate(cuts):
        rows = slice(at, at + size)
        first = (first_own[rows, :].astype(FULL) + first_got[rows, :].astype(FULL)).astype(LOW)
        second = (second_own[rows, :].astype(FULL) + second_got[rows, :].astype(FULL)).astype(LOW)
        mine, theirs = outs[2 * i], outs[2 * i + 1]

        @pl.when(flags[1] == 1)
        def _():
            mine[:size, :] = first
            theirs[:size, :] = second

        @pl.when(flags[1] == 0)
        def _():
            mine[:size, :] = second
            theirs[:size, :] = first

    for values, out in zip(small, outs[-2:]):
        split_rows(values[...], out)


def split_rows(values, out):
    first = out.shape[0] - EXTRA
    rounded = values.astype(LOW)
    out[first : first + EXTRA // 2, :] = rounded
    out[first + EXTRA // 2 :, :] = (values - rounded.astype(FULL)).astype(LOW)


def joined_rows(ref):
    first = ref.shape[0] - EXTRA
    return ref[first : first + EXTRA // 2, :].astype(FULL) + ref[first + EXTRA // 2 :, :].astype(FULL)


def ready_pieces(flags, first, second, sizes, at=0, small=()):
    cuts = []
    for size in sizes:
        cuts.append((at, size))
        at += size
    width = first[0].shape[1]
    outs = [shape(size, width) for size in sizes for _ in (0, 1)]
    if small:
        outs[-2:] = [shape(sizes[-1] + EXTRA, width)] * 2
    got = call(
        functools.partial(ready_kernel, tuple(cuts), len(small)), (flags, *first, *second, *small), outs, scalars=1
    )
    return [(got[2 * i], got[2 * i + 1]) for i in range(len(sizes))]


def sums_kernel(extra, *refs):
    count = len(refs) // 3
    for i in range(count):
        left, right, out = refs[2 * i], refs[2 * i + 1], refs[2 * count + i]
        if not extra[i]:
            out[...] = (left[...].astype(FULL) + right[...].astype(FULL)).astype(LOW)
        else:
            bulk = slice(0, out.shape[0] - EXTRA)
            out[bulk, :] = (left[bulk, :].astype(FULL) + right[bulk, :].astype(FULL)).astype(LOW)
            split_rows(joined_rows(left) + joined_rows(right), out)


def added(left, right, after=()):
    return call(added_kernel, (left, right), [shape(*left.shape, dtype=left.dtype)], after=after)[0]


def chosen_kernel(count, which, extra, flags, *refs):
    sums, gots, outs = refs[:count], refs[count : 2 * count], refs[2 * count :]
    outs, small = outs[: len(outs) - extra], outs[len(outs) - extra :]
    for flag, pieces in ((1, sums), (0, gots)):

        @pl.when(flags[which] == flag)
        def _():
            first = 0
            for out in outs:
                at, last = 0, first + out.shape[0]
                for piece in pieces:
                    low, high = max(first, at), min(last, at + piece.shape[0])
                    if low < high:
                        out[low - first : high - first, :] = piece[low - at : high - at, :].astype(FULL)
                    at += piece.shape[0]
                first = last
            for out in small:
                out[...] = joined_rows(pieces[-1])


def chosen(flags, stages, sizes, which, extra=False):
    if which is None:
        flags, which = jnp.ones_like(flags), 0
    operands = (flags, *[low for low, _ in stages], *[got for _, got in stages])
    outs = [shape(size, stages[0][0].shape[1], dtype=FULL) for size in (*sizes, EXTRA // 2)[: len(sizes) + extra]]
    return call(functools.partial(chosen_kernel, len(stages), which, int(extra)), operands, outs, scalars=1)


def micro_out_kernel(flags, mine, got, out):
    for flag, first, second in ((1, mine, got), (0, got, mine)):

        @pl.when(flags[1] == flag)
        def _():
            out[0] = first[...]
            out[1] = second[...]


def last_kernel(flags, part_low, part_high, got, mid_low, mid_high, in_low, in_high, gain, out, sums):
    for flag, part, mid, rows in ((1, part_low, mid_low, in_low), (0, part_high, mid_high, in_high)):

        @pl.when(flags[4] == flag)
        def _():
            grad_norm = part[...].astype(FULL) + got[...].astype(FULL)
            normed, inverse = norm_rows(rows[...].astype(FULL))
            out[...] = (mid[...] + norm_back(grad_norm, normed, inverse, gain[...])).astype(LOW)
            sums[0:1, :] = 2.0 * jnp.sum(grad_norm * normed, axis=0, keepdims=True)
            sums[1:2, :] = 2.0 * jnp.sum(grad_norm, axis=0, keepdims=True)


def last_rows(flags, parts, got, mids, rows, gain):
    n, d = got.shape
    return call(
        last_kernel, (flags, *parts, got, *mids, *rows, gain), [shape(n, d), shape(2, d, dtype=FULL)], scalars=1,
        micros=1.0,
    )


def gather_kernel(one_0, one_lo, one_hi, two_lo_0, two_hi_0, two_lo_1, two_hi_1, down_lo, down_hi, up_lo_0, up_hi_0, up_lo_1, up_hi_1, rows, own):
    half = own.shape[1]
    both = one_lo[...] + one_hi[...]
    rows[0:2, :] = one_0[...]
    rows[2:4, :] = two_lo_0[...] + two_hi_0[...]
    rows[4:5, :] = both[2:3]
    rows[5:7, :] = both[0:2]
    rows[7:9, :] = two_lo_1[...] + two_hi_1[...]
    rows[9:10, :] = down_lo[...] + down_hi[...]
    for i, hidden in enumerate((up_lo_0[...] + up_hi_0[...], up_lo_1[...] + up_hi_1[...])):
        rows[10 + i : 11 + i, :] = hidden[:, half:]
        own[i : i + 1, :] = hidden[:, :half]


def chip_kernel(rows, own, got, out):
    out[0:10, :] = rows[0:10, :] + got[0:10, :]
    out[10:12, :] = own[...] + got[10:12, :]


def layers_kernel(flags, rows, got, mine, theirs):
    both = (rows[0:10, :] + got[0:10, :]) * 0.5
    for flag, first, second in ((1, mine, theirs), (0, theirs, mine)):

        @pl.when(flags[1] == flag)
        def _():
            first[...] = jnp.zeros_like(first)
            second[...] = jnp.zeros_like(second)
            first[0:5, :] = both[0:5]
            first[5:6, :] = rows[10:11, :]
            second[0:5, :] = both[5:10]
            second[5:6, :] = rows[11:12, :]


def fill(out, wholes, axis, first):
    if axis:
        out[...] = wholes[0][:, first : first + out.shape[1]]
        return
    at, last = 0, first + out.shape[0]
    for whole in wholes:
        low, high = max(first, at), min(last, at + whole.shape[0])
        if low < high:
            out[low - first : high - first, :] = whole[low - at : high - at, :]
        at += whole.shape[0]


def half_kernel(axis, flags, *refs):
    *wholes, out = refs
    for flag in (1, 0):

        @pl.when(flags[3] == flag)
        def _():
            fill(out, wholes, axis, 0 if flag else out.shape[axis])


def half_of(flags, wholes, axis, after=()):
    dims = [sum(w.shape[0] for w in wholes), wholes[0].shape[1]]
    dims[axis] //= 2
    return call(functools.partial(half_kernel, axis), (flags, *wholes), [shape(*dims)], scalars=1, after=after)[0]


def pick_kernel(layer, count, got_count, flags, *refs):
    wholes, gots, outs = refs[:count], refs[count : count + got_count], refs[count + got_count :]
    ways = [(flags[1] == 1 - layer, wholes), (flags[1] == layer, gots)]
    if got_count > 1:
        swapped = (gots[1], gots[0], *gots[2:])
        ways = [ways[0]] + [((flags[1] == layer) & (flags[3] == flag), x) for flag, x in ((1, gots), (0, swapped))]
    for wanted, sources in ways:

        @pl.when(wanted)
        def _():
            at = 0
            for out in outs:
                fill(out, sources, 0, at)
                at += out.shape[0]


def picked(flags, layer, wholes, gots, sizes, after=()):
    outs = [shape(size, wholes[0].shape[1]) for size in sizes]
    kernel = functools.partial(pick_kernel, layer, len(wholes), len(gots))
    return call(kernel, (flags, *wholes, *gots), outs, scalars=1, after=after)


def stack_kernel(*refs):
    *wholes, out = refs
    fill(out, wholes, 0, 0)


def stacked_rows(wholes, after):
    rows = sum(w.shape[0] for w in wholes)
    return call(stack_kernel, wholes, [shape(rows, wholes[0].shape[1])], after=after)[0]


def copy_kernel(source, out):
    out[...] = source[...]


def copied(source, after):
    return call(copy_kernel, (source,), [shape(*source.shape)], after=after)[0]


def micro_kernel(flags, *refs):
    *arrays, out = refs
    n = arrays[0].shape[1]
    for flag in (1, 0):

        @pl.when(flags[1] == flag)
        def _():
            for i, both in enumerate(arrays):
                out[i * n : (i + 1) * n, :] = both[1 - flag]


def output_kernel(flags, mid_low, mid_high, part_low, part_high, got, bias, out):
    for flag, mid, part in ((1, mid_low, part_low), (0, mid_high, part_high)):

        @pl.when(flags[4] == flag)
        def _():
            out[...] = (mid[...] + (part[...].astype(FULL) + got[...].astype(FULL)) + bias[...]).astype(LOW)


def own_kernel(flags, if_low, if_high, out):
    for flag, rows in ((1, if_low), (0, if_high)):

        @pl.when(flags[4] == flag)
        def _():
            out[...] = rows[...]


def own_or(flags, if_low, if_high, after=()):
    return call(own_kernel, (flags, if_low, if_high), [shape(*if_low.shape)], scalars=1, after=after)[0]


def output_rows(flags, mids, parts, got, bias):
    return call(output_kernel, (flags, *mids, *parts, got, bias), [shape(*got.shape)], scalars=1)[0]


def body(
    inputs, cotangent, segments, ln1_gain, ln1_bias, w_query, w_key, w_value, w_out,
    ln2_gain, ln2_bias, w_up, b_up, w_down, b_down, *, n_batch,
):
    LATEST.clear()
    CHAINED[0] = False
    n, d = inputs.shape[1:]
    half = w_up.shape[2]
    section = lax.axis_index("section")
    tensor = lax.axis_index("tensor")
    batch = lax.axis_index("batch")
    on_first = section == 0
    early = tensor < 2
    outer = (tensor == 0) | (tensor == 3)
    middle = (batch == 1) | (batch == 2)
    even = batch % 2 == 0
    flags = jnp.stack([outer, on_first, middle, even, early]).astype(jnp.int32)
    paired = n_batch % 2 == 0
    beside = [(i, i ^ 1) for i in range(n_batch)]

    def across(value):
        return lax.ppermute(value, "section", SWAP)

    qkv_parts = (w_query[0].T, w_key[0].T, w_value[0].T)
    CHAINED[0] = True
    got_qkv = across(half_of(flags, qkv_parts, 0) if paired else stacked_rows(qkv_parts, ()))
    own_rows = call(micro_kernel, (flags, inputs, cotangent), [shape(2 * n, d)], scalars=1)[0]
    other_rows = to_partner(own_rows)
    got_wo = across(copied(w_out[0], ()))
    small_own = jnp.concatenate([ln1_gain, ln1_bias, ln2_gain, ln2_bias, b_down, b_up], axis=0)
    small_other = across(small_own)
    if paired:
        got_up = across(half_of(flags, (w_up[0],), 0))
        got_down = across(copied(w_down[0], (small_other,)))
        gots_feed = (got_up, lax.ppermute(got_up, "batch", beside), got_down)
    else:
        gots_feed = (across(stacked_rows((w_up[0], w_down[0]), ())),)
    CHAINED[0] = False
    gots_qkv = (got_qkv, lax.ppermute(got_qkv, "batch", beside)) if paired else jnp.split(got_qkv, 2)

    def low_high(own, other):
        return jnp.where(early, own, other), jnp.where(early, other, own)

    rows_in = low_high(own_rows[:n], other_rows[:n])
    grad_last = low_high(own_rows[n:], other_rows[n:])

    segment = jnp.where(on_first, segments[0, 0], segments[1, 0])
    low_at = jnp.where(outer, 0, 1)
    block_at = {"own_low": low_at, "sib_low": 1 - low_at, "own_high": 3 - low_at, "sib_high": 2 + low_at}

    def block_bias(query, key_blocks):
        span = jnp.arange(n)
        query_at = block_at[query] * n + span
        query_seg = lax.dynamic_slice_in_dim(segment, block_at[query] * n, n)
        rows = []
        for key in key_blocks:
            key_at = key * n + span
            key_seg = lax.dynamic_slice_in_dim(segment, key * n, n)
            kept = (key_at[:, None] <= query_at[None, :]) & (key_seg[:, None] == query_seg[None, :])
            rows.append(jnp.where(kept, 0.0, MASKED).astype(FULL))
        return jnp.concatenate(rows, axis=0)

    biases = (
        block_bias("own_low", [block_at["own_low"], block_at["sib_low"]]),
        block_bias(
            "own_high",
            [block_at["sib_low"], block_at["own_high"], jnp.where(outer, block_at["sib_high"], block_at["own_low"])],
        ),
    )

    def layer_rows(layer):
        small = jnp.where(section == layer, small_own, small_other)
        rows = [small[i : i + 1] for i in range(6)]
        return rows[:5] + [(rows[5], to_sibling(rows[5]))]

    small_0, small_1 = layer_rows(0), layer_rows(1)

    def weights(layer, wholes, gots, sizes, after):
        return [(own, to_sibling(own)) for own in picked(flags, layer, wholes, gots, sizes, after)]

    def qkv_weight(layer, after=()):
        return weights(layer, qkv_parts, gots_qkv, [3 * w_query.shape[2]], after)[0]

    def out_weight(layer, after=()):
        return weights(layer, (w_out[0],), (got_wo,), [w_out.shape[1]], after)[0]

    def feed_weights(layer, after=()):
        return weights(layer, (w_up[0], w_down[0]), gots_feed, [d, half], after)

    def attend_low(projected, sib, wo):
        return attend(False, projected[2], (projected[3], sib[0]), biases[0], *wo, None)

    def attend_high(both, sib, wo):
        return attend(True, both[1][2], (sib[0], both[1][3], sib[1], both[0][3]), biases[1], *wo, flags)

    qkv_0 = qkv_weight(0, (got_wo,))
    wo_0 = out_weight(0)
    tied = (small_0[5][1], small_1[5][1])
    proj_0, sib_0 = [], []
    for i in (0, 1):
        proj_0.append(project((rows_in[i],), small_0[0], small_0[1], qkv_0, True, tied))
        sib_0.append(to_sibling(proj_0[i][4]))
    att_0 = [attend_low(proj_0[0], sib_0, wo_0)]
    got = [to_partner(att_0[0][2])]
    att_0.append(attend_high(proj_0, sib_0, wo_0))
    got.append(to_partner(att_0[1][2]))
    if paired:
        (up_0,) = weights(0, (w_up[0],), gots_feed[:2], [d], (att_0[1][2],))
        (down_0,) = weights(0, (w_down[0],), gots_feed[2:], [half], got)
    else:
        up_0, down_0 = feed_weights(0, got)
    feed_0, feed_got, after = [], [], ()
    for i in (0, 1):
        feed_0.append(
            feed(proj_0[i][0], att_0[i][2], got[i], small_0[2], small_0[3], up_0, small_0[5], down_0, after=after)
        )
        feed_got.append(to_partner(feed_0[i][4]))
        if i == 0:
            qkv_1 = qkv_weight(1, (feed_0[0][4],))
            wo_1 = out_weight(1, (feed_0[0][4],))
            after = (qkv_1[0], wo_1[0])

    proj_1, sib_1, att_1, got, after = [], [], [], [], (feed_0[1][4], wo_1[1])
    for i in (0, 1):
        source = (feed_0[i][0], feed_0[i][4], feed_got[i], small_0[4])
        proj_1.append(project(source, small_1[0], small_1[1], qkv_1, False, after))
        sib_1.append(to_sibling(proj_1[i][4]))
        if i == 0:
            up_1, down_1 = feed_weights(1, (proj_1[0][2],))
            after = (up_1[0], down_1[0])
            att_1.append(attend_low(proj_1[0], sib_1, wo_1))
        else:
            att_1.append(attend_high(proj_1, sib_1, wo_1))
        got.append(to_partner(att_1[i][2]))
    feed_1, back_got = [], []
    for i in (0, 1):
        feed_1.append(
            feed(proj_1[i][0], att_1[i][2], got[i], small_1[2], small_1[3], up_1, small_1[5], down_1, grad_last[i])
        )
        back_got.append(to_partner(feed_1[i][4]))

    def grads_feed(g, grads, a_two, dz):
        plan = (
            ((4, 5), 0, d, (6, 7), 0, half, 0, 0),
            ((4, 5), 0, d, (6, 7), half, half, 1, 0),
            ((0, 1), 0, half, (2, 3), 0, d, 0, d),
            ((0, 1), half, half, (2, 3), 0, d, 1, d),
        )
        return outer_products((*g, *grads, *a_two, *dz), plan, d + half, d)

    def grads_attend(o, lows, a_one, d_own, d_sib):
        w, w3 = o[0].shape[1] // 2, d_own[0].shape[1]
        plan = (
            ((6, 7), 0, w3, (4, 5), 0, d, 0, 0),
            ((8, 9), 0, w3, (4, 5), 0, d, 1, 0),
            ((0, 1), 0, w, (2, 3), 0, d, 0, w3),
            ((0, 1), w, w, (2, 3), 0, d, 1, w3),
        )
        return outer_products((*o, *lows, *a_one, *d_own, *d_sib), plan, w3 + w, d)

    mids = [f[0] for f in feed_1]
    by_feed_1 = grads_feed([f[2] for f in feed_1], grad_last, [f[1] for f in feed_1], [f[3] for f in feed_1])
    feed_1_got = to_sibling(by_feed_1[1])
    out_parts = down([f[2] for f in feed_1], down_1)
    def attend_backward(i, mids, parts, grads, gain, wo, projected, sib, att, earlier, long=False):
        return attend_back(
            bool(i), flags, mids[i], parts[i], back_got[i], grads[i], gain, wo, projected[i][2],
            [p[3] for p in projected], sib, biases[i], att[i][1], earlier, long,
        )

    ab_1 = []
    for i in (0, 1):
        earlier = ab_1[0][4:6] if i else ()
        ab_1.append(
            attend_backward(i, mids, [f[4] for f in feed_1], grad_last, small_1[2], wo_1, proj_1, sib_1, att_1, earlier)
        )
    mid_grads_1, lows_1, dq = [[a[k] for a in ab_1] for k in (0, 1, 3)]
    keep, send = ab_1[1][4:6], ab_1[1][6:8]
    kv_got = [to_sibling(x) for x in send]
    back_1, part_got = [], []
    for i in (0, 1):
        back_1.append(project_back(dq[i], keep[i], kv_got[i], qkv_1))
        part_got.append(to_partner(back_1[i][2]))
    by_att_1 = grads_attend(
        [a[0] for a in att_1], lows_1, [p[1] for p in proj_1], [b[0] for b in back_1], [b[1] for b in back_1]
    )
    att_1_got = to_sibling(by_att_1[1])

    fb_0, back_got, after = [], [], by_att_1
    for i in (0, 1):
        fb_0.append(
            feed_back(
                mid_grads_1[i], back_1[i][2], part_got[i], proj_1[i][0], small_1[0], feed_0[i][3], up_0, down_0, after
            )
        )
        after = ()
        back_got.append(to_partner(fb_0[i][3]))
    grad_mid = [f[0] for f in fb_0]
    by_feed_0 = grads_feed([f[2] for f in feed_0], grad_mid, [f[1] for f in feed_0], [f[2] for f in fb_0])
    feed_0_got = to_sibling(by_feed_0[1])

    CHAINED[0] = True
    along = [[(0, 1), (3, 2)], [(1, 2), (2, 1)], [(1, 0), (2, 3)]]
    feed_pieces = ready_pieces(
        flags, (by_feed_0[0], feed_0_got), (by_feed_1[0], feed_1_got), [(d + half) // 3] * 3
    )
    stage, hops = {}, {}

    def begin(k, piece):
        stage[k], hops[k] = (piece[0], across(piece[1])), 0

    def advance(*ks, after=(), extra=4):
        if n_batch != 4:
            ks = [k for k in ks if hops[k] == 0]
        if not ks:
            return
        values = call(
            functools.partial(sums_kernel, tuple(k == extra for k in ks)), [x for k in ks for x in stage[k]], [shape(*stage[k][0].shape) for k in ks],
            after=[stage[k][1] for k in after], micros=0.5 * len(ks),
        )
        for k, value in zip(ks, values):
            stage[k] = (value, lax.ppermute(value, "batch", along[hops[k]]) if n_batch == 4 else value)
            hops[k] += 1

    def settled(ks, sizes, extra=False):
        if n_batch == 4:
            return chosen(flags, [stage[k] for k in ks], sizes, 2, extra)
        return chosen(flags, [(lax.psum(stage[k][0], "batch"), stage[k][0]) for k in ks], sizes, None, extra)

    begin(0, feed_pieces[0])
    begin(1, feed_pieces[1])
    begin(2, feed_pieces[2])
    parts_0 = [f[3] for f in fb_0]
    mids_0 = [f[0] for f in feed_0]
    ab_0 = []
    for i in (0, 1):
        earlier = ab_0[0][4:6] if i else ()
        ab_0.append(
            attend_backward(i, mids_0, parts_0, grad_mid, small_0[2], wo_0, proj_0, sib_0, att_0, earlier, True)
        )
    mid_grads_0, lows_0, dq = [[a[k] for a in ab_0] for k in (0, 1, 3)]
    keep, send = ab_0[1][4:6], ab_0[1][6:8]
    advance(0)
    kv_got = [to_sibling(x) for x in send]
    back_0 = [project_back(dq[i], keep[i], kv_got[i], qkv_0) for i in (0, 1)]
    part_got = to_partner(own_or(flags, back_0[1][2], back_0[0][2]))
    by_att_0 = grads_attend(
        [a[0] for a in att_0], lows_0, [p[1] for p in proj_0], [b[0] for b in back_0], [b[1] for b in back_0]
    )
    att_0_got = to_sibling(by_att_0[1])
    att_rows = by_att_0[0].shape[0]
    att_sides = (by_att_0[0], att_0_got), (by_att_1[0], att_1_got)

    last, one_0 = last_rows(flags, [b[2] for b in back_0], part_got, mid_grads_0, rows_in, small_0[0])
    operands = (
        one_0, fb_0[0][1], fb_0[1][1], ab_0[0][2], ab_0[1][2], ab_1[0][2], ab_1[1][2], feed_1[0][6], feed_1[1][6], fb_0[0][4], fb_0[1][4],
        feed_1[0][5], feed_1[1][5],
    )
    rows, own = call(gather_kernel, operands, [shape(12, d, dtype=FULL), shape(2, half, dtype=FULL)])
    rows = call(chip_kernel, (rows, own, to_sibling(rows)), [shape(12, d, dtype=FULL)])[0]
    advance(0, 1)
    small = call(layers_kernel, (flags, rows, to_partner(rows)), [shape(EXTRA // 2, d, dtype=FULL)] * 2, scalars=1)
    att_pieces = ready_pieces(flags, *att_sides, [att_rows // 2] * 2, small=small)
    begin(3, att_pieces[0])
    begin(4, att_pieces[1])
    advance(2, 1, 0)

    def micro_sent(first, second):
        mine = jnp.where(on_first, first, second)
        return mine, across(jnp.where(on_first, second, first))

    def micro_out(mine, got):
        return call(micro_out_kernel, (flags, mine, got), [shape(2, n, d)], scalars=1)[0][None]

    advance(3, 2, 1)
    backward = micro_sent(last, jnp.where(early, *grad_mid))
    out_got = to_partner(own_or(flags, out_parts[1], out_parts[0]))
    advance(4, 3, 2, after=(0,))
    out_1 = output_rows(flags, mids, out_parts, out_got, small_1[4])
    forward = micro_sent(jnp.where(early, *[p[0] for p in proj_1]), out_1)
    advance(4, 3, after=(1,))
    advance(4, after=(2,))
    up_total, down_total = settled((0, 1, 2), [d, half])
    query_total, key_total = settled((3,), [att_rows // 4] * 2)
    backward_out = micro_out(*backward)
    forward_out = micro_out(*forward)
    value_total, out_total, sums = settled((4,), [att_rows // 4] * 2, True)
    att_totals = [query_total, key_total, value_total, out_total]
    return (
        forward_out,
        backward_out,
        sums[0:1],
        sums[1:2],
        *[x.T[None] for x in att_totals[:3]],
        att_totals[3][None],
        sums[2:3],
        sums[3:4],
        up_total[None],
        sums[5:6],
        down_total[None],
        sums[4:5],
    )


def solution(mesh):
    rows = P(None, ("batch", "tensor"), None)
    layer = P("section", None)
    by_column = P("section", None, "tensor")
    by_row = P("section", "tensor", None)
    kept = P("section", None, ("batch", "tensor"), None)
    return jax.shard_map(
        functools.partial(body, n_batch=mesh.shape["batch"]),
        mesh=mesh,
        in_specs=(
            rows, rows, P(None, "batch", None), layer, layer, by_column, by_column, by_column, by_row,
            layer, layer, by_column, P("section", "tensor"), by_row, layer,
        ),
        out_specs=(
            kept, kept, layer, layer, by_column, by_column, by_column, by_row,
            layer, layer, by_column, P("section", "tensor"), by_row, layer,
        ),
        check_vma=False,
    )
```

```python
import functools

import jax
import jax.numpy as jnp
from jax import lax
from jax.experimental import pallas as pl
from jax.experimental.pallas import tpu as pltpu
from jax.sharding import PartitionSpec as P

HEAD_DIM = 64
EPSILON = 1e-05
LOW = jnp.bfloat16
FULL = jnp.float32
SCALING = HEAD_DIM**-0.5
EXTRA = 32
MASKED = -1e30
VMEM_BYTES = 16 * 1024 * 1024

SIBLING = [(0, 1), (1, 0), (2, 3), (3, 2)]
PARTNER = [(0, 3), (3, 0), (1, 2), (2, 1)]
SWAP = [(0, 1), (1, 0)]


def dot(left, right):
    return jnp.dot(left, right, preferred_element_type=FULL)


def dot_rows(left, right):
    return lax.dot_general(left, right, (((0,), (0,)), ((), ())), preferred_element_type=FULL)


def dot_back(left, right):
    return lax.dot_general(left, right, (((1,), (1,)), ((), ())), preferred_element_type=FULL)


def norm_rows(values):
    center = values - jnp.mean(values, axis=-1, keepdims=True)
    inverse = lax.rsqrt(jnp.mean(center * center, axis=-1, keepdims=True) + EPSILON)
    return center * inverse, inverse


def norm_back(grad_norm, normed, inverse, gain):
    scaled = grad_norm * gain
    mean_one = jnp.mean(scaled, axis=-1, keepdims=True)
    mean_two = jnp.mean(scaled * normed, axis=-1, keepdims=True)
    return inverse * (scaled - mean_one - normed * mean_two)


def to_partner(value):
    return lax.ppermute(value, "tensor", PARTNER)


def to_sibling(value):
    return lax.ppermute(value, "tensor", SIBLING)


LATEST = []
CHAINED = [False]
PACE = 6e7


def call(kernel, operands, outs, scalars=0, scratch=(), after=(), micros=0.6):
    after = (*LATEST, *after) if CHAINED[0] else tuple(after)
    count, waited = len(operands), len(after)
    specs = [pl.BlockSpec(memory_space=pltpu.SMEM)] * scalars
    specs += [pl.BlockSpec(memory_space=pltpu.VMEM)] * (count - scalars)
    specs += [pl.BlockSpec(memory_space=pl.ANY)] * waited
    got = pl.pallas_call(
        lambda *refs: kernel(*refs[:count], *refs[count + waited :]),
        out_shape=tuple(outs),
        in_specs=specs,
        out_specs=tuple(pl.BlockSpec(memory_space=pltpu.VMEM) for _ in outs),
        scratch_shapes=list(scratch),
        compiler_params=pltpu.CompilerParams(vmem_limit_bytes=VMEM_BYTES),
        cost_estimate=pl.CostEstimate(flops=int(micros * PACE), bytes_accessed=1024, transcendentals=0),
    )(*operands, *after)
    LATEST[:] = [min(got, key=lambda array: array.size)]
    return got


def shape(*dims, dtype=LOW):
    return jax.ShapeDtypeStruct(dims, dtype)


def halves(pieces):
    middle = len(pieces) // 2
    return pieces[:middle], pieces[middle:]


def stacked(pieces, axis=0):
    return jnp.concatenate([p[...] for p in pieces], axis=axis) if len(pieces) > 1 else pieces[0][...]


def project_kernel(first, *refs):
    if first:
        rows_ref, gain, bias, *ws, a_ref, q_ref, kv_ref, send_ref = refs
        layer_in = rows_ref[...].astype(FULL)
    else:
        mid, part, got, b_down, gain, bias, *ws, in_ref, a_ref, q_ref, kv_ref, send_ref = refs
        low = (mid[...] + (part[...].astype(FULL) + got[...].astype(FULL)) + b_down[...]).astype(LOW)
        in_ref[...] = low
        layer_in = low.astype(FULL)
    normed, _ = norm_rows(layer_in)
    a_one = (normed * gain[...] + bias[...]).astype(LOW)
    a_ref[...] = a_one
    own, sib = [dot_back(a_one, stacked(w)).astype(LOW) for w in halves(ws)]
    w = own.shape[1] // 3
    q_own, k_own, v_own = own[:, :w], own[:, w : 2 * w], own[:, 2 * w :]
    q_sib, k_sib, v_sib = sib[:, :w], sib[:, w : 2 * w], sib[:, 2 * w :]
    q_ref[...] = jnp.concatenate([q_own, q_sib], axis=1) * jnp.asarray(SCALING, LOW)
    kv_ref[...] = jnp.concatenate([k_own, k_sib, v_own, v_sib], axis=1)
    send_ref[...] = jnp.concatenate([k_sib, k_own, v_sib, v_own], axis=1)


def project(source, gain, bias, weights, first, after=()):
    n, d = source[0].shape
    h = sum(w.shape[0] for w in weights) // 3
    outs = [shape(n, d), shape(n, h), shape(n, 2 * h), shape(n, 2 * h)]
    if not first:
        outs = [shape(n, d)] + outs
    got = call(
        functools.partial(project_kernel, first),
        (*source, gain, bias, *weights),
        outs,
        after=after,
        micros=1.1,
    )
    return got if not first else (source[0], *got)


def pair_masks(q_pair):
    lane = lax.broadcasted_iota(jnp.int32, q_pair.shape, 1)
    zero = jnp.zeros_like(q_pair)
    return jnp.where(lane < HEAD_DIM, q_pair, zero), jnp.where(lane < HEAD_DIM, zero, q_pair)


def attend_kernel(late, *refs):
    if late:
        outer, q_ref, sib_low, own_high, sib_high, own_low, bias_ref, wo_own, wo_sib, o_ref, lse_ref, part_ref, extra = refs

        @pl.when(outer[0] == 1)
        def _():
            extra[...] = sib_high[...]

        @pl.when(outer[0] == 0)
        def _():
            extra[...] = own_low[...]

        kv = jnp.concatenate([sib_low[...], own_high[...], extra[...]], axis=0)
    else:
        q_ref, own_low, sib_low, bias_ref, wo_own, wo_sib, o_ref, lse_ref, part_ref = refs
        kv = jnp.concatenate([own_low[...], sib_low[...]], axis=0)
    h = kv.shape[1] // 2
    keys, values = kv[:, :h], kv[:, h:]
    values_t = values.T
    outs, sums = [], []
    for pair in range(h // 128):
        lanes = slice(pair * 128, pair * 128 + 128)
        for j, q in enumerate(pair_masks(q_ref[:, lanes])):
            head = 2 * pair + j
            scores = dot_back(keys[:, lanes], q) + bias_ref[...]
            highest = jnp.max(scores, axis=0, keepdims=True)
            e = jnp.exp(scores - highest)
            total = jnp.sum(e, axis=0, keepdims=True)
            mixed = dot(values_t[head * HEAD_DIM : (head + 1) * HEAD_DIM], e.astype(LOW))
            outs.append(mixed * (1.0 / total))
            sums.append(highest + jnp.log(total))
    o = jnp.concatenate(outs, axis=0).T.astype(LOW)
    o_ref[...] = o
    lse_ref[...] = jnp.concatenate(sums + sums[: 8 - len(sums)], axis=0)
    half = wo_own.shape[0]
    part_ref[...] = (dot(o[:, :half], wo_own[...]) + dot(o[:, half:], wo_sib[...])).astype(LOW)


def attend(late, q, blocks, bias, wo_own, wo_sib, outer, after=()):
    n, h = q.shape
    d = wo_own.shape[1]
    operands = ((outer,) if late else ()) + (q, *blocks, bias, wo_own, wo_sib)
    return call(
        functools.partial(attend_kernel, late),
        operands,
        [shape(n, h), shape(8, n, dtype=FULL), shape(n, d)],
        scalars=1 if late else 0,
        scratch=[pltpu.VMEM((n, 2 * h), LOW)] if late else (),
        after=after,
        micros=4.5 if late else 3.2,
    )


def gelu_parts(z):
    c = 0.7978845608028654
    square = z * z
    t = jnp.tanh(c * (z + 0.044715 * (square * z)))
    half = 0.5 * (1.0 + t)
    return z * half, half + 0.5 * z * (1.0 - t * t) * (c + (3.0 * 0.044715 * c) * square)


def feed_kernel(last, ups, dns, *refs):
    refs = (*refs[:7], refs[7 : 7 + ups], refs[7 + ups : 7 + ups + dns], *refs[7 + ups + dns :])
    if last:
        (u, part, got, gain, bias, b_own, b_sib, ups, dns, grad_ref,
         mid_ref, a_ref, g_ref, dz_ref, back_ref, hidden_sum, row_sum) = refs
    else:
        (u, part, got, gain, bias, b_own, b_sib, ups, dns,
         mid_ref, a_ref, g_ref, slope_ref, out_ref) = refs
    mid = u[...].astype(FULL) + (part[...].astype(FULL) + got[...].astype(FULL))
    mid_ref[...] = mid
    normed, _ = norm_rows(mid)
    a_two = (normed * gain[...] + bias[...]).astype(LOW)
    a_ref[...] = a_two
    f = b_own.shape[1]
    step = 256
    total = jnp.zeros(mid.shape, FULL)
    for side, (up, b, dn) in enumerate(zip(halves(ups), (b_own, b_sib), halves(dns))):
        up, dn = stacked(up, axis=1), stacked(dn)
        for at in range(0, f, step):
            cols = slice(at, at + step)
            here = slice(side * f + at, side * f + at + step)
            z = dot(a_two, up[:, cols]) + b[:, cols]
            g, slope = gelu_parts(z)
            g = g.astype(LOW)
            g_ref[:, here] = g
            if last:
                dz = (dot_back(grad_ref[...], dn[cols, :]) * slope).astype(LOW)
                dz_ref[:, here] = dz
                hidden_sum[:, here] = jnp.sum(dz.astype(FULL), axis=0, keepdims=True)
                total = total + dot_back(dz, up[:, cols])
            else:
                slope_ref[:, here] = slope.astype(LOW)
                total = total + dot(g, dn[cols, :])
    if last:
        back_ref[...] = total.astype(LOW)
        row_sum[...] = jnp.sum(grad_ref[...].astype(FULL), axis=0, keepdims=True)
    else:
        out_ref[...] = total.astype(LOW)


def feed(u, part, got, gain, bias, up, b_up, dn, grad=None, after=()):
    n, d = u.shape
    f = b_up[0].shape[1]
    last = grad is not None
    outs = [shape(n, d, dtype=FULL), shape(n, d), shape(n, 2 * f), shape(n, 2 * f), shape(n, d)]
    operands = (u, part, got, gain, bias, *b_up, *up, *dn) + ((grad,) if last else ())
    if last:
        outs += [shape(1, 2 * f, dtype=FULL), shape(1, d, dtype=FULL)]
    return call(functools.partial(feed_kernel, last, len(up), len(dn)), operands, outs, after=after, micros=3.2)


def feed_back_kernel(ups, dns, mid_grad, part, got, in_ref, gain, slope, *refs):
    grad_ref, sums_ref, dz_ref, back_ref, hidden_sum = refs[ups + dns :]
    ups, dns = refs[:ups], refs[ups : ups + dns]
    grad_norm = part[...].astype(FULL) + got[...].astype(FULL)
    normed, inverse = norm_rows(in_ref[...].astype(FULL))
    grad = (mid_grad[...] + norm_back(grad_norm, normed, inverse, gain[...])).astype(LOW)
    grad_ref[...] = grad
    sums_ref[...] = jnp.concatenate(
        [
            jnp.sum(grad_norm * normed, axis=0, keepdims=True),
            jnp.sum(grad_norm, axis=0, keepdims=True),
            jnp.sum(grad.astype(FULL), axis=0, keepdims=True),
        ],
        axis=0,
    )
    f = slope.shape[1] // 2
    step = 256
    total = jnp.zeros(grad.shape, FULL)
    for side, (up, dn) in enumerate(zip(halves(ups), halves(dns))):
        up, dn = stacked(up, axis=1), stacked(dn)
        for at in range(0, f, step):
            cols = slice(at, at + step)
            here = slice(side * f + at, side * f + at + step)
            dz = (dot_back(grad, dn[cols, :]) * slope[:, here].astype(FULL)).astype(LOW)
            dz_ref[:, here] = dz
            hidden_sum[:, here] = jnp.sum(dz.astype(FULL), axis=0, keepdims=True)
            total = total + dot_back(dz, up[:, cols])
    back_ref[...] = total.astype(LOW)


def feed_back(mid_grad, part, got, layer_in, gain, slope, up, dn, after=()):
    n, d = mid_grad.shape
    f = slope.shape[1] // 2
    outs = [shape(n, d), shape(3, d, dtype=FULL), shape(n, 2 * f), shape(n, d), shape(1, 2 * f, dtype=FULL)]
    return call(
        functools.partial(feed_back_kernel, len(up), len(dn)), (mid_grad, part, got, layer_in, gain, slope, *up, *dn), outs, after=after, micros=2.9
    )


def attend_back_kernel(late, *refs):
    if late:
        (flags, mid, part, got, grad, gain, wo_own, wo_sib, q_ref, bias, lse, own_low, own_high, sib_low, sib_high,
         low_kept, low_sent, mid_ref, low_ref, sums_ref, dq_ref, keep_low, keep_high, send_low, send_high,
         extra, acc_low, acc_high) = refs
        outside = flags[0].astype(FULL)

        @pl.when(flags[0] == 1)
        def _():
            extra[...] = sib_high[...]

        @pl.when(flags[0] == 0)
        def _():
            extra[...] = own_low[...]

        blocks = (sib_low, own_high, extra)
    else:
        (mid, part, got, grad, gain, wo_own, wo_sib, q_ref, bias, lse, own_low, sib_low,
         mid_ref, low_ref, sums_ref, dq_ref, keep_low, acc_low) = refs
        blocks = (own_low, sib_low)
    n = mid.shape[0]
    grad_norm = part[...].astype(FULL) + got[...].astype(FULL)
    normed, inverse = norm_rows(mid[...])
    mid_grad = grad[...].astype(FULL) + norm_back(grad_norm, normed, inverse, gain[...])
    mid_ref[...] = mid_grad
    low = mid_grad.astype(LOW)
    low_ref[...] = low
    sums_ref[0:1, :] = jnp.sum(grad_norm * normed, axis=0, keepdims=True)
    sums_ref[1:2, :] = jnp.sum(grad_norm, axis=0, keepdims=True)
    do = jnp.concatenate([dot_back(low, wo_own[...]), dot_back(low, wo_sib[...])], axis=1).astype(LOW)
    kv = jnp.concatenate([b[...] for b in blocks], axis=0)
    h = kv.shape[1] // 2
    keys, values = kv[:, :h], kv[:, h:]
    keys_t = keys.T
    dq = []
    for pair in range(h // 128):
        lanes = slice(pair * 128, pair * 128 + 128)
        dk = dv = None
        qs_two, do_two = pair_masks(q_ref[:, lanes]), pair_masks(do[:, lanes])
        for j in (0, 1):
            head = 2 * pair + j
            scores = dot_back(keys[:, lanes], qs_two[j]) + bias[...]
            p = jnp.exp(scores - lse[head : head + 1, :])
            dp = dot_back(values[:, lanes], do_two[j])
            inner = jnp.sum(p * dp, axis=0, keepdims=True)
            ds = (p * (dp - inner)).astype(LOW)
            dv_now = dot(p.astype(LOW), do_two[j])
            dk_now = dot(ds, qs_two[j])
            dk = dk_now if dk is None else dk + dk_now
            dv = dv_now if dv is None else dv + dv_now
            dq.append(dot(keys_t[head * HEAD_DIM : (head + 1) * HEAD_DIM], ds) * SCALING)
        for value, where in ((dk, lanes), (dv, slice(h + pair * 128, h + pair * 128 + 128))):
            if late:
                acc_low[:, where] = low_sent[:, where] + value[:n]
                keep_high[:, where] = value[n : 2 * n]
                keep_low[:, where] = low_kept[:, where] + value[2 * n :] * (1.0 - outside)
                acc_high[:, where] = value[2 * n :] * outside
            else:
                keep_low[:, where] = value[:n]
                acc_low[:, where] = value[n:]
    dq_ref[...] = jnp.concatenate(dq, axis=0).T.astype(LOW)
    if late:
        for acc, out in ((acc_low, send_low), (acc_high, send_high)):
            send = acc[...].astype(LOW)
            w = send.shape[1] // 4
            out[...] = jnp.concatenate(
                [send[:, w : 2 * w], send[:, :w], send[:, 3 * w :], send[:, 2 * w : 3 * w]], axis=1
            )


def attend_back(late, flags, mid, part, got, grad, gain, wo, q, own, sib, bias, lse, earlier, long):
    n, d = mid.shape
    h = q.shape[1]
    outs = [shape(n, d, dtype=FULL), shape(n, d), shape(2, d, dtype=FULL), shape(n, h)]
    outs += [shape(n, 2 * h, dtype=FULL)] * 2
    common = (mid, part, got, grad, gain, *wo, q, bias, lse)
    if late:
        outs += [shape(n, 2 * h)] * 2
        operands = (flags, *common, *own, *sib, *earlier)
    else:
        operands = (*common, own[0], sib[0])
    return call(
        functools.partial(attend_back_kernel, late),
        operands,
        outs,
        scalars=int(late),
        scratch=[pltpu.VMEM((n, 2 * h), LOW)] + [pltpu.VMEM((n, 2 * h), FULL)] * 2 if late else (),
        micros=300.0 if long else 5.5 if late else 4.0,
    )


def project_back_kernel(dq, keep, got, *refs):
    *ws, own_ref, sib_ref, part_ref = refs
    dkv = (keep[...] + got[...].astype(FULL)).astype(LOW)
    w = dkv.shape[1] // 4
    own = jnp.concatenate([dq[:, :w], dkv[:, :w], dkv[:, 2 * w : 3 * w]], axis=1)
    sib = jnp.concatenate([dq[:, w:], dkv[:, w : 2 * w], dkv[:, 3 * w :]], axis=1)
    own_ref[...] = own
    sib_ref[...] = sib
    w_own, w_sib = [stacked(x) for x in halves(ws)]
    part_ref[...] = (dot(own, w_own) + dot(sib, w_sib)).astype(LOW)


def project_back(dq, keep, got, weights):
    n = dq.shape[0]
    w, d = sum(x.shape[0] for x in weights) // 2, weights[0].shape[1]
    outs = [shape(n, w), shape(n, w), shape(n, d)]
    return call(project_back_kernel, (dq, keep, got, *weights), outs, micros=0.9)


def outer_kernel(plan, *refs):
    outs = refs[-2:]
    for lefts, first, count, rights, at, width, which, base in plan:
        right = jnp.concatenate([refs[i][:, at : at + width] for i in rights], axis=0)
        for row in range(0, count, 256):
            size = min(256, count - row)
            cols = slice(first + row, first + row + size)
            left = jnp.concatenate([refs[i][:, cols] for i in lefts], axis=0)
            outs[which][base + row : base + row + size, :] = dot_rows(left, right).astype(LOW)


def outer_products(operands, plan, rows, width, after=()):
    return call(functools.partial(outer_kernel, plan), operands, [shape(rows, width)] * 2, after=after, micros=2.5)


def down_kernel(count, *refs):
    gs, dns, outs = refs[:2], refs[2 : 2 + count], refs[2 + count :]
    dn = stacked(dns)
    for g, out in zip(gs, outs):
        out[...] = dot(g[...], dn).astype(LOW)


def down(gs, dns, after=()):
    n, d = gs[0].shape[0], dns[0].shape[1]
    return call(functools.partial(down_kernel, len(dns)), (*gs, *dns), [shape(n, d)] * 2, after=after, micros=1.4)


def ready_kernel(cuts, extra, flags, first_own, first_got, second_own, second_got, *refs):
    small, outs = refs[:extra], refs[extra:]
    for i, (at, size) in enumerate(cuts):
        rows = slice(at, at + size)
        first = (first_own[rows, :].astype(FULL) + first_got[rows, :].astype(FULL)).astype(LOW)
        second = (second_own[rows, :].astype(FULL) + second_got[rows, :].astype(FULL)).astype(LOW)
        mine, theirs = outs[2 * i], outs[2 * i + 1]

        @pl.when(flags[1] == 1)
        def _():
            mine[:size, :] = first
            theirs[:size, :] = second

        @pl.when(flags[1] == 0)
        def _():
            mine[:size, :] = second
            theirs[:size, :] = first

    for values, out in zip(small, outs[-2:]):
        split_rows(values[...], out)


def split_rows(values, out):
    first = out.shape[0] - EXTRA
    rounded = values.astype(LOW)
    out[first : first + EXTRA // 2, :] = rounded
    out[first + EXTRA // 2 :, :] = (values - rounded.astype(FULL)).astype(LOW)


def joined_rows(ref):
    first = ref.shape[0] - EXTRA
    return ref[first : first + EXTRA // 2, :].astype(FULL) + ref[first + EXTRA // 2 :, :].astype(FULL)


def ready_pieces(flags, first, second, sizes, at=0, small=()):
    cuts = []
    for size in sizes:
        cuts.append((at, size))
        at += size
    width = first[0].shape[1]
    outs = [shape(size, width) for size in sizes for _ in (0, 1)]
    if small:
        outs[-2:] = [shape(sizes[-1] + EXTRA, width)] * 2
    got = call(
        functools.partial(ready_kernel, tuple(cuts), len(small)), (flags, *first, *second, *small), outs, scalars=1
    )
    return [(got[2 * i], got[2 * i + 1]) for i in range(len(sizes))]


def sums_kernel(extra, *refs):
    count = len(refs) // 3
    for i in range(count):
        left, right, out = refs[2 * i], refs[2 * i + 1], refs[2 * count + i]
        if not extra[i]:
            out[...] = (left[...].astype(FULL) + right[...].astype(FULL)).astype(LOW)
        else:
            bulk = slice(0, out.shape[0] - EXTRA)
            out[bulk, :] = (left[bulk, :].astype(FULL) + right[bulk, :].astype(FULL)).astype(LOW)
            split_rows(joined_rows(left) + joined_rows(right), out)


def added(left, right, after=()):
    return call(added_kernel, (left, right), [shape(*left.shape, dtype=left.dtype)], after=after)[0]


def chosen_kernel(count, which, extra, flags, *refs):
    sums, gots, outs = refs[:count], refs[count : 2 * count], refs[2 * count :]
    outs, small = outs[: len(outs) - extra], outs[len(outs) - extra :]
    for flag, pieces in ((1, sums), (0, gots)):

        @pl.when(flags[which] == flag)
        def _():
            first = 0
            for out in outs:
                at, last = 0, first + out.shape[0]
                for piece in pieces:
                    low, high = max(first, at), min(last, at + piece.shape[0])
                    if low < high:
                        out[low - first : high - first, :] = piece[low - at : high - at, :].astype(FULL)
                    at += piece.shape[0]
                first = last
            for out in small:
                out[...] = joined_rows(pieces[-1])


def chosen(flags, stages, sizes, which, extra=False):
    if which is None:
        flags, which = jnp.ones_like(flags), 0
    operands = (flags, *[low for low, _ in stages], *[got for _, got in stages])
    outs = [shape(size, stages[0][0].shape[1], dtype=FULL) for size in (*sizes, EXTRA // 2)[: len(sizes) + extra]]
    return call(functools.partial(chosen_kernel, len(stages), which, int(extra)), operands, outs, scalars=1)


def micro_out_kernel(flags, mine, got, out):
    for flag, first, second in ((1, mine, got), (0, got, mine)):

        @pl.when(flags[1] == flag)
        def _():
            out[0] = first[...]
            out[1] = second[...]


def last_kernel(flags, part_low, part_high, got, mid_low, mid_high, in_low, in_high, gain, out, sums):
    for flag, part, mid, rows in ((1, part_low, mid_low, in_low), (0, part_high, mid_high, in_high)):

        @pl.when(flags[4] == flag)
        def _():
            grad_norm = part[...].astype(FULL) + got[...].astype(FULL)
            normed, inverse = norm_rows(rows[...].astype(FULL))
            out[...] = (mid[...] + norm_back(grad_norm, normed, inverse, gain[...])).astype(LOW)
            sums[0:1, :] = 2.0 * jnp.sum(grad_norm * normed, axis=0, keepdims=True)
            sums[1:2, :] = 2.0 * jnp.sum(grad_norm, axis=0, keepdims=True)


def last_rows(flags, parts, got, mids, rows, gain):
    n, d = got.shape
    return call(
        last_kernel, (flags, *parts, got, *mids, *rows, gain), [shape(n, d), shape(2, d, dtype=FULL)], scalars=1,
        micros=1.0,
    )


def gather_kernel(one_0, one_lo, one_hi, two_lo_0, two_hi_0, two_lo_1, two_hi_1, down_lo, down_hi, up_lo_0, up_hi_0, up_lo_1, up_hi_1, rows, own):
    half = own.shape[1]
    both = one_lo[...] + one_hi[...]
    rows[0:2, :] = one_0[...]
    rows[2:4, :] = two_lo_0[...] + two_hi_0[...]
    rows[4:5, :] = both[2:3]
    rows[5:7, :] = both[0:2]
    rows[7:9, :] = two_lo_1[...] + two_hi_1[...]
    rows[9:10, :] = down_lo[...] + down_hi[...]
    for i, hidden in enumerate((up_lo_0[...] + up_hi_0[...], up_lo_1[...] + up_hi_1[...])):
        rows[10 + i : 11 + i, :] = hidden[:, half:]
        own[i : i + 1, :] = hidden[:, :half]


def chip_kernel(rows, own, got, out):
    out[0:10, :] = rows[0:10, :] + got[0:10, :]
    out[10:12, :] = own[...] + got[10:12, :]


def layers_kernel(flags, rows, got, mine, theirs):
    both = (rows[0:10, :] + got[0:10, :]) * 0.5
    for flag, first, second in ((1, mine, theirs), (0, theirs, mine)):

        @pl.when(flags[1] == flag)
        def _():
            first[...] = jnp.zeros_like(first)
            second[...] = jnp.zeros_like(second)
            first[0:5, :] = both[0:5]
            first[5:6, :] = rows[10:11, :]
            second[0:5, :] = both[5:10]
            second[5:6, :] = rows[11:12, :]


def fill(out, wholes, axis, first):
    if axis:
        out[...] = wholes[0][:, first : first + out.shape[1]]
        return
    at, last = 0, first + out.shape[0]
    for whole in wholes:
        low, high = max(first, at), min(last, at + whole.shape[0])
        if low < high:
            out[low - first : high - first, :] = whole[low - at : high - at, :]
        at += whole.shape[0]


def half_kernel(axis, flags, *refs):
    *wholes, out = refs
    for flag in (1, 0):

        @pl.when(flags[3] == flag)
        def _():
            fill(out, wholes, axis, 0 if flag else out.shape[axis])


def half_rows_kernel(flags, *refs):
    *wholes, out, sems = refs
    size = out.shape[0]
    for flag in (1, 0):

        @pl.when(flags[3] == flag)
        def _():
            first, at, copies = 0 if flag else size, 0, []
            for i, whole in enumerate(wholes):
                low, high = max(first, at), min(first + size, at + whole.shape[0])
                if low < high:
                    rows = pl.ds(low - at, high - low)
                    copies.append(
                        pltpu.make_async_copy(whole.at[rows], out.at[pl.ds(low - first, high - low)], sems.at[i])
                    )
                at += whole.shape[0]
            for copy in copies:
                copy.start()
            for copy in copies:
                copy.wait()


def half_rows(flags, wholes):
    size = sum(w.shape[0] for w in wholes) // 2
    got = pl.pallas_call(
        half_rows_kernel,
        out_shape=shape(size, wholes[0].shape[1]),
        in_specs=[pl.BlockSpec(memory_space=pltpu.SMEM)] + [pl.BlockSpec(memory_space=pl.ANY)] * len(wholes),
        out_specs=pl.BlockSpec(memory_space=pltpu.VMEM),
        scratch_shapes=[pltpu.SemaphoreType.DMA((len(wholes),))],
        cost_estimate=pl.CostEstimate(flops=1024, bytes_accessed=1024, transcendentals=0),
    )(flags, *wholes)
    LATEST[:] = [got]
    return got


def half_of(flags, wholes, axis, after=()):
    dims = [sum(w.shape[0] for w in wholes), wholes[0].shape[1]]
    dims[axis] //= 2
    return call(functools.partial(half_kernel, axis), (flags, *wholes), [shape(*dims)], scalars=1, after=after)[0]


def pick_kernel(layer, count, got_count, flags, *refs):
    wholes, gots, outs = refs[:count], refs[count : count + got_count], refs[count + got_count :]
    ways = [(flags[1] == 1 - layer, wholes), (flags[1] == layer, gots)]
    if got_count > 1:
        swapped = (gots[1], gots[0], *gots[2:])
        ways = [ways[0]] + [((flags[1] == layer) & (flags[3] == flag), x) for flag, x in ((1, gots), (0, swapped))]
    for wanted, sources in ways:

        @pl.when(wanted)
        def _():
            at = 0
            for out in outs:
                fill(out, sources, 0, at)
                at += out.shape[0]


def picked(flags, layer, wholes, gots, sizes, after=()):
    outs = [shape(size, wholes[0].shape[1]) for size in sizes]
    kernel = functools.partial(pick_kernel, layer, len(wholes), len(gots))
    return call(kernel, (flags, *wholes, *gots), outs, scalars=1, after=after)


def stack_kernel(*refs):
    *wholes, out = refs
    fill(out, wholes, 0, 0)


def stacked_rows(wholes, after):
    rows = sum(w.shape[0] for w in wholes)
    return call(stack_kernel, wholes, [shape(rows, wholes[0].shape[1])], after=after)[0]


def copy_kernel(source, out):
    out[...] = source[...]


def copied(source, after):
    return call(copy_kernel, (source,), [shape(*source.shape)], after=after)[0]


def micro_kernel(flags, *refs):
    *arrays, out = refs
    n = arrays[0].shape[1]
    for flag in (1, 0):

        @pl.when(flags[1] == flag)
        def _():
            for i, both in enumerate(arrays):
                out[i * n : (i + 1) * n, :] = both[1 - flag]


def output_kernel(flags, mid_low, mid_high, part_low, part_high, got, bias, out):
    for flag, mid, part in ((1, mid_low, part_low), (0, mid_high, part_high)):

        @pl.when(flags[4] == flag)
        def _():
            out[...] = (mid[...] + (part[...].astype(FULL) + got[...].astype(FULL)) + bias[...]).astype(LOW)


def own_kernel(flags, if_low, if_high, out):
    for flag, rows in ((1, if_low), (0, if_high)):

        @pl.when(flags[4] == flag)
        def _():
            out[...] = rows[...]


def own_or(flags, if_low, if_high, after=()):
    return call(own_kernel, (flags, if_low, if_high), [shape(*if_low.shape)], scalars=1, after=after)[0]


def output_rows(flags, mids, parts, got, bias):
    return call(output_kernel, (flags, *mids, *parts, got, bias), [shape(*got.shape)], scalars=1)[0]


def body(
    inputs, cotangent, segments, ln1_gain, ln1_bias, w_query, w_key, w_value, w_out,
    ln2_gain, ln2_bias, w_up, b_up, w_down, b_down, *, n_batch,
):
    LATEST.clear()
    CHAINED[0] = False
    n, d = inputs.shape[1:]
    half = w_up.shape[2]
    section = lax.axis_index("section")
    tensor = lax.axis_index("tensor")
    batch = lax.axis_index("batch")
    on_first = section == 0
    early = tensor < 2
    outer = (tensor == 0) | (tensor == 3)
    middle = (batch == 1) | (batch == 2)
    even = batch % 2 == 0
    flags = jnp.stack([outer, on_first, middle, even, early]).astype(jnp.int32)
    paired = n_batch % 2 == 0
    beside = [(i, i ^ 1) for i in range(n_batch)]

    def across(value):
        return lax.ppermute(value, "section", SWAP)

    qkv_parts = (w_query[0].T, w_key[0].T, w_value[0].T)
    CHAINED[0] = True
    got_qkv = across(half_rows(flags, qkv_parts) if paired else stacked_rows(qkv_parts, ()))
    own_rows = call(micro_kernel, (flags, inputs, cotangent), [shape(2 * n, d)], scalars=1)[0]
    other_rows = to_partner(own_rows)
    got_wo = across(copied(w_out[0], ()))
    small_own = jnp.concatenate([ln1_gain, ln1_bias, ln2_gain, ln2_bias, b_down, b_up], axis=0)
    small_other = across(small_own)
    if paired:
        got_up = across(half_of(flags, (w_up[0],), 0))
        got_down = across(copied(w_down[0], (small_other,)))
        gots_feed = (got_up, lax.ppermute(got_up, "batch", beside), got_down)
    else:
        gots_feed = (across(stacked_rows((w_up[0], w_down[0]), ())),)
    CHAINED[0] = False
    gots_qkv = (got_qkv, lax.ppermute(got_qkv, "batch", beside)) if paired else jnp.split(got_qkv, 2)

    def low_high(own, other):
        return jnp.where(early, own, other), jnp.where(early, other, own)

    rows_in = low_high(own_rows[:n], other_rows[:n])
    grad_last = low_high(own_rows[n:], other_rows[n:])

    segment = jnp.where(on_first, segments[0, 0], segments[1, 0])
    low_at = jnp.where(outer, 0, 1)
    block_at = {"own_low": low_at, "sib_low": 1 - low_at, "own_high": 3 - low_at, "sib_high": 2 + low_at}

    def block_bias(query, key_blocks):
        span = jnp.arange(n)
        query_at = block_at[query] * n + span
        query_seg = lax.dynamic_slice_in_dim(segment, block_at[query] * n, n)
        rows = []
        for key in key_blocks:
            key_at = key * n + span
            key_seg = lax.dynamic_slice_in_dim(segment, key * n, n)
            kept = (key_at[:, None] <= query_at[None, :]) & (key_seg[:, None] == query_seg[None, :])
            rows.append(jnp.where(kept, 0.0, MASKED).astype(FULL))
        return jnp.concatenate(rows, axis=0)

    biases = (
        block_bias("own_low", [block_at["own_low"], block_at["sib_low"]]),
        block_bias(
            "own_high",
            [block_at["sib_low"], block_at["own_high"], jnp.where(outer, block_at["sib_high"], block_at["own_low"])],
        ),
    )

    def layer_rows(layer):
        small = jnp.where(section == layer, small_own, small_other)
        rows = [small[i : i + 1] for i in range(6)]
        return rows[:5] + [(rows[5], to_sibling(rows[5]))]

    small_0, small_1 = layer_rows(0), layer_rows(1)

    def weights(layer, wholes, gots, sizes, after):
        return [(own, to_sibling(own)) for own in picked(flags, layer, wholes, gots, sizes, after)]

    def qkv_weight(layer, after=()):
        return weights(layer, qkv_parts, gots_qkv, [3 * w_query.shape[2]], after)[0]

    def out_weight(layer, after=()):
        return weights(layer, (w_out[0],), (got_wo,), [w_out.shape[1]], after)[0]

    def feed_weights(layer, after=()):
        return weights(layer, (w_up[0], w_down[0]), gots_feed, [d, half], after)

    def attend_low(projected, sib, wo):
        return attend(False, projected[2], (projected[3], sib[0]), biases[0], *wo, None)

    def attend_high(both, sib, wo):
        return attend(True, both[1][2], (sib[0], both[1][3], sib[1], both[0][3]), biases[1], *wo, flags)

    qkv_0 = qkv_weight(0, (got_wo,))
    wo_0 = out_weight(0)
    tied = (small_0[5][1], small_1[5][1])
    proj_0, sib_0 = [], []
    for i in (0, 1):
        proj_0.append(project((rows_in[i],), small_0[0], small_0[1], qkv_0, True, tied))
        sib_0.append(to_sibling(proj_0[i][4]))
    att_0 = [attend_low(proj_0[0], sib_0, wo_0)]
    got = [to_partner(att_0[0][2])]
    att_0.append(attend_high(proj_0, sib_0, wo_0))
    got.append(to_partner(att_0[1][2]))
    if paired:
        (up_0,) = weights(0, (w_up[0],), gots_feed[:2], [d], (att_0[1][2],))
        (down_0,) = weights(0, (w_down[0],), gots_feed[2:], [half], got)
    else:
        up_0, down_0 = feed_weights(0, got)
    feed_0, feed_got, after = [], [], ()
    for i in (0, 1):
        feed_0.append(
            feed(proj_0[i][0], att_0[i][2], got[i], small_0[2], small_0[3], up_0, small_0[5], down_0, after=after)
        )
        feed_got.append(to_partner(feed_0[i][4]))
        if i == 0:
            qkv_1 = qkv_weight(1, (feed_0[0][4],))
            wo_1 = out_weight(1, (feed_0[0][4],))
            after = (qkv_1[0], wo_1[0])

    proj_1, sib_1, att_1, got, after = [], [], [], [], (feed_0[1][4], wo_1[1])
    for i in (0, 1):
        source = (feed_0[i][0], feed_0[i][4], feed_got[i], small_0[4])
        proj_1.append(project(source, small_1[0], small_1[1], qkv_1, False, after))
        sib_1.append(to_sibling(proj_1[i][4]))
        if i == 0:
            up_1, down_1 = feed_weights(1, (proj_1[0][2],))
            after = (up_1[0], down_1[0])
            att_1.append(attend_low(proj_1[0], sib_1, wo_1))
        else:
            att_1.append(attend_high(proj_1, sib_1, wo_1))
        got.append(to_partner(att_1[i][2]))
    feed_1, back_got = [], []
    for i in (0, 1):
        feed_1.append(
            feed(proj_1[i][0], att_1[i][2], got[i], small_1[2], small_1[3], up_1, small_1[5], down_1, grad_last[i])
        )
        back_got.append(to_partner(feed_1[i][4]))

    def grads_feed(g, grads, a_two, dz):
        plan = (
            ((4, 5), 0, d, (6, 7), 0, half, 0, 0),
            ((4, 5), 0, d, (6, 7), half, half, 1, 0),
            ((0, 1), 0, half, (2, 3), 0, d, 0, d),
            ((0, 1), half, half, (2, 3), 0, d, 1, d),
        )
        return outer_products((*g, *grads, *a_two, *dz), plan, d + half, d)

    def grads_attend(o, lows, a_one, d_own, d_sib):
        w, w3 = o[0].shape[1] // 2, d_own[0].shape[1]
        plan = (
            ((6, 7), 0, w3, (4, 5), 0, d, 0, 0),
            ((8, 9), 0, w3, (4, 5), 0, d, 1, 0),
            ((0, 1), 0, w, (2, 3), 0, d, 0, w3),
            ((0, 1), w, w, (2, 3), 0, d, 1, w3),
        )
        return outer_products((*o, *lows, *a_one, *d_own, *d_sib), plan, w3 + w, d)

    mids = [f[0] for f in feed_1]
    by_feed_1 = grads_feed([f[2] for f in feed_1], grad_last, [f[1] for f in feed_1], [f[3] for f in feed_1])
    feed_1_got = to_sibling(by_feed_1[1])
    out_parts = down([f[2] for f in feed_1], down_1)
    def attend_backward(i, mids, parts, grads, gain, wo, projected, sib, att, earlier, long=False):
        return attend_back(
            bool(i), flags, mids[i], parts[i], back_got[i], grads[i], gain, wo, projected[i][2],
            [p[3] for p in projected], sib, biases[i], att[i][1], earlier, long,
        )

    ab_1 = []
    for i in (0, 1):
        earlier = ab_1[0][4:6] if i else ()
        ab_1.append(
            attend_backward(i, mids, [f[4] for f in feed_1], grad_last, small_1[2], wo_1, proj_1, sib_1, att_1, earlier)
        )
    mid_grads_1, lows_1, dq = [[a[k] for a in ab_1] for k in (0, 1, 3)]
    keep, send = ab_1[1][4:6], ab_1[1][6:8]
    kv_got = [to_sibling(x) for x in send]
    back_1, part_got = [], []
    for i in (0, 1):
        back_1.append(project_back(dq[i], keep[i], kv_got[i], qkv_1))
        part_got.append(to_partner(back_1[i][2]))
    by_att_1 = grads_attend(
        [a[0] for a in att_1], lows_1, [p[1] for p in proj_1], [b[0] for b in back_1], [b[1] for b in back_1]
    )
    att_1_got = to_sibling(by_att_1[1])

    fb_0, back_got, after = [], [], by_att_1
    for i in (0, 1):
        fb_0.append(
            feed_back(
                mid_grads_1[i], back_1[i][2], part_got[i], proj_1[i][0], small_1[0], feed_0[i][3], up_0, down_0, after
            )
        )
        after = ()
        back_got.append(to_partner(fb_0[i][3]))
    grad_mid = [f[0] for f in fb_0]
    by_feed_0 = grads_feed([f[2] for f in feed_0], grad_mid, [f[1] for f in feed_0], [f[2] for f in fb_0])
    feed_0_got = to_sibling(by_feed_0[1])

    CHAINED[0] = True
    along = [[(0, 1), (3, 2)], [(1, 2), (2, 1)], [(1, 0), (2, 3)]]
    feed_pieces = ready_pieces(
        flags, (by_feed_0[0], feed_0_got), (by_feed_1[0], feed_1_got), [(d + half) // 3] * 3
    )
    stage, hops = {}, {}

    def begin(k, piece):
        stage[k], hops[k] = (piece[0], across(piece[1])), 0

    def advance(*ks, after=(), extra=4):
        if n_batch != 4:
            ks = [k for k in ks if hops[k] == 0]
        if not ks:
            return
        values = call(
            functools.partial(sums_kernel, tuple(k == extra for k in ks)), [x for k in ks for x in stage[k]], [shape(*stage[k][0].shape) for k in ks],
            after=[stage[k][1] for k in after], micros=0.5 * len(ks),
        )
        for k, value in zip(ks, values):
            stage[k] = (value, lax.ppermute(value, "batch", along[hops[k]]) if n_batch == 4 else value)
            hops[k] += 1

    def settled(ks, sizes, extra=False):
        if n_batch == 4:
            return chosen(flags, [stage[k] for k in ks], sizes, 2, extra)
        return chosen(flags, [(lax.psum(stage[k][0], "batch"), stage[k][0]) for k in ks], sizes, None, extra)

    begin(0, feed_pieces[0])
    begin(1, feed_pieces[1])
    begin(2, feed_pieces[2])
    parts_0 = [f[3] for f in fb_0]
    mids_0 = [f[0] for f in feed_0]
    ab_0 = []
    for i in (0, 1):
        earlier = ab_0[0][4:6] if i else ()
        ab_0.append(
            attend_backward(i, mids_0, parts_0, grad_mid, small_0[2], wo_0, proj_0, sib_0, att_0, earlier, True)
        )
    mid_grads_0, lows_0, dq = [[a[k] for a in ab_0] for k in (0, 1, 3)]
    keep, send = ab_0[1][4:6], ab_0[1][6:8]
    advance(0)
    kv_got = [to_sibling(x) for x in send]
    back_0 = [project_back(dq[i], keep[i], kv_got[i], qkv_0) for i in (0, 1)]
    part_got = to_partner(own_or(flags, back_0[1][2], back_0[0][2]))
    by_att_0 = grads_attend(
        [a[0] for a in att_0], lows_0, [p[1] for p in proj_0], [b[0] for b in back_0], [b[1] for b in back_0]
    )
    att_0_got = to_sibling(by_att_0[1])
    att_rows = by_att_0[0].shape[0]
    att_sides = (by_att_0[0], att_0_got), (by_att_1[0], att_1_got)

    last, one_0 = last_rows(flags, [b[2] for b in back_0], part_got, mid_grads_0, rows_in, small_0[0])
    operands = (
        one_0, fb_0[0][1], fb_0[1][1], ab_0[0][2], ab_0[1][2], ab_1[0][2], ab_1[1][2], feed_1[0][6], feed_1[1][6], fb_0[0][4], fb_0[1][4],
        feed_1[0][5], feed_1[1][5],
    )
    rows, own = call(gather_kernel, operands, [shape(12, d, dtype=FULL), shape(2, half, dtype=FULL)])
    rows = call(chip_kernel, (rows, own, to_sibling(rows)), [shape(12, d, dtype=FULL)])[0]
    advance(0, 1)
    small = call(layers_kernel, (flags, rows, to_partner(rows)), [shape(EXTRA // 2, d, dtype=FULL)] * 2, scalars=1)
    att_pieces = ready_pieces(flags, *att_sides, [att_rows // 2] * 2, small=small)
    begin(3, att_pieces[0])
    begin(4, att_pieces[1])
    advance(2, 1, 0)

    def micro_sent(first, second):
        mine = jnp.where(on_first, first, second)
        return mine, across(jnp.where(on_first, second, first))

    def micro_out(mine, got):
        return call(micro_out_kernel, (flags, mine, got), [shape(2, n, d)], scalars=1)[0][None]

    advance(3, 2, 1)
    backward = micro_sent(last, jnp.where(early, *grad_mid))
    out_got = to_partner(own_or(flags, out_parts[1], out_parts[0]))
    advance(4, 3, 2, after=(0,))
    out_1 = output_rows(flags, mids, out_parts, out_got, small_1[4])
    forward = micro_sent(jnp.where(early, *[p[0] for p in proj_1]), out_1)
    advance(4, 3, after=(1,))
    advance(4, after=(2,))
    up_total, down_total = settled((0, 1, 2), [d, half])
    query_total, key_total = settled((3,), [att_rows // 4] * 2)
    backward_out = micro_out(*backward)
    forward_out = micro_out(*forward)
    value_total, out_total, sums = settled((4,), [att_rows // 4] * 2, True)
    att_totals = [query_total, key_total, value_total, out_total]
    return (
        forward_out,
        backward_out,
        sums[0:1],
        sums[1:2],
        *[x.T[None] for x in att_totals[:3]],
        att_totals[3][None],
        sums[2:3],
        sums[3:4],
        up_total[None],
        sums[5:6],
        down_total[None],
        sums[4:5],
    )


def solution(mesh):
    rows = P(None, ("batch", "tensor"), None)
    layer = P("section", None)
    by_column = P("section", None, "tensor")
    by_row = P("section", "tensor", None)
    kept = P("section", None, ("batch", "tensor"), None)
    return jax.shard_map(
        functools.partial(body, n_batch=mesh.shape["batch"]),
        mesh=mesh,
        in_specs=(
            rows, rows, P(None, "batch", None), layer, layer, by_column, by_column, by_column, by_row,
            layer, layer, by_column, P("section", "tensor"), by_row, layer,
        ),
        out_specs=(
            kept, kept, layer, layer, by_column, by_column, by_column, by_row,
            layer, layer, by_column, P("section", "tensor"), by_row, layer,
        ),
        check_vma=False,
    )
```

```python
import functools

import jax
import jax.numpy as jnp
from jax import lax
from jax.experimental import pallas as pl
from jax.experimental.pallas import tpu as pltpu
from jax.sharding import PartitionSpec as P

HEAD_DIM = 64
EPSILON = 1e-05
LOW = jnp.bfloat16
FULL = jnp.float32
SCALING = HEAD_DIM**-0.5
EXTRA = 32
MASKED = -1e30
VMEM_BYTES = 16 * 1024 * 1024

SIBLING = [(0, 1), (1, 0), (2, 3), (3, 2)]
PARTNER = [(0, 3), (3, 0), (1, 2), (2, 1)]
SWAP = [(0, 1), (1, 0)]


def dot(left, right):
    return jnp.dot(left, right, preferred_element_type=FULL)


def dot_rows(left, right):
    return lax.dot_general(left, right, (((0,), (0,)), ((), ())), preferred_element_type=FULL)


def dot_back(left, right):
    return lax.dot_general(left, right, (((1,), (1,)), ((), ())), preferred_element_type=FULL)


def norm_rows(values):
    center = values - jnp.mean(values, axis=-1, keepdims=True)
    inverse = lax.rsqrt(jnp.mean(center * center, axis=-1, keepdims=True) + EPSILON)
    return center * inverse, inverse


def norm_back(grad_norm, normed, inverse, gain):
    scaled = grad_norm * gain
    mean_one = jnp.mean(scaled, axis=-1, keepdims=True)
    mean_two = jnp.mean(scaled * normed, axis=-1, keepdims=True)
    return inverse * (scaled - mean_one - normed * mean_two)


def to_partner(value):
    return lax.ppermute(value, "tensor", PARTNER)


def to_sibling(value):
    return lax.ppermute(value, "tensor", SIBLING)


LATEST = []
CHAINED = [False]
PACE = 6e7


def call(kernel, operands, outs, scalars=0, scratch=(), after=(), micros=0.6):
    after = (*LATEST, *after) if CHAINED[0] else tuple(after)
    count, waited = len(operands), len(after)
    specs = [pl.BlockSpec(memory_space=pltpu.SMEM)] * scalars
    specs += [pl.BlockSpec(memory_space=pltpu.VMEM)] * (count - scalars)
    specs += [pl.BlockSpec(memory_space=pl.ANY)] * waited
    got = pl.pallas_call(
        lambda *refs: kernel(*refs[:count], *refs[count + waited :]),
        out_shape=tuple(outs),
        in_specs=specs,
        out_specs=tuple(pl.BlockSpec(memory_space=pltpu.VMEM) for _ in outs),
        scratch_shapes=list(scratch),
        compiler_params=pltpu.CompilerParams(vmem_limit_bytes=VMEM_BYTES),
        cost_estimate=pl.CostEstimate(flops=int(micros * PACE), bytes_accessed=1024, transcendentals=0),
    )(*operands, *after)
    LATEST[:] = [min(got, key=lambda array: array.size)]
    return got


def shape(*dims, dtype=LOW):
    return jax.ShapeDtypeStruct(dims, dtype)


def halves(pieces):
    middle = len(pieces) // 2
    return pieces[:middle], pieces[middle:]


def stacked(pieces, axis=0):
    return jnp.concatenate([p[...] for p in pieces], axis=axis) if len(pieces) > 1 else pieces[0][...]


def project_kernel(first, *refs):
    if first:
        rows_ref, gain, bias, *ws, a_ref, q_ref, kv_ref, send_ref = refs
        layer_in = rows_ref[...].astype(FULL)
    else:
        mid, part, got, b_down, gain, bias, *ws, in_ref, a_ref, q_ref, kv_ref, send_ref = refs
        low = (mid[...] + (part[...].astype(FULL) + got[...].astype(FULL)) + b_down[...]).astype(LOW)
        in_ref[...] = low
        layer_in = low.astype(FULL)
    normed, _ = norm_rows(layer_in)
    a_one = (normed * gain[...] + bias[...]).astype(LOW)
    a_ref[...] = a_one
    own, sib = [dot_back(a_one, stacked(w)).astype(LOW) for w in halves(ws)]
    w = own.shape[1] // 3
    q_own, k_own, v_own = own[:, :w], own[:, w : 2 * w], own[:, 2 * w :]
    q_sib, k_sib, v_sib = sib[:, :w], sib[:, w : 2 * w], sib[:, 2 * w :]
    q_ref[...] = jnp.concatenate([q_own, q_sib], axis=1) * jnp.asarray(SCALING, LOW)
    kv_ref[...] = jnp.concatenate([k_own, k_sib, v_own, v_sib], axis=1)
    send_ref[...] = jnp.concatenate([k_sib, k_own, v_sib, v_own], axis=1)


def project(source, gain, bias, weights, first, after=()):
    n, d = source[0].shape
    h = sum(w.shape[0] for w in weights) // 3
    outs = [shape(n, d), shape(n, h), shape(n, 2 * h), shape(n, 2 * h)]
    if not first:
        outs = [shape(n, d)] + outs
    got = call(
        functools.partial(project_kernel, first),
        (*source, gain, bias, *weights),
        outs,
        after=after,
        micros=1.1,
    )
    return got if not first else (source[0], *got)


def pair_masks(q_pair):
    lane = lax.broadcasted_iota(jnp.int32, q_pair.shape, 1)
    zero = jnp.zeros_like(q_pair)
    return jnp.where(lane < HEAD_DIM, q_pair, zero), jnp.where(lane < HEAD_DIM, zero, q_pair)


def attend_kernel(late, *refs):
    if late:
        outer, q_ref, sib_low, own_high, sib_high, own_low, bias_ref, wo_own, wo_sib, o_ref, lse_ref, part_ref, extra = refs

        @pl.when(outer[0] == 1)
        def _():
            extra[...] = sib_high[...]

        @pl.when(outer[0] == 0)
        def _():
            extra[...] = own_low[...]

        kv = jnp.concatenate([sib_low[...], own_high[...], extra[...]], axis=0)
    else:
        q_ref, own_low, sib_low, bias_ref, wo_own, wo_sib, o_ref, lse_ref, part_ref = refs
        kv = jnp.concatenate([own_low[...], sib_low[...]], axis=0)
    h = kv.shape[1] // 2
    keys, values = kv[:, :h], kv[:, h:]
    values_t = values.T
    outs, sums = [], []
    for pair in range(h // 128):
        lanes = slice(pair * 128, pair * 128 + 128)
        for j, q in enumerate(pair_masks(q_ref[:, lanes])):
            head = 2 * pair + j
            scores = dot_back(keys[:, lanes], q) + bias_ref[...]
            highest = jnp.max(scores, axis=0, keepdims=True)
            e = jnp.exp(scores - highest)
            total = jnp.sum(e, axis=0, keepdims=True)
            mixed = dot(values_t[head * HEAD_DIM : (head + 1) * HEAD_DIM], e.astype(LOW))
            outs.append(mixed * (1.0 / total))
            sums.append(highest + jnp.log(total))
    o = jnp.concatenate(outs, axis=0).T.astype(LOW)
    o_ref[...] = o
    lse_ref[...] = jnp.concatenate(sums + sums[: 8 - len(sums)], axis=0)
    half = wo_own.shape[0]
    part_ref[...] = (dot(o[:, :half], wo_own[...]) + dot(o[:, half:], wo_sib[...])).astype(LOW)


def attend(late, q, blocks, bias, wo_own, wo_sib, outer, after=()):
    n, h = q.shape
    d = wo_own.shape[1]
    operands = ((outer,) if late else ()) + (q, *blocks, bias, wo_own, wo_sib)
    return call(
        functools.partial(attend_kernel, late),
        operands,
        [shape(n, h), shape(8, n, dtype=FULL), shape(n, d)],
        scalars=1 if late else 0,
        scratch=[pltpu.VMEM((n, 2 * h), LOW)] if late else (),
        after=after,
        micros=4.5 if late else 3.2,
    )


def gelu_parts(z):
    c = 0.7978845608028654
    square = z * z
    t = jnp.tanh(c * (z + 0.044715 * (square * z)))
    half = 0.5 * (1.0 + t)
    return z * half, half + 0.5 * z * (1.0 - t * t) * (c + (3.0 * 0.044715 * c) * square)


def feed_kernel(last, ups, dns, *refs):
    refs = (*refs[:7], refs[7 : 7 + ups], refs[7 + ups : 7 + ups + dns], *refs[7 + ups + dns :])
    if last:
        (u, part, got, gain, bias, b_own, b_sib, ups, dns, grad_ref,
         mid_ref, a_ref, g_ref, dz_ref, back_ref, hidden_sum, row_sum) = refs
    else:
        (u, part, got, gain, bias, b_own, b_sib, ups, dns,
         mid_ref, a_ref, g_ref, slope_ref, out_ref) = refs
    mid = u[...].astype(FULL) + (part[...].astype(FULL) + got[...].astype(FULL))
    mid_ref[...] = mid
    normed, _ = norm_rows(mid)
    a_two = (normed * gain[...] + bias[...]).astype(LOW)
    a_ref[...] = a_two
    f = b_own.shape[1]
    step = 256
    total = jnp.zeros(mid.shape, FULL)
    for side, (up, b, dn) in enumerate(zip(halves(ups), (b_own, b_sib), halves(dns))):
        up, dn = stacked(up, axis=1), stacked(dn)
        for at in range(0, f, step):
            cols = slice(at, at + step)
            here = slice(side * f + at, side * f + at + step)
            z = dot(a_two, up[:, cols]) + b[:, cols]
            g, slope = gelu_parts(z)
            g = g.astype(LOW)
            g_ref[:, here] = g
            if last:
                dz = (dot_back(grad_ref[...], dn[cols, :]) * slope).astype(LOW)
                dz_ref[:, here] = dz
                hidden_sum[:, here] = jnp.sum(dz.astype(FULL), axis=0, keepdims=True)
                total = total + dot_back(dz, up[:, cols])
            else:
                slope_ref[:, here] = slope.astype(LOW)
                total = total + dot(g, dn[cols, :])
    if last:
        back_ref[...] = total.astype(LOW)
        row_sum[...] = jnp.sum(grad_ref[...].astype(FULL), axis=0, keepdims=True)
    else:
        out_ref[...] = total.astype(LOW)


def feed(u, part, got, gain, bias, up, b_up, dn, grad=None, after=()):
    n, d = u.shape
    f = b_up[0].shape[1]
    last = grad is not None
    outs = [shape(n, d, dtype=FULL), shape(n, d), shape(n, 2 * f), shape(n, 2 * f), shape(n, d)]
    operands = (u, part, got, gain, bias, *b_up, *up, *dn) + ((grad,) if last else ())
    if last:
        outs += [shape(1, 2 * f, dtype=FULL), shape(1, d, dtype=FULL)]
    return call(functools.partial(feed_kernel, last, len(up), len(dn)), operands, outs, after=after, micros=3.2)


def feed_back_kernel(ups, dns, mid_grad, part, got, in_ref, gain, slope, *refs):
    grad_ref, sums_ref, dz_ref, back_ref, hidden_sum = refs[ups + dns :]
    ups, dns = refs[:ups], refs[ups : ups + dns]
    grad_norm = part[...].astype(FULL) + got[...].astype(FULL)
    normed, inverse = norm_rows(in_ref[...].astype(FULL))
    grad = (mid_grad[...] + norm_back(grad_norm, normed, inverse, gain[...])).astype(LOW)
    grad_ref[...] = grad
    sums_ref[...] = jnp.concatenate(
        [
            jnp.sum(grad_norm * normed, axis=0, keepdims=True),
            jnp.sum(grad_norm, axis=0, keepdims=True),
            jnp.sum(grad.astype(FULL), axis=0, keepdims=True),
        ],
        axis=0,
    )
    f = slope.shape[1] // 2
    step = 256
    total = jnp.zeros(grad.shape, FULL)
    for side, (up, dn) in enumerate(zip(halves(ups), halves(dns))):
        up, dn = stacked(up, axis=1), stacked(dn)
        for at in range(0, f, step):
            cols = slice(at, at + step)
            here = slice(side * f + at, side * f + at + step)
            dz = (dot_back(grad, dn[cols, :]) * slope[:, here].astype(FULL)).astype(LOW)
            dz_ref[:, here] = dz
            hidden_sum[:, here] = jnp.sum(dz.astype(FULL), axis=0, keepdims=True)
            total = total + dot_back(dz, up[:, cols])
    back_ref[...] = total.astype(LOW)


def feed_back(mid_grad, part, got, layer_in, gain, slope, up, dn, after=()):
    n, d = mid_grad.shape
    f = slope.shape[1] // 2
    outs = [shape(n, d), shape(3, d, dtype=FULL), shape(n, 2 * f), shape(n, d), shape(1, 2 * f, dtype=FULL)]
    return call(
        functools.partial(feed_back_kernel, len(up), len(dn)), (mid_grad, part, got, layer_in, gain, slope, *up, *dn), outs, after=after, micros=2.9
    )


def attend_back_kernel(late, *refs):
    if late:
        (flags, mid, part, got, grad, gain, wo_own, wo_sib, q_ref, bias, lse, own_low, own_high, sib_low, sib_high,
         low_kept, low_sent, mid_ref, low_ref, sums_ref, dq_ref, keep_low, keep_high, send_low, send_high,
         extra, acc_low, acc_high) = refs
        outside = flags[0].astype(FULL)

        @pl.when(flags[0] == 1)
        def _():
            extra[...] = sib_high[...]

        @pl.when(flags[0] == 0)
        def _():
            extra[...] = own_low[...]

        blocks = (sib_low, own_high, extra)
    else:
        (mid, part, got, grad, gain, wo_own, wo_sib, q_ref, bias, lse, own_low, sib_low,
         mid_ref, low_ref, sums_ref, dq_ref, keep_low, acc_low) = refs
        blocks = (own_low, sib_low)
    n = mid.shape[0]
    grad_norm = part[...].astype(FULL) + got[...].astype(FULL)
    normed, inverse = norm_rows(mid[...])
    mid_grad = grad[...].astype(FULL) + norm_back(grad_norm, normed, inverse, gain[...])
    mid_ref[...] = mid_grad
    low = mid_grad.astype(LOW)
    low_ref[...] = low
    sums_ref[0:1, :] = jnp.sum(grad_norm * normed, axis=0, keepdims=True)
    sums_ref[1:2, :] = jnp.sum(grad_norm, axis=0, keepdims=True)
    do = jnp.concatenate([dot_back(low, wo_own[...]), dot_back(low, wo_sib[...])], axis=1).astype(LOW)
    kv = jnp.concatenate([b[...] for b in blocks], axis=0)
    h = kv.shape[1] // 2
    keys, values = kv[:, :h], kv[:, h:]
    keys_t = keys.T
    dq = []
    for pair in range(h // 128):
        lanes = slice(pair * 128, pair * 128 + 128)
        dk = dv = None
        qs_two, do_two = pair_masks(q_ref[:, lanes]), pair_masks(do[:, lanes])
        for j in (0, 1):
            head = 2 * pair + j
            scores = dot_back(keys[:, lanes], qs_two[j]) + bias[...]
            p = jnp.exp(scores - lse[head : head + 1, :])
            dp = dot_back(values[:, lanes], do_two[j])
            inner = jnp.sum(p * dp, axis=0, keepdims=True)
            ds = (p * (dp - inner)).astype(LOW)
            dv_now = dot(p.astype(LOW), do_two[j])
            dk_now = dot(ds, qs_two[j])
            dk = dk_now if dk is None else dk + dk_now
            dv = dv_now if dv is None else dv + dv_now
            dq.append(dot(keys_t[head * HEAD_DIM : (head + 1) * HEAD_DIM], ds) * SCALING)
        for value, where in ((dk, lanes), (dv, slice(h + pair * 128, h + pair * 128 + 128))):
            if late:
                acc_low[:, where] = low_sent[:, where] + value[:n]
                keep_high[:, where] = value[n : 2 * n]
                keep_low[:, where] = low_kept[:, where] + value[2 * n :] * (1.0 - outside)
                acc_high[:, where] = value[2 * n :] * outside
            else:
                keep_low[:, where] = value[:n]
                acc_low[:, where] = value[n:]
    dq_ref[...] = jnp.concatenate(dq, axis=0).T.astype(LOW)
    if late:
        for acc, out in ((acc_low, send_low), (acc_high, send_high)):
            send = acc[...].astype(LOW)
            w = send.shape[1] // 4
            out[...] = jnp.concatenate(
                [send[:, w : 2 * w], send[:, :w], send[:, 3 * w :], send[:, 2 * w : 3 * w]], axis=1
            )


def attend_back(late, flags, mid, part, got, grad, gain, wo, q, own, sib, bias, lse, earlier, long):
    n, d = mid.shape
    h = q.shape[1]
    outs = [shape(n, d, dtype=FULL), shape(n, d), shape(2, d, dtype=FULL), shape(n, h)]
    outs += [shape(n, 2 * h, dtype=FULL)] * 2
    common = (mid, part, got, grad, gain, *wo, q, bias, lse)
    if late:
        outs += [shape(n, 2 * h)] * 2
        operands = (flags, *common, *own, *sib, *earlier)
    else:
        operands = (*common, own[0], sib[0])
    return call(
        functools.partial(attend_back_kernel, late),
        operands,
        outs,
        scalars=int(late),
        scratch=[pltpu.VMEM((n, 2 * h), LOW)] + [pltpu.VMEM((n, 2 * h), FULL)] * 2 if late else (),
        micros=300.0 if long else 5.5 if late else 4.0,
    )


def project_back_kernel(dq, keep, got, *refs):
    *ws, own_ref, sib_ref, part_ref = refs
    dkv = (keep[...] + got[...].astype(FULL)).astype(LOW)
    w = dkv.shape[1] // 4
    own = jnp.concatenate([dq[:, :w], dkv[:, :w], dkv[:, 2 * w : 3 * w]], axis=1)
    sib = jnp.concatenate([dq[:, w:], dkv[:, w : 2 * w], dkv[:, 3 * w :]], axis=1)
    own_ref[...] = own
    sib_ref[...] = sib
    w_own, w_sib = [stacked(x) for x in halves(ws)]
    part_ref[...] = (dot(own, w_own) + dot(sib, w_sib)).astype(LOW)


def project_back(dq, keep, got, weights):
    n = dq.shape[0]
    w, d = sum(x.shape[0] for x in weights) // 2, weights[0].shape[1]
    outs = [shape(n, w), shape(n, w), shape(n, d)]
    return call(project_back_kernel, (dq, keep, got, *weights), outs, micros=0.9)


def outer_kernel(plan, *refs):
    outs = refs[-2:]
    for lefts, first, count, rights, at, width, which, base in plan:
        right = jnp.concatenate([refs[i][:, at : at + width] for i in rights], axis=0)
        for row in range(0, count, 256):
            size = min(256, count - row)
            cols = slice(first + row, first + row + size)
            left = jnp.concatenate([refs[i][:, cols] for i in lefts], axis=0)
            outs[which][base + row : base + row + size, :] = dot_rows(left, right).astype(LOW)


def outer_products(operands, plan, rows, width, after=()):
    return call(functools.partial(outer_kernel, plan), operands, [shape(rows, width)] * 2, after=after, micros=2.5)


def down_kernel(count, *refs):
    gs, dns, outs = refs[:2], refs[2 : 2 + count], refs[2 + count :]
    dn = stacked(dns)
    for g, out in zip(gs, outs):
        out[...] = dot(g[...], dn).astype(LOW)


def down(gs, dns, after=()):
    n, d = gs[0].shape[0], dns[0].shape[1]
    return call(functools.partial(down_kernel, len(dns)), (*gs, *dns), [shape(n, d)] * 2, after=after, micros=1.4)


def ready_kernel(cuts, extra, flags, first_own, first_got, second_own, second_got, *refs):
    small, outs = refs[:extra], refs[extra:]
    for i, (at, size) in enumerate(cuts):
        rows = slice(at, at + size)
        first = (first_own[rows, :].astype(FULL) + first_got[rows, :].astype(FULL)).astype(LOW)
        second = (second_own[rows, :].astype(FULL) + second_got[rows, :].astype(FULL)).astype(LOW)
        mine, theirs = outs[2 * i], outs[2 * i + 1]

        @pl.when(flags[1] == 1)
        def _():
            mine[:size, :] = first
            theirs[:size, :] = second

        @pl.when(flags[1] == 0)
        def _():
            mine[:size, :] = second
            theirs[:size, :] = first

    for values, out in zip(small, outs[-2:]):
        split_rows(values[...], out)


def split_rows(values, out):
    first = out.shape[0] - EXTRA
    rounded = values.astype(LOW)
    out[first : first + EXTRA // 2, :] = rounded
    out[first + EXTRA // 2 :, :] = (values - rounded.astype(FULL)).astype(LOW)


def joined_rows(ref):
    first = ref.shape[0] - EXTRA
    return ref[first : first + EXTRA // 2, :].astype(FULL) + ref[first + EXTRA // 2 :, :].astype(FULL)


def ready_pieces(flags, first, second, sizes, at=0, small=()):
    cuts = []
    for size in sizes:
        cuts.append((at, size))
        at += size
    width = first[0].shape[1]
    outs = [shape(size, width) for size in sizes for _ in (0, 1)]
    if small:
        outs[-2:] = [shape(sizes[-1] + EXTRA, width)] * 2
    got = call(
        functools.partial(ready_kernel, tuple(cuts), len(small)), (flags, *first, *second, *small), outs, scalars=1
    )
    return [(got[2 * i], got[2 * i + 1]) for i in range(len(sizes))]


def sums_kernel(extra, *refs):
    count = len(refs) // 3
    for i in range(count):
        left, right, out = refs[2 * i], refs[2 * i + 1], refs[2 * count + i]
        if not extra[i]:
            out[...] = (left[...].astype(FULL) + right[...].astype(FULL)).astype(LOW)
        else:
            bulk = slice(0, out.shape[0] - EXTRA)
            out[bulk, :] = (left[bulk, :].astype(FULL) + right[bulk, :].astype(FULL)).astype(LOW)
            split_rows(joined_rows(left) + joined_rows(right), out)


def added(left, right, after=()):
    return call(added_kernel, (left, right), [shape(*left.shape, dtype=left.dtype)], after=after)[0]


def chosen_kernel(count, which, extra, flags, *refs):
    sums, gots, outs = refs[:count], refs[count : 2 * count], refs[2 * count :]
    outs, small = outs[: len(outs) - extra], outs[len(outs) - extra :]
    for flag, pieces in ((1, sums), (0, gots)):

        @pl.when(flags[which] == flag)
        def _():
            first = 0
            for out in outs:
                at, last = 0, first + out.shape[0]
                for piece in pieces:
                    low, high = max(first, at), min(last, at + piece.shape[0])
                    if low < high:
                        out[low - first : high - first, :] = piece[low - at : high - at, :].astype(FULL)
                    at += piece.shape[0]
                first = last
            for out in small:
                out[...] = joined_rows(pieces[-1])


def chosen(flags, stages, sizes, which, extra=False):
    if which is None:
        flags, which = jnp.ones_like(flags), 0
    operands = (flags, *[low for low, _ in stages], *[got for _, got in stages])
    outs = [shape(size, stages[0][0].shape[1], dtype=FULL) for size in (*sizes, EXTRA // 2)[: len(sizes) + extra]]
    return call(functools.partial(chosen_kernel, len(stages), which, int(extra)), operands, outs, scalars=1)


def micro_out_kernel(flags, mine, got, out):
    for flag, first, second in ((1, mine, got), (0, got, mine)):

        @pl.when(flags[1] == flag)
        def _():
            out[0] = first[...]
            out[1] = second[...]


def last_kernel(flags, part_low, part_high, got, mid_low, mid_high, in_low, in_high, gain, out, sums):
    for flag, part, mid, rows in ((1, part_low, mid_low, in_low), (0, part_high, mid_high, in_high)):

        @pl.when(flags[4] == flag)
        def _():
            grad_norm = part[...].astype(FULL) + got[...].astype(FULL)
            normed, inverse = norm_rows(rows[...].astype(FULL))
            out[...] = (mid[...] + norm_back(grad_norm, normed, inverse, gain[...])).astype(LOW)
            sums[0:1, :] = 2.0 * jnp.sum(grad_norm * normed, axis=0, keepdims=True)
            sums[1:2, :] = 2.0 * jnp.sum(grad_norm, axis=0, keepdims=True)


def last_rows(flags, parts, got, mids, rows, gain):
    n, d = got.shape
    return call(
        last_kernel, (flags, *parts, got, *mids, *rows, gain), [shape(n, d), shape(2, d, dtype=FULL)], scalars=1,
        micros=1.0,
    )


def gather_kernel(one_0, one_lo, one_hi, two_lo_0, two_hi_0, two_lo_1, two_hi_1, down_lo, down_hi, up_lo_0, up_hi_0, up_lo_1, up_hi_1, rows, own):
    half = own.shape[1]
    both = one_lo[...] + one_hi[...]
    rows[0:2, :] = one_0[...]
    rows[2:4, :] = two_lo_0[...] + two_hi_0[...]
    rows[4:5, :] = both[2:3]
    rows[5:7, :] = both[0:2]
    rows[7:9, :] = two_lo_1[...] + two_hi_1[...]
    rows[9:10, :] = down_lo[...] + down_hi[...]
    for i, hidden in enumerate((up_lo_0[...] + up_hi_0[...], up_lo_1[...] + up_hi_1[...])):
        rows[10 + i : 11 + i, :] = hidden[:, half:]
        own[i : i + 1, :] = hidden[:, :half]


def chip_kernel(rows, own, got, out):
    out[0:10, :] = rows[0:10, :] + got[0:10, :]
    out[10:12, :] = own[...] + got[10:12, :]


def layers_kernel(flags, rows, got, mine, theirs):
    both = (rows[0:10, :] + got[0:10, :]) * 0.5
    for flag, first, second in ((1, mine, theirs), (0, theirs, mine)):

        @pl.when(flags[1] == flag)
        def _():
            first[...] = jnp.zeros_like(first)
            second[...] = jnp.zeros_like(second)
            first[0:5, :] = both[0:5]
            first[5:6, :] = rows[10:11, :]
            second[0:5, :] = both[5:10]
            second[5:6, :] = rows[11:12, :]


def fill(out, wholes, axis, first):
    if axis:
        out[...] = wholes[0][:, first : first + out.shape[1]]
        return
    at, last = 0, first + out.shape[0]
    for whole in wholes:
        low, high = max(first, at), min(last, at + whole.shape[0])
        if low < high:
            out[low - first : high - first, :] = whole[low - at : high - at, :]
        at += whole.shape[0]


def half_kernel(axis, flags, *refs):
    *wholes, out = refs
    for flag in (1, 0):

        @pl.when(flags[3] == flag)
        def _():
            fill(out, wholes, axis, 0 if flag else out.shape[axis])


def half_rows_kernel(flags, *refs):
    *wholes, out, sems = refs
    size = out.shape[0]
    for flag in (1, 0):

        @pl.when(flags[3] == flag)
        def _():
            first, at, copies = 0 if flag else size, 0, []
            for i, whole in enumerate(wholes):
                low, high = max(first, at), min(first + size, at + whole.shape[0])
                if low < high:
                    rows = pl.ds(low - at, high - low)
                    copies.append(
                        pltpu.make_async_copy(whole.at[rows], out.at[pl.ds(low - first, high - low)], sems.at[i])
                    )
                at += whole.shape[0]
            for copy in copies:
                copy.start()
            for copy in copies:
                copy.wait()


def half_rows(flags, wholes):
    size = sum(w.shape[0] for w in wholes) // 2
    got = pl.pallas_call(
        half_rows_kernel,
        out_shape=shape(size, wholes[0].shape[1]),
        in_specs=[pl.BlockSpec(memory_space=pltpu.SMEM)] + [pl.BlockSpec(memory_space=pl.ANY)] * len(wholes),
        out_specs=pl.BlockSpec(memory_space=pltpu.VMEM),
        scratch_shapes=[pltpu.SemaphoreType.DMA((len(wholes),))],
        cost_estimate=pl.CostEstimate(flops=1024, bytes_accessed=1024, transcendentals=0),
    )(flags, *wholes)
    LATEST[:] = [got]
    return got


def half_of(flags, wholes, axis, after=()):
    dims = [sum(w.shape[0] for w in wholes), wholes[0].shape[1]]
    dims[axis] //= 2
    return call(functools.partial(half_kernel, axis), (flags, *wholes), [shape(*dims)], scalars=1, after=after)[0]


def pick_kernel(layer, count, got_count, flags, *refs):
    wholes, gots, outs = refs[:count], refs[count : count + got_count], refs[count + got_count :]
    ways = [(flags[1] == 1 - layer, wholes), (flags[1] == layer, gots)]
    if got_count > 1:
        swapped = (gots[1], gots[0], *gots[2:])
        ways = [ways[0]] + [((flags[1] == layer) & (flags[3] == flag), x) for flag, x in ((1, gots), (0, swapped))]
    for wanted, sources in ways:

        @pl.when(wanted)
        def _():
            at = 0
            for out in outs:
                fill(out, sources, 0, at)
                at += out.shape[0]


def picked(flags, layer, wholes, gots, sizes, after=()):
    outs = [shape(size, wholes[0].shape[1]) for size in sizes]
    kernel = functools.partial(pick_kernel, layer, len(wholes), len(gots))
    return call(kernel, (flags, *wholes, *gots), outs, scalars=1, after=after)


def stack_kernel(*refs):
    *wholes, out = refs
    fill(out, wholes, 0, 0)


def stacked_rows(wholes, after):
    rows = sum(w.shape[0] for w in wholes)
    return call(stack_kernel, wholes, [shape(rows, wholes[0].shape[1])], after=after)[0]


def copy_kernel(source, out):
    out[...] = source[...]


def copied(source, after):
    return call(copy_kernel, (source,), [shape(*source.shape)], after=after)[0]


def micro_kernel(flags, *refs):
    *arrays, out = refs
    n = arrays[0].shape[1]
    for flag in (1, 0):

        @pl.when(flags[1] == flag)
        def _():
            for i, both in enumerate(arrays):
                out[i * n : (i + 1) * n, :] = both[1 - flag]


def output_kernel(flags, mid_low, mid_high, part_low, part_high, got, bias, out):
    for flag, mid, part in ((1, mid_low, part_low), (0, mid_high, part_high)):

        @pl.when(flags[4] == flag)
        def _():
            out[...] = (mid[...] + (part[...].astype(FULL) + got[...].astype(FULL)) + bias[...]).astype(LOW)


def own_kernel(flags, if_low, if_high, out):
    for flag, rows in ((1, if_low), (0, if_high)):

        @pl.when(flags[4] == flag)
        def _():
            out[...] = rows[...]


def own_or(flags, if_low, if_high, after=()):
    return call(own_kernel, (flags, if_low, if_high), [shape(*if_low.shape)], scalars=1, after=after)[0]


def output_rows(flags, mids, parts, got, bias):
    return call(output_kernel, (flags, *mids, *parts, got, bias), [shape(*got.shape)], scalars=1)[0]


def body(
    inputs, cotangent, segments, ln1_gain, ln1_bias, w_query, w_key, w_value, w_out,
    ln2_gain, ln2_bias, w_up, b_up, w_down, b_down, *, n_batch,
):
    LATEST.clear()
    CHAINED[0] = False
    n, d = inputs.shape[1:]
    half = w_up.shape[2]
    section = lax.axis_index("section")
    tensor = lax.axis_index("tensor")
    batch = lax.axis_index("batch")
    on_first = section == 0
    early = tensor < 2
    outer = (tensor == 0) | (tensor == 3)
    middle = (batch == 1) | (batch == 2)
    even = batch % 2 == 0
    flags = jnp.stack([outer, on_first, middle, even, early]).astype(jnp.int32)
    paired = n_batch % 2 == 0
    beside = [(i, i ^ 1) for i in range(n_batch)]

    def across(value):
        return lax.ppermute(value, "section", SWAP)

    qkv_parts = (w_query[0].T, w_key[0].T, w_value[0].T)
    CHAINED[0] = True
    got_qkv = across(half_rows(flags, qkv_parts) if paired else stacked_rows(qkv_parts, ()))
    own_rows = call(micro_kernel, (flags, inputs, cotangent), [shape(2 * n, d)], scalars=1)[0]
    other_rows = to_partner(own_rows)
    got_wo = across(copied(w_out[0], ()))
    small_own = jnp.concatenate([ln1_gain, ln1_bias, ln2_gain, ln2_bias, b_down, b_up], axis=0)
    small_other = across(small_own)
    if paired:
        got_up = across(half_of(flags, (w_up[0],), 0))
        got_down = across(copied(w_down[0], (small_other,)))
        gots_feed = (got_up, lax.ppermute(got_up, "batch", beside), got_down)
    else:
        gots_feed = (across(stacked_rows((w_up[0], w_down[0]), ())),)
    CHAINED[0] = False
    gots_qkv = (got_qkv, lax.ppermute(got_qkv, "batch", beside)) if paired else jnp.split(got_qkv, 2)

    def low_high(own, other):
        return jnp.where(early, own, other), jnp.where(early, other, own)

    rows_in = low_high(own_rows[:n], other_rows[:n])
    grad_last = low_high(own_rows[n:], other_rows[n:])

    segment = jnp.where(on_first, segments[0, 0], segments[1, 0])
    low_at = jnp.where(outer, 0, 1)
    block_at = {"own_low": low_at, "sib_low": 1 - low_at, "own_high": 3 - low_at, "sib_high": 2 + low_at}

    def block_bias(query, key_blocks):
        span = jnp.arange(n)
        query_at = block_at[query] * n + span
        query_seg = lax.dynamic_slice_in_dim(segment, block_at[query] * n, n)
        rows = []
        for key in key_blocks:
            key_at = key * n + span
            key_seg = lax.dynamic_slice_in_dim(segment, key * n, n)
            kept = (key_at[:, None] <= query_at[None, :]) & (key_seg[:, None] == query_seg[None, :])
            rows.append(jnp.where(kept, 0.0, MASKED).astype(FULL))
        return jnp.concatenate(rows, axis=0)

    biases = (
        block_bias("own_low", [block_at["own_low"], block_at["sib_low"]]),
        block_bias(
            "own_high",
            [block_at["sib_low"], block_at["own_high"], jnp.where(outer, block_at["sib_high"], block_at["own_low"])],
        ),
    )

    def layer_rows(layer):
        small = jnp.where(section == layer, small_own, small_other)
        rows = [small[i : i + 1] for i in range(6)]
        return rows[:5] + [(rows[5], to_sibling(rows[5]))]

    small_0, small_1 = layer_rows(0), layer_rows(1)

    def weights(layer, wholes, gots, sizes, after):
        return [(own, to_sibling(own)) for own in picked(flags, layer, wholes, gots, sizes, after)]

    def qkv_weight(layer, after=()):
        return weights(layer, qkv_parts, gots_qkv, [3 * w_query.shape[2]], after)[0]

    def out_weight(layer, after=()):
        return weights(layer, (w_out[0],), (got_wo,), [w_out.shape[1]], after)[0]

    def feed_weights(layer, after=()):
        return weights(layer, (w_up[0], w_down[0]), gots_feed, [d, half], after)

    def attend_low(projected, sib, wo):
        return attend(False, projected[2], (projected[3], sib[0]), biases[0], *wo, None)

    def attend_high(both, sib, wo):
        return attend(True, both[1][2], (sib[0], both[1][3], sib[1], both[0][3]), biases[1], *wo, flags)

    qkv_0 = qkv_weight(0, (got_wo,))
    wo_0 = out_weight(0)
    tied = (small_0[5][1], small_1[5][1])
    proj_0, sib_0 = [], []
    for i in (0, 1):
        proj_0.append(project((rows_in[i],), small_0[0], small_0[1], qkv_0, True, tied))
        sib_0.append(to_sibling(proj_0[i][4]))
    att_0 = [attend_low(proj_0[0], sib_0, wo_0)]
    got = [to_partner(att_0[0][2])]
    att_0.append(attend_high(proj_0, sib_0, wo_0))
    got.append(to_partner(att_0[1][2]))
    if paired:
        (up_0,) = weights(0, (w_up[0],), gots_feed[:2], [d], (att_0[1][2],))
        (down_0,) = weights(0, (w_down[0],), gots_feed[2:], [half], got)
    else:
        up_0, down_0 = feed_weights(0, got)
    feed_0, feed_got, after = [], [], ()
    for i in (0, 1):
        feed_0.append(
            feed(proj_0[i][0], att_0[i][2], got[i], small_0[2], small_0[3], up_0, small_0[5], down_0, after=after)
        )
        feed_got.append(to_partner(feed_0[i][4]))
        if i == 0:
            qkv_1 = qkv_weight(1, (feed_0[0][4],))
            wo_1 = out_weight(1, (feed_0[0][4],))
            after = (qkv_1[0], wo_1[0])

    proj_1, sib_1, att_1, got, after = [], [], [], [], (feed_0[1][4], wo_1[1])
    for i in (0, 1):
        source = (feed_0[i][0], feed_0[i][4], feed_got[i], small_0[4])
        proj_1.append(project(source, small_1[0], small_1[1], qkv_1, False, after))
        sib_1.append(to_sibling(proj_1[i][4]))
        if i == 0:
            up_1, down_1 = feed_weights(1, (proj_1[0][2],))
            after = (up_1[0], down_1[0])
            att_1.append(attend_low(proj_1[0], sib_1, wo_1))
        else:
            att_1.append(attend_high(proj_1, sib_1, wo_1))
        got.append(to_partner(att_1[i][2]))
    feed_1, back_got = [], []
    for i in (0, 1):
        feed_1.append(
            feed(proj_1[i][0], att_1[i][2], got[i], small_1[2], small_1[3], up_1, small_1[5], down_1, grad_last[i])
        )
        back_got.append(to_partner(feed_1[i][4]))

    def grads_feed(g, grads, a_two, dz):
        plan = (
            ((4, 5), 0, d, (6, 7), 0, half, 0, 0),
            ((4, 5), 0, d, (6, 7), half, half, 1, 0),
            ((0, 1), 0, half, (2, 3), 0, d, 0, d),
            ((0, 1), half, half, (2, 3), 0, d, 1, d),
        )
        return outer_products((*g, *grads, *a_two, *dz), plan, d + half, d)

    def grads_attend(o, lows, a_one, d_own, d_sib):
        w, w3 = o[0].shape[1] // 2, d_own[0].shape[1]
        plan = (
            ((6, 7), 0, w3, (4, 5), 0, d, 0, 0),
            ((8, 9), 0, w3, (4, 5), 0, d, 1, 0),
            ((0, 1), 0, w, (2, 3), 0, d, 0, w3),
            ((0, 1), w, w, (2, 3), 0, d, 1, w3),
        )
        return outer_products((*o, *lows, *a_one, *d_own, *d_sib), plan, w3 + w, d)

    mids = [f[0] for f in feed_1]
    by_feed_1 = grads_feed([f[2] for f in feed_1], grad_last, [f[1] for f in feed_1], [f[3] for f in feed_1])
    feed_1_got = to_sibling(by_feed_1[1])
    out_parts = down([f[2] for f in feed_1], down_1)
    def attend_backward(i, mids, parts, grads, gain, wo, projected, sib, att, earlier, long=False):
        return attend_back(
            bool(i), flags, mids[i], parts[i], back_got[i], grads[i], gain, wo, projected[i][2],
            [p[3] for p in projected], sib, biases[i], att[i][1], earlier, long,
        )

    ab_1 = []
    for i in (0, 1):
        earlier = ab_1[0][4:6] if i else ()
        ab_1.append(
            attend_backward(i, mids, [f[4] for f in feed_1], grad_last, small_1[2], wo_1, proj_1, sib_1, att_1, earlier)
        )
    mid_grads_1, lows_1, dq = [[a[k] for a in ab_1] for k in (0, 1, 3)]
    keep, send = ab_1[1][4:6], ab_1[1][6:8]
    kv_got = [to_sibling(x) for x in send]
    back_1, part_got = [], []
    for i in (0, 1):
        back_1.append(project_back(dq[i], keep[i], kv_got[i], qkv_1))
        part_got.append(to_partner(back_1[i][2]))
    by_att_1 = grads_attend(
        [a[0] for a in att_1], lows_1, [p[1] for p in proj_1], [b[0] for b in back_1], [b[1] for b in back_1]
    )
    att_1_got = to_sibling(by_att_1[1])

    fb_0, back_got, after = [], [], by_att_1
    for i in (0, 1):
        fb_0.append(
            feed_back(
                mid_grads_1[i], back_1[i][2], part_got[i], proj_1[i][0], small_1[0], feed_0[i][3], up_0, down_0, after
            )
        )
        after = ()
        back_got.append(to_partner(fb_0[i][3]))
    grad_mid = [f[0] for f in fb_0]
    by_feed_0 = grads_feed([f[2] for f in feed_0], grad_mid, [f[1] for f in feed_0], [f[2] for f in fb_0])
    feed_0_got = to_sibling(by_feed_0[1])

    CHAINED[0] = True
    along = [[(0, 1), (3, 2)], [(1, 2), (2, 1)], [(1, 0), (2, 3)]]
    feed_pieces = ready_pieces(
        flags, (by_feed_0[0], feed_0_got), (by_feed_1[0], feed_1_got), [(d + half) // 3] * 3
    )
    stage, hops = {}, {}

    def begin(k, piece):
        stage[k], hops[k] = (piece[0], across(piece[1])), 0

    def advance(*ks, after=(), extra=3):
        if n_batch != 4:
            ks = [k for k in ks if hops[k] == 0]
        if not ks:
            return
        values = call(
            functools.partial(sums_kernel, tuple(k == extra for k in ks)), [x for k in ks for x in stage[k]], [shape(*stage[k][0].shape) for k in ks],
            after=[stage[k][1] for k in after], micros=0.5 * len(ks),
        )
        for k, value in zip(ks, values):
            stage[k] = (value, lax.ppermute(value, "batch", along[hops[k]]) if n_batch == 4 else value)
            hops[k] += 1

    def settled(ks, sizes, extra=False):
        if n_batch == 4:
            return chosen(flags, [stage[k] for k in ks], sizes, 2, extra)
        return chosen(flags, [(lax.psum(stage[k][0], "batch"), stage[k][0]) for k in ks], sizes, None, extra)

    begin(0, feed_pieces[0])
    begin(1, feed_pieces[1])
    begin(2, feed_pieces[2])
    parts_0 = [f[3] for f in fb_0]
    mids_0 = [f[0] for f in feed_0]
    ab_0 = []
    for i in (0, 1):
        earlier = ab_0[0][4:6] if i else ()
        ab_0.append(
            attend_backward(i, mids_0, parts_0, grad_mid, small_0[2], wo_0, proj_0, sib_0, att_0, earlier, True)
        )
    mid_grads_0, lows_0, dq = [[a[k] for a in ab_0] for k in (0, 1, 3)]
    keep, send = ab_0[1][4:6], ab_0[1][6:8]
    advance(0)
    kv_got = [to_sibling(x) for x in send]
    back_0 = [project_back(dq[i], keep[i], kv_got[i], qkv_0) for i in (0, 1)]
    part_got = to_partner(own_or(flags, back_0[1][2], back_0[0][2]))
    by_att_0 = grads_attend(
        [a[0] for a in att_0], lows_0, [p[1] for p in proj_0], [b[0] for b in back_0], [b[1] for b in back_0]
    )
    att_0_got = to_sibling(by_att_0[1])
    att_rows = by_att_0[0].shape[0]
    att_sides = (by_att_0[0], att_0_got), (by_att_1[0], att_1_got)

    last, one_0 = last_rows(flags, [b[2] for b in back_0], part_got, mid_grads_0, rows_in, small_0[0])
    operands = (
        one_0, fb_0[0][1], fb_0[1][1], ab_0[0][2], ab_0[1][2], ab_1[0][2], ab_1[1][2], feed_1[0][6], feed_1[1][6], fb_0[0][4], fb_0[1][4],
        feed_1[0][5], feed_1[1][5],
    )
    rows, own = call(gather_kernel, operands, [shape(12, d, dtype=FULL), shape(2, half, dtype=FULL)])
    rows = call(chip_kernel, (rows, own, to_sibling(rows)), [shape(12, d, dtype=FULL)])[0]
    advance(0, 1)
    small = call(layers_kernel, (flags, rows, to_partner(rows)), [shape(EXTRA // 2, d, dtype=FULL)] * 2, scalars=1)
    att_pieces = ready_pieces(flags, *att_sides, [att_rows // 2] * 2, small=small)
    begin(3, att_pieces[1])
    begin(4, att_pieces[0])
    advance(2, 1, 0)

    def micro_sent(first, second):
        mine = jnp.where(on_first, first, second)
        return mine, across(jnp.where(on_first, second, first))

    def micro_out(mine, got):
        return call(micro_out_kernel, (flags, mine, got), [shape(2, n, d)], scalars=1)[0][None]

    advance(3, 2, 1)
    backward = micro_sent(last, jnp.where(early, *grad_mid))
    out_got = to_partner(own_or(flags, out_parts[1], out_parts[0]))
    advance(4, 3, 2, after=(0,))
    out_1 = output_rows(flags, mids, out_parts, out_got, small_1[4])
    forward = micro_sent(jnp.where(early, *[p[0] for p in proj_1]), out_1)
    advance(4, 3, after=(1,))
    advance(4, after=(2,))
    up_total, down_total = settled((0, 1, 2), [d, half])
    value_total, out_total, sums = settled((3,), [att_rows // 4] * 2, True)
    backward_out = micro_out(*backward)
    forward_out = micro_out(*forward)
    query_total, key_total = settled((4,), [att_rows // 4] * 2)
    att_totals = [query_total, key_total, value_total, out_total]
    return (
        forward_out,
        backward_out,
        sums[0:1],
        sums[1:2],
        *[x.T[None] for x in att_totals[:3]],
        att_totals[3][None],
        sums[2:3],
        sums[3:4],
        up_total[None],
        sums[5:6],
        down_total[None],
        sums[4:5],
    )


def solution(mesh):
    rows = P(None, ("batch", "tensor"), None)
    layer = P("section", None)
    by_column = P("section", None, "tensor")
    by_row = P("section", "tensor", None)
    kept = P("section", None, ("batch", "tensor"), None)
    return jax.shard_map(
        functools.partial(body, n_batch=mesh.shape["batch"]),
        mesh=mesh,
        in_specs=(
            rows, rows, P(None, "batch", None), layer, layer, by_column, by_column, by_column, by_row,
            layer, layer, by_column, P("section", "tensor"), by_row, layer,
        ),
        out_specs=(
            kept, kept, layer, layer, by_column, by_column, by_column, by_row,
            layer, layer, by_column, P("section", "tensor"), by_row, layer,
        ),
        check_vma=False,
    )
```
